128 devices in a mesh: section: 2 (over core), fsdp: 8 (over z, y_lo), dp: 8 (over x, y_hi).
Axes of the slice: x: 4, y: 4 (y_hi: 2, y_lo: 2; y = y_hi * 2 + y_lo), z: 4, core: 2. Of those that a mesh axis runs over, the one named last changes fastest.
Arguments:
- boundary: bfloat16 [2, 2, 8, 1024, 960], P('section', None, 'dp', 'fsdp'), may hold values from -6 to 6
- lengths: int32 [8, 2, 4], P('dp'), may hold values from 0 to 1024, as said below
- query_weight: bfloat16 [2, 960, 960], P('section', 'fsdp'), may hold values from -0.1875 to 0.1875
- key_matrix: bfloat16 [2, 960, 320], P('section', 'fsdp'), may hold values from -0.1875 to 0.1875
- value_matrix: bfloat16 [2, 960, 320], P('section', 'fsdp'), may hold values from -0.1875 to 0.1875
- output_weight: bfloat16 [2, 960, 960], P('section', 'fsdp'), may hold values from -0.75 to 0.75
- gate_weight: bfloat16 [2, 960, 2560], P('section', 'fsdp'), may hold values from -0.1875 to 0.1875
- up_weight: bfloat16 [2, 960, 2560], P('section', 'fsdp'), may hold values from -0.1875 to 0.1875
- down_weight: bfloat16 [2, 2560, 960], P('section', 'fsdp'), may hold values from -0.125 to 0.125
- first_gain: bfloat16 [2, 960], P('section', 'fsdp'), may hold values from 0.099609375 to 1.8984375
- second_gain: bfloat16 [2, 960], P('section', 'fsdp'), may hold values from 0.099609375 to 1.8984375
Outputs:
- boundary_out: bfloat16 [2, 2, 8, 1024, 960], P('section', None, 'dp', 'fsdp')
- query_grad: float32 [2, 960, 960], P('section', 'fsdp')
- key_grad: float32 [2, 960, 320], P('section', 'fsdp')
- value_grad: float32 [2, 960, 320], P('section', 'fsdp')
- output_grad: float32 [2, 960, 960], P('section', 'fsdp')
- gate_grad: float32 [2, 960, 2560], P('section', 'fsdp')
- up_grad: float32 [2, 960, 2560], P('section', 'fsdp')
- down_grad: float32 [2, 2560, 960], P('section', 'fsdp')
- first_gain_grad: float32 [2, 960], P('section', 'fsdp')
- second_gain_grad: float32 [2, 960], P('section', 'fsdp')
The draws below stay inside these ranges and needn't reach their ends.
Inputs may be any that keep to these rules, and one draw needn't show every extreme that they name: For each group and micro-batch the 4 lengths sum to at most 1024; rows beyond the sum are padding; a length may be 0.
All inputs are finite; a program needn't handle non-finite values.
Results may differ from the reference program's by a relative error of at most 0.025.
Values may be sent and summed in bfloat16 or wider, within the bound.
No kernel may reach another device: no remote copies, remote signals or barrier semaphores. Data moves between devices by JAX's collectives and lax.ppermute only.
A program may use at most 192 MiB of HBM per device.

```python
import jax
import jax.numpy as jnp
from jax import lax

MODEL_WIDTH = 960
QUERY_HEADS = 15
KEY_VALUE_HEADS = 5
HEAD_SIZE = 64
FF = 2560
MB = 2
SEQS = 4
ROWS = 1024
ROWS_DEV = 128
GROUPS = 8
LAYER_COUNT = 2


def draw_lengths(key, part):
    key = jax.random.fold_in(key, 7)
    subkeys = jax.random.split(key, 5)
    filled = jax.random.randint(subkeys[0], (GROUPS, MB, 1), ROWS // 2, ROWS + 1)
    cut_points = jax.random.randint(subkeys[1], (GROUPS, MB, SEQS - 1), 0, ROWS + 1)
    cut_points = jnp.sort(jnp.minimum(cut_points, filled), axis=-1)
    leading = jnp.zeros((GROUPS, MB, 1), jnp.int32)
    boundaries = jnp.concatenate([leading, cut_points, filled], axis=-1)
    pieces = boundaries[:, :, 1:] - boundaries[:, :, :-1]
    remainder = jax.random.randint(subkeys[2], (GROUPS,), 0, ROWS_DEV)
    widest = jax.random.randint(subkeys[3], (), 0, GROUPS)
    remainder = jnp.where(jnp.arange(GROUPS) == widest, 0, remainder)
    chosen = jax.random.randint(subkeys[4], (GROUPS,), 0, MB)
    position = jnp.arange(SEQS)[None, :]
    spanning = jnp.where(position == 0, ROWS - remainder[:, None], jnp.where(position == 1, remainder[:, None], 0))
    chosen_mask = (jnp.arange(MB)[None, :] == chosen[:, None])[:, :, None]
    return jnp.where(chosen_mask, spanning[:, None, :], pieces).astype(jnp.int32)


def shard_levels(own_key, shape, shards, smallest, largest):
    gain = 1.0
    for axis_at, shards_of in shards:
        heights = jax.random.uniform(jax.random.fold_in(jax.random.fold_in(own_key, 6), axis_at), (shards_of,), jnp.float32, smallest / len(shards), largest / len(shards))
        gain = gain * jnp.repeat(jnp.exp(heights), shape[axis_at] // shards_of).reshape((-1,) + (1,) * (len(shape) - 1 - axis_at))
    return gain


def scatter_about(rng, shape, deviation, most, shards=(), kind=jnp.bfloat16):
    factor_of = shard_levels(rng, shape, shards, -0.22, 0.18) if shards else 1.0
    values = jax.random.normal(rng, shape, jnp.float32) * deviation * factor_of
    return jnp.minimum(jnp.maximum(values, -most), most).astype(kind)


def setup_inputs(seed: int = 0) -> dict:
    seeds = jax.random.split(jax.random.key(seed), 12)
    return {
        "boundary": scatter_about(seeds[0], (LAYER_COUNT, MB, GROUPS, ROWS, MODEL_WIDTH), 1.0, 6.0, ((0, 2), (2, 8), (3, 8))),
        "lengths": draw_lengths(jax.random.fold_in(seeds[11], 71), 0),
        "query_weight": scatter_about(seeds[2], (LAYER_COUNT, MODEL_WIDTH, QUERY_HEADS * HEAD_SIZE), MODEL_WIDTH ** -0.5, 0.1875, ((0, 2), (1, 8))),
        "key_matrix": scatter_about(seeds[3], (LAYER_COUNT, MODEL_WIDTH, KEY_VALUE_HEADS * HEAD_SIZE), MODEL_WIDTH ** -0.5, 0.1875, ((0, 2), (1, 8))),
        "value_matrix": scatter_about(seeds[4], (LAYER_COUNT, MODEL_WIDTH, KEY_VALUE_HEADS * HEAD_SIZE), MODEL_WIDTH ** -0.5, 0.1875, ((0, 2), (1, 8))),
        "output_weight": scatter_about(seeds[5], (LAYER_COUNT, QUERY_HEADS * HEAD_SIZE, MODEL_WIDTH), (QUERY_HEADS * HEAD_SIZE // 16) ** -0.5, 0.75, ((0, 2), (1, 8))),
        "gate_weight": scatter_about(seeds[6], (LAYER_COUNT, MODEL_WIDTH, FF), MODEL_WIDTH ** -0.5, 0.1875, ((0, 2), (1, 8))),
        "up_weight": scatter_about(seeds[7], (LAYER_COUNT, MODEL_WIDTH, FF), MODEL_WIDTH ** -0.5, 0.1875, ((0, 2), (1, 8))),
        "down_weight": scatter_about(seeds[8], (LAYER_COUNT, FF, MODEL_WIDTH), FF ** -0.5, 0.125, ((0, 2), (1, 8))),
        "first_gain": jnp.clip(1.0 + 0.18 * jax.random.normal(seeds[9], (LAYER_COUNT, MODEL_WIDTH), jnp.float32), 0.099609375, 1.8984375).astype(jnp.bfloat16),
        "second_gain": jnp.clip(1.0 + 0.18 * jax.random.normal(seeds[10], (LAYER_COUNT, MODEL_WIDTH), jnp.float32), 0.099609375, 1.8984375).astype(jnp.bfloat16),
    }


@jax.custom_vjp
def lower_half(v):
    return lax.optimization_barrier(v.astype(jnp.bfloat16)).astype(jnp.float32)

@jax.custom_vjp
def lower_half_backward(v):
    return v

def low_keep(v):
    return (lower_half(v), None)

def low_pass(kept, grad):
    return (grad,)

def back_keep(v):
    return (v, None)

def back_low(kept, grad):
    return (lower_half(grad),)
lower_half.defvjp(low_keep, low_pass)
lower_half_backward.defvjp(back_keep, back_low)
EPS = 1e-05
SCALE = 0.125
MASKED = -1e+30
HIGH = lax.Precision.HIGHEST

def matrix_product(left, right):
    return jnp.dot(left, right, precision=HIGH, preferred_element_type=jnp.float32)

def segment_rows(seq_lengths, row_index):
    seq_ends = jnp.cumsum(seq_lengths).astype(jnp.int32)
    starts = (seq_ends - seq_lengths).astype(jnp.int32)
    segment = lax.optimization_barrier(jnp.sum((row_index[:, None] >= seq_ends[None, :]).astype(jnp.int32), axis=1)).astype(jnp.int32)
    slot_ids = jnp.arange(seq_lengths.shape[0], dtype=jnp.int32)
    row_start = lax.optimization_barrier(jnp.sum(jnp.where(segment[:, None] == slot_ids[None, :], starts[None, :], 0), axis=1)).astype(jnp.int32)
    return (segment, (row_index - row_start).astype(jnp.int32))

def rotary_tables(position):
    frequency = 10000.0 ** (-2.0 * jnp.arange(HEAD_SIZE // 2, dtype=jnp.float32) / HEAD_SIZE)
    angles = position.astype(jnp.float32)[:, None] * frequency[None, :]
    return (jnp.cos(angles)[:, None, :], jnp.sin(angles)[:, None, :])

def rotary_embedding(vector, cosine_table, sine_portion):
    first_half = vector[..., :HEAD_SIZE // 2]
    second_half = vector[..., HEAD_SIZE // 2:]
    return jnp.concatenate([first_half * cosine_table - second_half * sine_portion, second_half * cosine_table + first_half * sine_portion], axis=-1)

def rms_scale(values):
    return lax.rsqrt(lax.optimization_barrier(jnp.mean(values * values, axis=-1, keepdims=True)) + EPS)

def one_layer(inputs, weights, cosine_table, sine_portion, allowed):
    w_query, key_projection_weight, value_projection_weight, output_projection_weight, w_gate, w_up, w_down, gain_one, gain_two = weights
    count_of_rows = inputs.shape[0]
    normalized_input = lower_half(inputs * rms_scale(inputs) * gain_one)
    query_rows = lower_half_backward(matrix_product(normalized_input, w_query)).reshape(count_of_rows, QUERY_HEADS, HEAD_SIZE)
    key_row_block = lower_half_backward(matrix_product(normalized_input, key_projection_weight)).reshape(count_of_rows, KEY_VALUE_HEADS, HEAD_SIZE)
    value_row_block = lower_half_backward(lower_half(matrix_product(normalized_input, value_projection_weight))).reshape(count_of_rows, KEY_VALUE_HEADS, HEAD_SIZE)
    query_rows = lower_half(rotary_embedding(query_rows, cosine_table, sine_portion)).reshape(count_of_rows, KEY_VALUE_HEADS, QUERY_HEADS // KEY_VALUE_HEADS, HEAD_SIZE)
    key_row_block = lower_half(rotary_embedding(key_row_block, cosine_table, sine_portion))
    scores = lower_half_backward(jnp.einsum('qghd,kgd->ghqk', query_rows, key_row_block, precision=HIGH) * SCALE)
    scores = jnp.where(allowed, scores, MASKED)
    row_max = lax.optimization_barrier(jnp.max(scores, axis=-1, keepdims=True))
    exponent = jnp.exp(scores - row_max)
    attention = lower_half(exponent / lax.optimization_barrier(jnp.sum(exponent, axis=-1, keepdims=True)))
    mixture = jnp.einsum('ghqk,kgd->qghd', attention, value_row_block, precision=HIGH)
    mixture = lower_half_backward(lower_half(mixture)).reshape(count_of_rows, QUERY_HEADS * HEAD_SIZE)
    middle = inputs + lower_half_backward(matrix_product(mixture, output_projection_weight))
    normed_two = lower_half(middle * rms_scale(middle) * gain_two)
    gate_pre = lower_half_backward(matrix_product(normed_two, w_gate))
    up_pre = lower_half_backward(matrix_product(normed_two, w_up))
    hidden = lower_half(jax.nn.silu(gate_pre) * up_pre)
    return middle + lower_half_backward(matrix_product(hidden, w_down))

def one_block(inputs, seq_lengths, weights_first, weights_second):
    row_index = jnp.arange(ROWS, dtype=jnp.int32)
    segment, position = segment_rows(seq_lengths, row_index)
    allowed = (segment[:, None] == segment[None, :]) & (row_index[:, None] >= row_index[None, :])
    cosine_table, sine_portion = rotary_tables(position)
    middle = lower_half_backward(lower_half(one_layer(inputs, weights_first, cosine_table, sine_portion, allowed)))
    return one_layer(middle, weights_second, cosine_table, sine_portion, allowed)

def forward(inputs, seq_lengths, weights_first, weights_second):
    checked = jax.checkpoint(one_block)

    def run_item(item):
        return checked(item[0], item[1], weights_first, weights_second)
    return lax.map(run_item, (inputs, seq_lengths))

def reference(boundary, lengths, query_weight, key_matrix, value_matrix, output_weight, gate_weight, up_weight, down_weight, first_gain, second_gain):
    stacks = (query_weight, key_matrix, value_matrix, output_weight, gate_weight, up_weight, down_weight, first_gain, second_gain)
    weights_first = tuple((item[0].astype(jnp.float32) for item in stacks))
    weights_second = tuple((item[1].astype(jnp.float32) for item in stacks))
    inputs = boundary[0].astype(jnp.float32).reshape(MB * GROUPS, ROWS, MODEL_WIDTH)
    seq_lengths = jnp.transpose(lengths, (1, 0, 2)).reshape(MB * GROUPS, SEQS).astype(jnp.int32)
    row_index = jnp.arange(ROWS, dtype=jnp.int32)

    def segment_only(single):
        return segment_rows(single, row_index)[0]
    segment = jax.vmap(segment_only)(seq_lengths)
    live = (segment < SEQS).astype(jnp.float32)
    cotangent = boundary[1].astype(jnp.float32).reshape(MB * GROUPS, ROWS, MODEL_WIDTH) * live[:, :, None]

    def whole(layer_input, first_set, second_set):
        return forward(layer_input, seq_lengths, first_set, second_set)
    outputs, pullback = jax.vjp(whole, inputs, weights_first, weights_second)
    grad_inputs, grads_first, grads_second = pullback(cotangent)
    edges = jnp.stack([grad_inputs, outputs]).reshape(2, MB, GROUPS, ROWS, MODEL_WIDTH).astype(jnp.bfloat16)
    stacked = tuple((jnp.stack([one_grad, two_grad]) for one_grad, two_grad in zip(grads_first, grads_second)))
    return (edges, stacked[0], stacked[1], stacked[2], stacked[3], stacked[4], stacked[5], stacked[6], stacked[7], stacked[8])
```

```python
import jax
import jax.numpy as jnp
from jax import lax
from jax.sharding import PartitionSpec as P

QUERY_HEADS = 15
KEY_VALUE_HEADS = 5
HEAD_SIZE = 64


EPS = 1e-05
SCALE = 0.125
MASKED = -1e30


BF16 = jnp.bfloat16
F32 = jnp.float32
WIDTH = 960
PART = 120
PADDED = 128
SPREAD = 1024
UNIT = 1280
FF_PART = 320
FF_QUARTER = 80
DOWN_COLS = 512
DOWN_SKIP = 64
ROW_QUARTER = 32
KV_WIDTH = KEY_VALUE_HEADS * HEAD_SIZE
DISTANCES = (0, -1, 1, 2)


def segment_rows(seq_lengths, row_index):
    seq_ends = jnp.cumsum(seq_lengths)
    starts = seq_ends - seq_lengths
    segment = jnp.sum((row_index[:, None] >= seq_ends[None, :]).astype(jnp.int32), axis=1)
    slot_ids = jnp.arange(seq_lengths.shape[0], dtype=jnp.int32)
    row_start = jnp.sum(
        jnp.where(segment[:, None] == slot_ids[None, :], starts[None, :], 0), axis=1
    )
    return (segment, row_index - row_start)


def rotary_tables(position):
    frequency = 10000.0 ** (-2.0 * jnp.arange(HEAD_SIZE // 2, dtype=jnp.float32) / HEAD_SIZE)
    angles = position.astype(jnp.float32)[:, None] * frequency[None, :]
    return (jnp.cos(angles)[:, None, :], jnp.sin(angles)[:, None, :])


def rotary_embedding(vector, cosine_table, sine_portion):
    first_half = vector[..., : HEAD_SIZE // 2]
    second_half = vector[..., HEAD_SIZE // 2 :]
    return jnp.concatenate(
        [
            first_half * cosine_table - second_half * sine_portion,
            second_half * cosine_table + first_half * sine_portion,
        ],
        axis=-1,
    )


def rotary_embedding_backward(grad, cosine_table, sine_portion):
    first_half = grad[..., : HEAD_SIZE // 2]
    second_half = grad[..., HEAD_SIZE // 2 :]
    return jnp.concatenate(
        [
            first_half * cosine_table + second_half * sine_portion,
            second_half * cosine_table - first_half * sine_portion,
        ],
        axis=-1,
    )


def rms_scale(values):
    return lax.rsqrt(jnp.mean(values * values, axis=-1, keepdims=True) + EPS)


def outer_sum(left, right):
    return lax.dot_general(
        left, right, (((0,), (0,)), ((), ())), preferred_element_type=jnp.float32
    )


def backward_product(grad, weight):
    return lax.dot_general(
        grad, weight, (((1,), (1,)), ((), ())), preferred_element_type=jnp.float32
    )


def z_step(value, step):
    return lax.ppermute(value, "fsdp", [(i, (i + 2 * step) % 8) for i in range(8)])


def x_step(value, step):
    return lax.ppermute(value, "dp", [(i, (i + 2 * step) % 8) for i in range(8)])


def y_near(value):
    return lax.ppermute(value, "fsdp", [(i, i ^ 1) for i in range(8)])


def y_far(value):
    return lax.ppermute(value, "dp", [(i, i ^ 1) for i in range(8)])


def sibling(value):
    return lax.ppermute(value, "section", [(0, 1), (1, 0)])


def ring_gather(step, way, block):
    before = step(block, 1)
    after = step(block, -1)
    far = step(before if way == 1 else after, way)
    return [block, before, after, far]


def ring_sum(step, way, chunk):
    relayed = step(chunk(2).astype(BF16), way)
    other = step(chunk(-way).astype(BF16), -way)
    nearer = (chunk(way).astype(F32) + relayed.astype(F32)).astype(BF16)
    return chunk(0).astype(F32) + other.astype(F32) + step(nearer, way).astype(F32)


def direct_sum(step, chunk):
    total = chunk(0).astype(F32)
    for distance in (1, -1, 2):
        total = total + step(chunk(distance).astype(BF16), distance).astype(F32)
    return total


class Place:
    def __init__(self):
        self.section = lax.axis_index("section")
        self.shard = lax.axis_index("fsdp")
        dp = lax.axis_index("dp")
        self.z, self.y = self.shard // 2, self.shard % 2
        self.x = dp // 2
        self.first = self.section == 0
        self.near_shards = jnp.stack(
            [(self.z + d) % 4 * 2 + (self.y + near) % 2 for d in DISTANCES for near in (0, 1)]
        )
        row = lax.broadcasted_iota(jnp.int32, (WIDTH, SPREAD), 0)
        column = jnp.arange(SPREAD, dtype=jnp.int32)
        self.z_shard = jnp.repeat(self.near_shards, PADDED)
        self.by_z = (
            (row // PART == self.z_shard[None]) & (row % PART == (column % PADDED)[None])
        ).astype(BF16)
        quarters = jnp.repeat(jnp.stack([(self.x + d) % 4 for d in DISTANCES]), SPREAD // 4)
        shards = jnp.tile(jnp.repeat(self.near_shards, ROW_QUARTER), 4)
        inner = quarters * ROW_QUARTER + column % ROW_QUARTER
        self.by_x = ((row // PART == shards[None]) & (row % PART == inner[None])).astype(BF16)

    def role(self, zero, one):
        return jnp.where(self.first, zero, one)

    def roles(self, mine, other):
        return (jnp.where(self.first, mine, other), jnp.where(self.first, other, mine))


def spread(value, places):
    return jnp.dot(value, places, preferred_element_type=F32).astype(BF16)


def unspread(value, places):
    high = lax.reduce_precision(value, 8, 7)
    both = jnp.concatenate([high.astype(BF16), (value - high).astype(BF16)], axis=1)
    return backward_product(both, jnp.concatenate([places, places], axis=1))


def product(left, right):
    return jnp.dot(left, right, preferred_element_type=F32)


def gate(value, *others):
    late = False
    for other in others:
        corner = other[(0,) * other.ndim]
        late = late | (corner != corner)
    return jax.tree.map(lambda part: jnp.where(late, jnp.zeros_like(part), part), value)


def gather_first(place, own):
    pair = jnp.concatenate([own, y_near(own)], axis=0)
    blocks = ring_gather(z_step, 1, pair)
    mine = jnp.concatenate(blocks, axis=0)
    return (mine, sibling(mine), blocks[-1])


def gather_down(place, own):
    other = y_near(own)
    low, high = (jnp.where(place.y == 0, own, other), jnp.where(place.y == 0, other, own))
    pair = jnp.concatenate([low, high], axis=0)
    blocks = ring_gather(z_step, -1, pair)
    mine = jnp.concatenate(blocks, axis=0)
    return (mine, sibling(mine), blocks[-1])


def gather_column(place, own):
    quarter = lax.dynamic_slice_in_dim(own, place.x * ROW_QUARTER, ROW_QUARTER, 0)
    pair = jnp.concatenate([quarter, y_near(quarter)], axis=0)
    return ring_gather(z_step, -1, pair)


def gather_wide(column):
    before = x_step(column, 1)
    after = x_step(column, -1)
    half = column.shape[0] // 2
    far = [x_step(before[:half], 1), x_step(after[half:], -1)]
    mine = jnp.concatenate([column, before, after] + far, axis=0)
    return (mine, sibling(mine), far[0])


def layer_weights(place, column, first, down):
    one = gather_first(place, first)
    two = gather_wide(column)
    low = gather_down(place, down)
    gains = one[0].reshape(8, PADDED, UNIT)[:, PART : PART + 2, :PADDED]
    gains = backward_product(gains.transpose(1, 0, 2).reshape(2, SPREAD), place.by_z)
    return (one, two, low, gains[:1], gains[1:])


def gather_rows(own):
    pair = jnp.concatenate([own, y_near(own)], axis=0)
    return jnp.concatenate(ring_gather(z_step, 1, pair), axis=0)


def scatter_rows(partial):
    parts = partial.reshape(4, -1, partial.shape[1])
    pair = ring_sum(z_step, -1, lambda distance: parts[DISTANCES.index(distance)])
    rows = pair.shape[0] // 2
    return pair[:rows] + y_near(pair[rows:].astype(BF16)).astype(F32)


def down_columns(place, hidden):
    size = 2 * FF_PART
    return jnp.concatenate(
        [
            lax.dynamic_slice_in_dim(hidden, (place.z + d) % 4 * size, size, 1)
            for d in DISTANCES
        ],
        axis=1,
    )


def forward_layer(place, inputs, weights, cosine_table, sine_portion, allowed):
    one, two, low, gain_one, gain_two = weights
    count_of_rows = inputs.shape[0]
    inv_one = rms_scale(inputs)
    normed_one = spread((inputs * inv_one * gain_one).astype(BF16), place.by_z)
    query_key, value_part = place.roles(product(normed_one, one[0]), product(normed_one, one[1]))
    value_part = value_part[:, WIDTH:].astype(BF16)
    turned = rotary_embedding(
        query_key.reshape(count_of_rows, QUERY_HEADS + KEY_VALUE_HEADS, HEAD_SIZE),
        cosine_table,
        sine_portion,
    ).astype(BF16)
    query_rows = turned[:, :QUERY_HEADS].reshape(
        count_of_rows, KEY_VALUE_HEADS, QUERY_HEADS // KEY_VALUE_HEADS, HEAD_SIZE
    )
    key_portion = turned[:, QUERY_HEADS:].reshape(count_of_rows, KV_WIDTH)
    key_value = gather_rows(jnp.concatenate([key_portion, value_part], axis=1))
    key_row_block = key_value[:, :KV_WIDTH].reshape(-1, KEY_VALUE_HEADS, HEAD_SIZE)
    value_row_block = key_value[:, KV_WIDTH:].reshape(-1, KEY_VALUE_HEADS, HEAD_SIZE)
    scores = (
        jnp.einsum("qghd,kgd->ghqk", query_rows, key_row_block, preferred_element_type=F32)
        * SCALE
    )
    scores = jnp.where(allowed, scores, MASKED)
    row_max = jnp.max(scores, axis=-1, keepdims=True)
    exponent = jnp.exp(scores - row_max)
    total = jnp.sum(exponent, axis=-1, keepdims=True)
    attention = (exponent / total).astype(BF16)
    log_total = row_max + jnp.log(total)
    mixture = jnp.einsum(
        "ghqk,kgd->qghd", attention, value_row_block, preferred_element_type=F32
    )
    mixture = spread(
        mixture.astype(BF16).reshape(count_of_rows, QUERY_HEADS * HEAD_SIZE), place.by_z
    )
    unused, projected = place.roles(product(mixture, one[0]), product(mixture, one[1]))
    middle = inputs + projected[:, :WIDTH]
    inv_two = rms_scale(middle)
    normed_two = spread((middle * inv_two * gain_two).astype(BF16), place.by_x)
    gate_pre, up_pre = place.roles(product(normed_two, two[0]), product(normed_two, two[1]))
    hidden = down_columns(place, (jax.nn.silu(gate_pre) * up_pre).astype(BF16))
    left, right = place.roles(product(hidden, low[0]), product(hidden, low[1]))
    result = middle + jnp.concatenate([left, right[:, DOWN_SKIP:]], axis=1)
    stored = (
        inputs,
        inv_one,
        normed_one,
        query_rows,
        key_row_block,
        value_row_block,
        log_total,
        mixture,
        middle,
        inv_two,
        normed_two,
        gate_pre,
        up_pre,
        hidden,
    )
    return (result, stored)


def with_sibling(own, sent):
    return jnp.concatenate([own, sibling(sent)], axis=0)


def norm_backward(grad, unit, inverse, gain):
    scaled = grad * gain
    return inverse * (scaled - unit * jnp.mean(scaled * unit, axis=-1, keepdims=True))


def partial_chunks(left, right):
    size = left.shape[1] // 4

    def chunk(distance):
        at = DISTANCES.index(distance)
        return outer_sum(left[:, at * size : (at + 1) * size], right).astype(BF16)

    return chunk


def by_quarter(place, block, rows):
    quarters = block.reshape(4, rows, block.shape[-1])

    def quarter(distance):
        return lax.dynamic_index_in_dim(quarters, (place.x + distance) % 4, 0, keepdims=False)

    return quarter


def reduce_first(left, right):
    return ring_sum(z_step, 1, partial_chunks(left, right))


def reduce_down(place, left, right):
    pair = ring_sum(z_step, -1, partial_chunks(left, right)).astype(BF16)
    pair = pair.reshape(2, PADDED, UNIT)
    return jnp.concatenate(
        [
            lax.dynamic_index_in_dim(pair, place.y, 0, keepdims=False),
            lax.dynamic_index_in_dim(pair, 1 - place.y, 0, keepdims=False),
        ],
        axis=0,
    ).astype(F32)


def reduce_wide(left, right):
    chunk = partial_chunks(left, right)
    half = SPREAD // 8
    from_before = x_step(outer_sum(left[:, -2 * half : -half], right).astype(BF16), 1)
    from_after = x_step(outer_sum(left[:, -half:], right).astype(BF16), -1)
    after = chunk(1).astype(F32) + jnp.pad(from_before, ((0, half), (0, 0))).astype(F32)
    before = chunk(-1).astype(F32) + jnp.pad(from_after, ((half, 0), (0, 0))).astype(F32)
    column = (
        chunk(0).astype(F32)
        + x_step(after.astype(BF16), 1).astype(F32)
        + x_step(before.astype(BF16), -1).astype(F32)
    )
    parts = column.reshape(4, 2 * ROW_QUARTER, 2 * UNIT)
    pair = ring_sum(z_step, 1, lambda distance: parts[DISTANCES.index(distance)])
    quarter = pair[:ROW_QUARTER] + y_near(pair[ROW_QUARTER:].astype(BF16)).astype(F32)
    return ((from_before, from_after), column, quarter)


def quarter_of(place, pair):
    block = pair[:PADDED] + y_near(pair[PADDED:].astype(BF16)).astype(F32)
    return direct_sum(x_step, by_quarter(place, block, ROW_QUARTER))


def finish(place, quarter):
    low = quarter.astype(BF16)
    piece = (low.astype(F32) + y_far(low).astype(F32)).astype(BF16)
    whole = jnp.zeros((4,) + piece.shape, BF16)
    for distance in DISTANCES:
        block = step_from(piece, distance)
        whole = lax.dynamic_update_slice_in_dim(
            whole, block[None], (place.x + distance) % 4, 0
        )
    return whole.reshape(-1, piece.shape[-1])


def step_from(piece, distance):
    return piece if distance == 0 else x_step(piece, -distance)


def backward_layer(
    place, grad_out, weights, stored, waits, cosine_table, sine_portion, allowed
):
    one, two, low, gain_one, gain_two = weights
    (
        inputs,
        inv_one,
        normed_one,
        query_rows,
        key_row_block,
        value_row_block,
        log_total,
        mixture,
        middle,
        inv_two,
        normed_two,
        gate_pre,
        up_pre,
        hidden,
    ) = stored
    count_of_rows = grad_out.shape[0]
    grad_low = grad_out.astype(BF16)
    left_low = grad_low[:, :DOWN_COLS]
    right_low = grad_low[:, WIDTH - DOWN_COLS :]
    right_once = jnp.where(jnp.arange(DOWN_COLS)[None] < DOWN_SKIP, 0, right_low)
    mine_low, other_low = place.roles(left_low, right_once)
    hidden_grads = backward_product(mine_low, low[0]) + backward_product(other_low, low[1])
    size = 2 * FF_PART
    hidden_grad = jnp.zeros_like(hidden_grads)
    for at, distance in enumerate(DISTANCES):
        hidden_grad = lax.dynamic_update_slice_in_dim(
            hidden_grad,
            hidden_grads[:, at * size : (at + 1) * size],
            (place.z + distance) % 4 * size,
            1,
        )
    sigmoid_gate = jax.nn.sigmoid(gate_pre)
    grad_gate = (
        hidden_grad * up_pre * sigmoid_gate * (1.0 + gate_pre * (1.0 - sigmoid_gate))
    ).astype(BF16)
    grad_up = (hidden_grad * gate_pre * sigmoid_gate).astype(BF16)
    mine, other = place.roles(grad_gate, grad_up)
    spread_two = backward_product(mine, two[0]) + backward_product(other, two[1])
    left_rows = with_sibling(*2 * (jnp.concatenate([hidden, normed_two], axis=1),))
    right_rows = with_sibling(
        jnp.concatenate([place.role(left_low, right_low), mine], axis=1),
        jnp.concatenate([place.role(right_low, left_low), other], axis=1),
    )
    down = reduce_down(place, left_rows[:, : 2 * UNIT], right_rows[:, :DOWN_COLS])
    wide = reduce_wide(left_rows[:, 2 * UNIT :], right_rows[:, DOWN_COLS:])
    grad_normed_two = unspread(spread_two, place.by_x)
    unit_two = middle * inv_two
    grad_gain_two = jnp.sum(grad_normed_two * unit_two, axis=0)
    grad_normed_two = gate(grad_normed_two, *waits[0])
    grad_mid = grad_out + norm_backward(grad_normed_two, unit_two, inv_two, gain_two)
    none_narrow = jnp.zeros((count_of_rows, KV_WIDTH), BF16)
    output_side = jnp.concatenate([grad_mid.astype(BF16), none_narrow], axis=1)
    none = jnp.zeros_like(output_side)
    mine, other = place.roles(none, output_side)
    grad_mixture = (
        unspread(backward_product(mine, one[0]) + backward_product(other, one[1]), place.by_z)
        .astype(BF16)
        .reshape(count_of_rows, KEY_VALUE_HEADS, QUERY_HEADS // KEY_VALUE_HEADS, HEAD_SIZE)
    )
    scores = (
        jnp.einsum("qghd,kgd->ghqk", query_rows, key_row_block, preferred_element_type=F32)
        * SCALE
    )
    scores = jnp.where(allowed, scores, MASKED)
    attention_full = jnp.exp(scores - log_total)
    attention = attention_full.astype(BF16)
    value_gradient = jnp.einsum(
        "ghqk,qghd->kgd", attention, grad_mixture, preferred_element_type=F32
    )
    grad_attention = jnp.einsum(
        "qghd,kgd->ghqk", grad_mixture, value_row_block, preferred_element_type=F32
    )
    row_dots = jnp.sum(attention_full * grad_attention, axis=-1, keepdims=True)
    grad_scores = (attention_full * (grad_attention - row_dots)).astype(BF16)
    key_gradient = (
        jnp.einsum("ghqk,qghd->kgd", grad_scores, query_rows, preferred_element_type=F32)
        * SCALE
    )
    far, column, wide = wide
    key_gradient = gate(key_gradient, *waits[1], *far)
    key_value = scatter_rows(
        jnp.concatenate(
            [key_gradient.reshape(-1, KV_WIDTH), value_gradient.reshape(-1, KV_WIDTH)], axis=1
        ).astype(BF16)
    )
    grad_queries = (
        jnp.einsum("ghqk,kgd->qghd", grad_scores, key_row_block, preferred_element_type=F32)
        * SCALE
    )
    key_gradient, value_low = (key_value[:, :KV_WIDTH], key_value[:, KV_WIDTH:].astype(BF16))
    grad_query_key = rotary_embedding_backward(
        jnp.concatenate(
            [
                grad_queries.reshape(count_of_rows, QUERY_HEADS, HEAD_SIZE),
                key_gradient.reshape(count_of_rows, KEY_VALUE_HEADS, HEAD_SIZE),
            ],
            axis=1,
        ),
        cosine_table,
        sine_portion,
    )
    grad_query_key = grad_query_key.reshape(count_of_rows, UNIT).astype(BF16)
    value_side = jnp.concatenate([jnp.zeros((count_of_rows, WIDTH), BF16), value_low], axis=1)
    mine, other = place.roles(grad_query_key, value_side)
    grad_normed = unspread(
        backward_product(mine, one[0]) + backward_product(other, one[1]), place.by_z
    )
    unit_one = inputs * inv_one
    grad_gain_one = jnp.sum(grad_normed * unit_one, axis=0)
    grad_in = grad_mid + norm_backward(grad_normed, unit_one, inv_one, gain_one)
    gain_rows = jnp.stack([grad_gain_one.reshape(8, PART), grad_gain_two.reshape(8, PART)], axis=1)
    gain_rows = jnp.pad(gain_rows.reshape(16, PART).astype(BF16), ((0, 0), (0, UNIT - PART)))
    number = jnp.arange(16, dtype=jnp.int32)[:, None]
    inner = (jnp.arange(SPREAD, dtype=jnp.int32) % PADDED)[None]
    gain_place = (number // 2 == place.z_shard[None]) & (PART + number % 2 == inner)
    left_rows = with_sibling(
        jnp.concatenate([place.role(normed_one, mixture), normed_one], axis=1),
        jnp.concatenate([place.role(mixture, normed_one), normed_one], axis=1),
    )
    right_rows = with_sibling(
        jnp.concatenate([place.role(grad_query_key, output_side), place.role(none, value_side)], 1),
        jnp.concatenate([place.role(output_side, grad_query_key), place.role(value_side, none)], 1),
    )
    left_rows = gate(left_rows, *waits[2])
    left_rows = jnp.concatenate(
        [left_rows[:, :SPREAD], left_rows[:, SPREAD:], gain_place.astype(BF16)], axis=0
    )
    right_rows = jnp.concatenate([right_rows[:, :UNIT], right_rows[:, UNIT:], gain_rows], axis=0)
    return (
        gate(grad_in, down, column),
        (reduce_first(left_rows, right_rows), down, wide),
    )


def per_device(
    boundary,
    lengths,
    query_weight,
    key_matrix,
    value_matrix,
    output_weight,
    gate_weight,
    up_weight,
    down_weight,
    first_gain,
    second_gain,
):
    place = Place()
    first = place.first
    slab = boundary[0, :, 0]
    rows_dev = slab.shape[1]
    exchanged = sibling(jnp.where(first, slab[1], slab[0]))
    inputs = jnp.where(first, slab[0], exchanged).astype(F32)
    cotangent = jnp.where(first, exchanged, slab[1]).astype(F32)

    gains = jnp.pad(
        jnp.concatenate([first_gain, second_gain], axis=0), ((0, 6), (0, UNIT - PART))
    )
    role_packs = (
        (
            jnp.concatenate(
                [jnp.concatenate([query_weight[0], key_matrix[0]], axis=1), gains], axis=0
            ),
            jnp.pad(gate_weight[0], ((0, PADDED - PART), (0, 0))),
            down_weight[0, :, :DOWN_COLS],
        ),
        (
            jnp.concatenate(
                [jnp.concatenate([output_weight[0], value_matrix[0]], axis=1), gains], axis=0
            ),
            jnp.pad(up_weight[0], ((0, PADDED - PART), (0, 0))),
            down_weight[0, :, WIDTH - DOWN_COLS :],
        ),
    )
    layer_packs = ([], [])
    for zero, one in zip(*role_packs):
        kept = jnp.where(first, zero, one)
        other = sibling(jnp.where(first, one, zero))
        layer_packs[0].append(jnp.where(first, kept, other))
        layer_packs[1].append(jnp.where(first, other, kept))
    first_pack, wide_pack, down_pack = layer_packs[0]
    blocks = gather_column(place, wide_pack)
    column = jnp.concatenate(blocks, axis=0)
    weights_first = layer_weights(place, column, first_pack, gate(down_pack, blocks[3]))
    first_pack, wide_pack, down_pack = layer_packs[1]
    blocks = gather_column(place, gate(wide_pack, blocks[3]))

    seq_lengths = jnp.where(first, lengths[0, 0], lengths[0, 1])
    inner = jnp.arange(rows_dev, dtype=jnp.int32)
    own_rows = place.shard * rows_dev + inner
    all_rows = (place.near_shards[:, None] * rows_dev + inner[None]).reshape(-1)
    segment_mine, position_mine = segment_rows(seq_lengths, own_rows)
    segment_all, unused_position = segment_rows(seq_lengths, all_rows)
    allowed = (segment_mine[:, None] == segment_all[None, :]) & (
        own_rows[:, None] >= all_rows[None, :]
    )
    cosine_table, sine_portion = rotary_tables(position_mine)
    live_rows = (segment_mine < seq_lengths.shape[0]).astype(F32)

    geometry = (cosine_table, sine_portion, allowed)
    middle, stored_first = forward_layer(place, inputs, weights_first, *geometry)
    blocks[0], first_pack, down_pack = gate(
        (blocks[0], first_pack, down_pack), stored_first[4]
    )
    column = jnp.concatenate(blocks, axis=0)
    weights_second = layer_weights(place, column, first_pack, down_pack)
    middle = middle.astype(BF16).astype(F32)
    result, stored_second = forward_layer(place, middle, weights_second, *geometry)
    grad, pending = backward_layer(
        place, cotangent * live_rows[:, None], weights_second, stored_second, ((), (), ()), *geometry
    )
    pair, down, wide = pending
    wide = jnp.concatenate([quarter_of(place, down), wide], axis=1)
    low = quarter_of(place, pair)
    early_second, late_second = (finish(place, wide), finish(place, low))
    waits = ((pair,), (wide, low), (early_second, late_second))
    grad = grad.astype(BF16).astype(F32)
    grad, remaining = backward_layer(
        place, grad, weights_first, stored_first, waits, *geometry
    )

    ends = (grad.astype(BF16), result.astype(BF16))
    received = sibling(jnp.where(first, ends[1], ends[0]))
    boundary_out = jnp.where(
        first, jnp.stack([ends[0], received]), jnp.stack([received, ends[1]])
    )[None, :, None]

    pair, down, wide = remaining
    early_first = finish(place, jnp.concatenate([quarter_of(place, down), wide], axis=1))
    late_first = finish(place, quarter_of(place, pair))
    sums = []
    for for_first, for_second in ((early_first, early_second), (late_first, late_second)):
        own = jnp.where(first, for_first, for_second)
        other = sibling(jnp.where(first, for_second, for_first))
        sums.append([value.astype(F32) for value in place.roles(own, other)])
    down_left, down_right = [value[:, :UNIT].reshape(FF_PART, DOWN_COLS) for value in sums[0]]
    gate_sum, up_sum = [value[:, UNIT:] for value in sums[0]]
    query_key, output_value = sums[1]
    gain_sums = query_key[PART : PART + 2, :PART] + output_value[PART : PART + 2, :PART]
    return (
        boundary_out,
        query_key[None, :PART, :WIDTH],
        query_key[None, :PART, WIDTH:],
        output_value[None, :PART, WIDTH:],
        output_value[None, :PART, :WIDTH],
        gate_sum[None, :PART],
        up_sum[None, :PART],
        jnp.concatenate([down_left, down_right[:, DOWN_SKIP:]], axis=1)[None],
        gain_sums[:1],
        gain_sums[1:],
    )


def solution(mesh):
    placed = (
        P("section", None, "dp", "fsdp", None),
        P("dp", None, None),
        P("section", "fsdp", None),
        P("section", "fsdp", None),
        P("section", "fsdp", None),
        P("section", "fsdp", None),
        P("section", "fsdp", None),
        P("section", "fsdp", None),
        P("section", "fsdp", None),
        P("section", "fsdp"),
        P("section", "fsdp"),
    )
    return jax.shard_map(
        per_device,
        mesh=mesh,
        in_specs=placed,
        out_specs=(
            P("section", None, "dp", "fsdp", None),
            P("section", "fsdp", None),
            P("section", "fsdp", None),
            P("section", "fsdp", None),
            P("section", "fsdp", None),
            P("section", "fsdp", None),
            P("section", "fsdp", None),
            P("section", "fsdp", None),
            P("section", "fsdp"),
            P("section", "fsdp"),
        ),
        check_vma=False,
    )
```

```python
import jax
import jax.numpy as jnp
from jax import lax
from jax.sharding import PartitionSpec as P

QUERY_HEADS = 15
KEY_VALUE_HEADS = 5
HEAD_SIZE = 64


EPS = 1e-05
SCALE = 0.125
MASKED = -1e30


BF16 = jnp.bfloat16
F32 = jnp.float32
WIDTH = 960
PART = 120
PADDED = 128
SPREAD = 1024
UNIT = 1280
FF_PART = 320
FF_QUARTER = 80
DOWN_COLS = 512
DOWN_SKIP = 64
ROW_QUARTER = 32
KV_WIDTH = KEY_VALUE_HEADS * HEAD_SIZE
DISTANCES = (0, -1, 1, 2)


def segment_rows(seq_lengths, row_index):
    seq_ends = jnp.cumsum(seq_lengths)
    starts = seq_ends - seq_lengths
    segment = jnp.sum((row_index[:, None] >= seq_ends[None, :]).astype(jnp.int32), axis=1)
    slot_ids = jnp.arange(seq_lengths.shape[0], dtype=jnp.int32)
    row_start = jnp.sum(
        jnp.where(segment[:, None] == slot_ids[None, :], starts[None, :], 0), axis=1
    )
    return (segment, row_index - row_start)


def rotary_tables(position):
    frequency = 10000.0 ** (-2.0 * jnp.arange(HEAD_SIZE // 2, dtype=jnp.float32) / HEAD_SIZE)
    angles = position.astype(jnp.float32)[:, None] * frequency[None, :]
    return (jnp.cos(angles)[:, None, :], jnp.sin(angles)[:, None, :])


def rotary_embedding(vector, cosine_table, sine_portion):
    first_half = vector[..., : HEAD_SIZE // 2]
    second_half = vector[..., HEAD_SIZE // 2 :]
    return jnp.concatenate(
        [
            first_half * cosine_table - second_half * sine_portion,
            second_half * cosine_table + first_half * sine_portion,
        ],
        axis=-1,
    )


def rotary_embedding_backward(grad, cosine_table, sine_portion):
    first_half = grad[..., : HEAD_SIZE // 2]
    second_half = grad[..., HEAD_SIZE // 2 :]
    return jnp.concatenate(
        [
            first_half * cosine_table + second_half * sine_portion,
            second_half * cosine_table - first_half * sine_portion,
        ],
        axis=-1,
    )


def rms_scale(values):
    return lax.rsqrt(jnp.mean(values * values, axis=-1, keepdims=True) + EPS)


def outer_sum(left, right):
    return lax.dot_general(
        left, right, (((0,), (0,)), ((), ())), preferred_element_type=jnp.float32
    )


def backward_product(grad, weight):
    return lax.dot_general(
        grad, weight, (((1,), (1,)), ((), ())), preferred_element_type=jnp.float32
    )


def z_step(value, step):
    return lax.ppermute(value, "fsdp", [(i, (i + 2 * step) % 8) for i in range(8)])


def x_step(value, step):
    return lax.ppermute(value, "dp", [(i, (i + 2 * step) % 8) for i in range(8)])


def y_near(value):
    return lax.ppermute(value, "fsdp", [(i, i ^ 1) for i in range(8)])


def y_far(value):
    return lax.ppermute(value, "dp", [(i, i ^ 1) for i in range(8)])


def sibling(value):
    return lax.ppermute(value, "section", [(0, 1), (1, 0)])


def ring_gather(step, way, block):
    before = step(block, 1)
    after = step(block, -1)
    far = step(before if way == 1 else after, way)
    return [block, before, after, far]


def ring_sum(step, way, chunk):
    relayed = step(chunk(2).astype(BF16), way)
    other = step(chunk(-way).astype(BF16), -way)
    nearer = (chunk(way).astype(F32) + relayed.astype(F32)).astype(BF16)
    return chunk(0).astype(F32) + other.astype(F32) + step(nearer, way).astype(F32)


class Place:
    def __init__(self):
        self.section = lax.axis_index("section")
        self.shard = lax.axis_index("fsdp")
        dp = lax.axis_index("dp")
        self.z, self.y = self.shard // 2, self.shard % 2
        self.x = dp // 2
        self.first = self.section == 0
        self.near_shards = jnp.stack(
            [(self.z + d) % 4 * 2 + (self.y + near) % 2 for d in DISTANCES for near in (0, 1)]
        )
        row = lax.broadcasted_iota(jnp.int32, (WIDTH, SPREAD), 0)
        column = jnp.arange(SPREAD, dtype=jnp.int32)
        self.z_shard = jnp.repeat(self.near_shards, PADDED)
        self.by_z = (
            (row // PART == self.z_shard[None]) & (row % PART == (column % PADDED)[None])
        ).astype(BF16)
        quarters = jnp.repeat(jnp.stack([(self.x + d) % 4 for d in DISTANCES]), SPREAD // 4)
        shards = jnp.tile(jnp.repeat(jnp.arange(8, dtype=jnp.int32), ROW_QUARTER), 4)
        inner = quarters * ROW_QUARTER + column % ROW_QUARTER
        self.by_x = ((row // PART == shards[None]) & (row % PART == inner[None])).astype(BF16)

    def role(self, zero, one):
        return jnp.where(self.first, zero, one)

    def roles(self, mine, other):
        return (jnp.where(self.first, mine, other), jnp.where(self.first, other, mine))


def spread(value, places):
    return jnp.dot(value, places, preferred_element_type=F32).astype(BF16)


def unspread(value, places):
    high = lax.reduce_precision(value, 8, 7)
    both = jnp.concatenate([high.astype(BF16), (value - high).astype(BF16)], axis=1)
    return backward_product(both, jnp.concatenate([places, places], axis=1))


def product(left, right):
    return jnp.dot(left, right, preferred_element_type=F32)


def gate(value, *others):
    late = False
    for other in others:
        corner = other[(0,) * other.ndim]
        late = late | (corner != corner)
    return jax.tree.map(lambda part: jnp.where(late, jnp.zeros_like(part), part), value)


def gather_first(place, own):
    pair = jnp.concatenate([own, y_near(own)], axis=0)
    blocks = ring_gather(z_step, 1, pair)
    mine = jnp.concatenate(blocks, axis=0)
    return (mine, sibling(mine), blocks[-1])


def gather_column(place, own):
    quarter = lax.dynamic_slice_in_dim(own, place.x * ROW_QUARTER, ROW_QUARTER, 0)
    return lax.all_gather(quarter, "fsdp", axis=0, tiled=True)


def gather_wide(column):
    before = x_step(column, 1)
    after = x_step(column, -1)
    half = column.shape[0] // 2
    far = [x_step(before[:half], 1), x_step(after[half:], -1)]
    mine = jnp.concatenate([column, before, after] + far, axis=0)
    return (mine, sibling(mine), far[0])


def layer_weights(place, first, column, low):
    one = gather_first(place, first)
    two = gather_wide(column)
    gains = one[0].reshape(8, PADDED, UNIT)[:, PART : PART + 2, :PADDED]
    gains = backward_product(gains.transpose(1, 0, 2).reshape(2, SPREAD), place.by_z)
    return (one, two, (low, sibling(low)), gains[:1], gains[1:])


def gather_rows(own):
    pair = jnp.concatenate([own, y_near(own)], axis=0)
    return jnp.concatenate(ring_gather(z_step, 1, pair), axis=0)


def scatter_rows(partial):
    parts = partial.reshape(4, -1, partial.shape[1])
    pair = ring_sum(z_step, -1, lambda distance: parts[DISTANCES.index(distance)])
    rows = pair.shape[0] // 2
    return pair[:rows] + y_near(pair[rows:].astype(BF16)).astype(F32)


def forward_layer(place, inputs, weights, cosine_table, sine_portion, allowed):
    one, two, low, gain_one, gain_two = weights
    count_of_rows = inputs.shape[0]
    inv_one = rms_scale(inputs)
    normed_one = spread((inputs * inv_one * gain_one).astype(BF16), place.by_z)
    query_key, value_part = place.roles(product(normed_one, one[0]), product(normed_one, one[1]))
    value_part = value_part[:, WIDTH:].astype(BF16)
    turned = rotary_embedding(
        query_key.reshape(count_of_rows, QUERY_HEADS + KEY_VALUE_HEADS, HEAD_SIZE),
        cosine_table,
        sine_portion,
    ).astype(BF16)
    query_rows = turned[:, :QUERY_HEADS].reshape(
        count_of_rows, KEY_VALUE_HEADS, QUERY_HEADS // KEY_VALUE_HEADS, HEAD_SIZE
    )
    key_portion = turned[:, QUERY_HEADS:].reshape(count_of_rows, KV_WIDTH)
    key_value = gather_rows(jnp.concatenate([key_portion, value_part], axis=1))
    key_row_block = key_value[:, :KV_WIDTH].reshape(-1, KEY_VALUE_HEADS, HEAD_SIZE)
    value_row_block = key_value[:, KV_WIDTH:].reshape(-1, KEY_VALUE_HEADS, HEAD_SIZE)
    scores = (
        jnp.einsum("qghd,kgd->ghqk", query_rows, key_row_block, preferred_element_type=F32)
        * SCALE
    )
    scores = jnp.where(allowed, scores, MASKED)
    row_max = jnp.max(scores, axis=-1, keepdims=True)
    exponent = jnp.exp(scores - row_max)
    total = jnp.sum(exponent, axis=-1, keepdims=True)
    attention = (exponent / total).astype(BF16)
    log_total = row_max + jnp.log(total)
    mixture = jnp.einsum(
        "ghqk,kgd->qghd", attention, value_row_block, preferred_element_type=F32
    )
    mixture = spread(
        mixture.astype(BF16).reshape(count_of_rows, QUERY_HEADS * HEAD_SIZE), place.by_z
    )
    unused, projected = place.roles(product(mixture, one[0]), product(mixture, one[1]))
    middle = inputs + projected[:, :WIDTH]
    inv_two = rms_scale(middle)
    normed_two = spread((middle * inv_two * gain_two).astype(BF16), place.by_x)
    gate_pre, up_pre = place.roles(product(normed_two, two[0]), product(normed_two, two[1]))
    hidden = (jax.nn.silu(gate_pre) * up_pre).astype(BF16)
    left, right = place.roles(product(hidden, low[0]), product(hidden, low[1]))
    result = middle + jnp.concatenate([left, right[:, DOWN_SKIP:]], axis=1)
    stored = (
        inputs,
        inv_one,
        normed_one,
        query_rows,
        key_row_block,
        value_row_block,
        log_total,
        mixture,
        middle,
        inv_two,
        normed_two,
        gate_pre,
        up_pre,
        hidden,
    )
    return (result, stored)


def with_sibling(own, sent):
    return jnp.concatenate([own, sibling(sent)], axis=0)


def norm_backward(grad, unit, inverse, gain):
    scaled = grad * gain
    return inverse * (scaled - unit * jnp.mean(scaled * unit, axis=-1, keepdims=True))


def partial_chunks(left, right):
    size = left.shape[1] // 4

    def chunk(distance):
        at = DISTANCES.index(distance)
        return outer_sum(left[:, at * size : (at + 1) * size], right).astype(BF16)

    return chunk


def reduce_first(left, right):
    return ring_sum(z_step, 1, partial_chunks(left, right))


def reduce_down(left, right):
    return lax.psum_scatter(
        outer_sum(left, right).astype(BF16), "fsdp", scatter_dimension=0, tiled=True
    )


def reduce_wide(place, left, right):
    chunk = partial_chunks(left, right)
    half = SPREAD // 8
    from_before = x_step(outer_sum(left[:, -2 * half : -half], right).astype(BF16), 1)
    from_after = x_step(outer_sum(left[:, -half:], right).astype(BF16), -1)
    after = chunk(1).astype(F32) + jnp.pad(from_before, ((0, half), (0, 0))).astype(F32)
    before = chunk(-1).astype(F32) + jnp.pad(from_after, ((half, 0), (0, 0))).astype(F32)
    column = (
        chunk(0).astype(F32)
        + x_step(after.astype(BF16), 1).astype(F32)
        + x_step(before.astype(BF16), -1).astype(F32)
    )
    parts = column.reshape(4, 2, ROW_QUARTER, 2 * UNIT)

    def part(distance):
        return lax.dynamic_index_in_dim(parts, (place.z + distance) % 4, 0, keepdims=False)

    pair = ring_sum(z_step, 1, part)
    mine = lax.dynamic_index_in_dim(pair, place.y, 0, keepdims=False)
    other = lax.dynamic_index_in_dim(pair, 1 - place.y, 0, keepdims=False)
    quarter = mine + y_near(other.astype(BF16)).astype(F32)
    return ((from_before, from_after), column, quarter)


def finish_wide(place, down, wide):
    whole = jnp.zeros((4, ROW_QUARTER, 2 * UNIT), BF16)
    whole = lax.dynamic_update_slice_in_dim(whole, wide.astype(BF16)[None], place.x, 0)
    both = [down.reshape(PADDED, UNIT), whole.reshape(PADDED, 2 * UNIT)]
    return lax.psum(jnp.concatenate(both, axis=1), "dp")


def finish_first(pair, early):
    block = pair[:PADDED] + y_near(pair[PADDED:].astype(BF16)).astype(F32)
    return lax.psum(gate(block, early).astype(BF16), "dp")


def backward_layer(
    place, grad_out, weights, stored, waits, cosine_table, sine_portion, allowed
):
    one, two, low, gain_one, gain_two = weights
    (
        inputs,
        inv_one,
        normed_one,
        query_rows,
        key_row_block,
        value_row_block,
        log_total,
        mixture,
        middle,
        inv_two,
        normed_two,
        gate_pre,
        up_pre,
        hidden,
    ) = stored
    count_of_rows = grad_out.shape[0]
    grad_low = grad_out.astype(BF16)
    left_low = grad_low[:, :DOWN_COLS]
    right_low = grad_low[:, WIDTH - DOWN_COLS :]
    right_once = jnp.where(jnp.arange(DOWN_COLS)[None] < DOWN_SKIP, 0, right_low)
    mine_low, other_low = place.roles(left_low, right_once)
    hidden_grad = backward_product(mine_low, low[0]) + backward_product(other_low, low[1])
    sigmoid_gate = jax.nn.sigmoid(gate_pre)
    grad_gate = (
        hidden_grad * up_pre * sigmoid_gate * (1.0 + gate_pre * (1.0 - sigmoid_gate))
    ).astype(BF16)
    grad_up = (hidden_grad * gate_pre * sigmoid_gate).astype(BF16)
    mine, other = place.roles(grad_gate, grad_up)
    spread_two = backward_product(mine, two[0]) + backward_product(other, two[1])
    left_rows = with_sibling(*2 * (jnp.concatenate([hidden, normed_two], axis=1),))
    right_rows = with_sibling(
        jnp.concatenate([place.role(left_low, right_low), mine], axis=1),
        jnp.concatenate([place.role(right_low, left_low), other], axis=1),
    )
    down = reduce_down(left_rows[:, : 2 * UNIT], right_rows[:, :DOWN_COLS])
    wide = reduce_wide(place, left_rows[:, 2 * UNIT :], right_rows[:, DOWN_COLS:])
    grad_normed_two = unspread(spread_two, place.by_x)
    unit_two = middle * inv_two
    grad_gain_two = jnp.sum(grad_normed_two * unit_two, axis=0)
    grad_normed_two = gate(grad_normed_two, *waits[0])
    grad_mid = grad_out + norm_backward(grad_normed_two, unit_two, inv_two, gain_two)
    none_narrow = jnp.zeros((count_of_rows, KV_WIDTH), BF16)
    output_side = jnp.concatenate([grad_mid.astype(BF16), none_narrow], axis=1)
    none = jnp.zeros_like(output_side)
    mine, other = place.roles(none, output_side)
    grad_mixture = (
        unspread(backward_product(mine, one[0]) + backward_product(other, one[1]), place.by_z)
        .astype(BF16)
        .reshape(count_of_rows, KEY_VALUE_HEADS, QUERY_HEADS // KEY_VALUE_HEADS, HEAD_SIZE)
    )
    scores = (
        jnp.einsum("qghd,kgd->ghqk", query_rows, key_row_block, preferred_element_type=F32)
        * SCALE
    )
    scores = jnp.where(allowed, scores, MASKED)
    attention_full = jnp.exp(scores - log_total)
    attention = attention_full.astype(BF16)
    value_gradient = jnp.einsum(
        "ghqk,qghd->kgd", attention, grad_mixture, preferred_element_type=F32
    )
    grad_attention = jnp.einsum(
        "qghd,kgd->ghqk", grad_mixture, value_row_block, preferred_element_type=F32
    )
    row_dots = jnp.sum(attention_full * grad_attention, axis=-1, keepdims=True)
    grad_scores = (attention_full * (grad_attention - row_dots)).astype(BF16)
    key_gradient = (
        jnp.einsum("ghqk,qghd->kgd", grad_scores, query_rows, preferred_element_type=F32)
        * SCALE
    )
    far, column, wide = wide
    key_gradient = gate(key_gradient, *waits[1], *far)
    key_value = scatter_rows(
        jnp.concatenate(
            [key_gradient.reshape(-1, KV_WIDTH), value_gradient.reshape(-1, KV_WIDTH)], axis=1
        ).astype(BF16)
    )
    grad_queries = (
        jnp.einsum("ghqk,kgd->qghd", grad_scores, key_row_block, preferred_element_type=F32)
        * SCALE
    )
    key_gradient, value_low = (key_value[:, :KV_WIDTH], key_value[:, KV_WIDTH:].astype(BF16))
    grad_query_key = rotary_embedding_backward(
        jnp.concatenate(
            [
                grad_queries.reshape(count_of_rows, QUERY_HEADS, HEAD_SIZE),
                key_gradient.reshape(count_of_rows, KEY_VALUE_HEADS, HEAD_SIZE),
            ],
            axis=1,
        ),
        cosine_table,
        sine_portion,
    )
    grad_query_key = grad_query_key.reshape(count_of_rows, UNIT).astype(BF16)
    value_side = jnp.concatenate([jnp.zeros((count_of_rows, WIDTH), BF16), value_low], axis=1)
    mine, other = place.roles(grad_query_key, value_side)
    grad_normed = unspread(
        backward_product(mine, one[0]) + backward_product(other, one[1]), place.by_z
    )
    unit_one = inputs * inv_one
    grad_gain_one = jnp.sum(grad_normed * unit_one, axis=0)
    grad_in = grad_mid + norm_backward(grad_normed, unit_one, inv_one, gain_one)
    gain_rows = jnp.stack([grad_gain_one.reshape(8, PART), grad_gain_two.reshape(8, PART)], axis=1)
    gain_rows = jnp.pad(gain_rows.reshape(16, PART).astype(BF16), ((0, 0), (0, UNIT - PART)))
    number = jnp.arange(16, dtype=jnp.int32)[:, None]
    inner = (jnp.arange(SPREAD, dtype=jnp.int32) % PADDED)[None]
    gain_place = (number // 2 == place.z_shard[None]) & (PART + number % 2 == inner)
    left_rows = with_sibling(
        jnp.concatenate([place.role(normed_one, mixture), normed_one], axis=1),
        jnp.concatenate([place.role(mixture, normed_one), normed_one], axis=1),
    )
    right_rows = with_sibling(
        jnp.concatenate([place.role(grad_query_key, output_side), place.role(none, value_side)], 1),
        jnp.concatenate([place.role(output_side, grad_query_key), place.role(value_side, none)], 1),
    )
    left_rows = gate(left_rows, *waits[2])
    left_rows = jnp.concatenate(
        [left_rows[:, :SPREAD], left_rows[:, SPREAD:], gain_place.astype(BF16)], axis=0
    )
    right_rows = jnp.concatenate([right_rows[:, :UNIT], right_rows[:, UNIT:], gain_rows], axis=0)
    return (
        gate(grad_in, column),
        (reduce_first(left_rows, right_rows), down, wide),
    )


def per_device(
    boundary,
    lengths,
    query_weight,
    key_matrix,
    value_matrix,
    output_weight,
    gate_weight,
    up_weight,
    down_weight,
    first_gain,
    second_gain,
):
    place = Place()
    first = place.first
    slab = boundary[0, :, 0]
    rows_dev = slab.shape[1]
    exchanged = sibling(jnp.where(first, slab[1], slab[0]))
    inputs = jnp.where(first, slab[0], exchanged).astype(F32)
    cotangent = jnp.where(first, exchanged, slab[1]).astype(F32)

    gains = jnp.pad(
        jnp.concatenate([first_gain, second_gain], axis=0), ((0, 6), (0, UNIT - PART))
    )
    role_packs = (
        (
            jnp.concatenate(
                [jnp.concatenate([query_weight[0], key_matrix[0]], axis=1), gains], axis=0
            ),
            jnp.pad(gate_weight[0], ((0, PADDED - PART), (0, 0))),
            down_weight[0, :, :DOWN_COLS],
        ),
        (
            jnp.concatenate(
                [jnp.concatenate([output_weight[0], value_matrix[0]], axis=1), gains], axis=0
            ),
            jnp.pad(up_weight[0], ((0, PADDED - PART), (0, 0))),
            down_weight[0, :, WIDTH - DOWN_COLS :],
        ),
    )
    layer_packs = ([], [])
    for zero, one in zip(*role_packs):
        kept = jnp.where(first, zero, one)
        other = sibling(jnp.where(first, one, zero))
        layer_packs[0].append(jnp.where(first, kept, other))
        layer_packs[1].append(jnp.where(first, other, kept))
    first_pack, wide_pack, down_pack = layer_packs[0]
    column = gather_column(place, wide_pack)
    low = lax.all_gather(gate(down_pack, column), "fsdp", axis=0, tiled=True)
    weights_first = layer_weights(place, first_pack, column, low)
    first_pack, wide_pack, down_pack = layer_packs[1]
    column = gather_column(place, gate(wide_pack, low))

    seq_lengths = jnp.where(first, lengths[0, 0], lengths[0, 1])
    inner = jnp.arange(rows_dev, dtype=jnp.int32)
    own_rows = place.shard * rows_dev + inner
    all_rows = (place.near_shards[:, None] * rows_dev + inner[None]).reshape(-1)
    segment_mine, position_mine = segment_rows(seq_lengths, own_rows)
    segment_all, unused_position = segment_rows(seq_lengths, all_rows)
    allowed = (segment_mine[:, None] == segment_all[None, :]) & (
        own_rows[:, None] >= all_rows[None, :]
    )
    cosine_table, sine_portion = rotary_tables(position_mine)
    live_rows = (segment_mine < seq_lengths.shape[0]).astype(F32)

    geometry = (cosine_table, sine_portion, allowed)
    middle, stored_first = forward_layer(place, inputs, weights_first, *geometry)
    low = lax.all_gather(gate(down_pack, column), "fsdp", axis=0, tiled=True)
    first_pack = gate(first_pack, stored_first[4])
    weights_second = layer_weights(place, first_pack, column, low)
    middle = middle.astype(BF16).astype(F32)
    result, stored_second = forward_layer(place, middle, weights_second, *geometry)
    grad, pending = backward_layer(
        place, cotangent * live_rows[:, None], weights_second, stored_second, ((), (), ()), *geometry
    )
    pair, down, wide = pending
    early_second = finish_wide(place, down, wide)
    late_second = finish_first(pair, early_second)
    waits = ((pair, wide), (), (early_second, late_second))
    grad = grad.astype(BF16).astype(F32)
    grad, remaining = backward_layer(
        place, grad, weights_first, stored_first, waits, *geometry
    )

    ends = (grad.astype(BF16), result.astype(BF16))
    received = sibling(jnp.where(first, ends[1], ends[0]))
    boundary_out = jnp.where(
        first, jnp.stack([ends[0], received]), jnp.stack([received, ends[1]])
    )[None, :, None]

    pair, down, wide = remaining
    early_first = finish_wide(place, down, wide)
    late_first = finish_first(pair, early_first)
    sums = []
    for for_first, for_second in ((early_first, early_second), (late_first, late_second)):
        own = jnp.where(first, for_first, for_second)
        other = sibling(jnp.where(first, for_second, for_first))
        sums.append([value.astype(F32) for value in place.roles(own, other)])
    down_left, down_right = [value[:, :UNIT].reshape(FF_PART, DOWN_COLS) for value in sums[0]]
    gate_sum, up_sum = [value[:, UNIT:] for value in sums[0]]
    query_key, output_value = sums[1]
    gain_sums = query_key[PART : PART + 2, :PART] + output_value[PART : PART + 2, :PART]
    return (
        boundary_out,
        query_key[None, :PART, :WIDTH],
        query_key[None, :PART, WIDTH:],
        output_value[None, :PART, WIDTH:],
        output_value[None, :PART, :WIDTH],
        gate_sum[None, :PART],
        up_sum[None, :PART],
        jnp.concatenate([down_left, down_right[:, DOWN_SKIP:]], axis=1)[None],
        gain_sums[:1],
        gain_sums[1:],
    )


def solution(mesh):
    placed = (
        P("section", None, "dp", "fsdp", None),
        P("dp", None, None),
        P("section", "fsdp", None),
        P("section", "fsdp", None),
        P("section", "fsdp", None),
        P("section", "fsdp", None),
        P("section", "fsdp", None),
        P("section", "fsdp", None),
        P("section", "fsdp", None),
        P("section", "fsdp"),
        P("section", "fsdp"),
    )
    return jax.shard_map(
        per_device,
        mesh=mesh,
        in_specs=placed,
        out_specs=(
            P("section", None, "dp", "fsdp", None),
            P("section", "fsdp", None),
            P("section", "fsdp", None),
            P("section", "fsdp", None),
            P("section", "fsdp", None),
            P("section", "fsdp", None),
            P("section", "fsdp", None),
            P("section", "fsdp", None),
            P("section", "fsdp"),
            P("section", "fsdp"),
        ),
        check_vma=False,
    )
```

```python
import jax
import jax.numpy as jnp
from jax import lax
from jax.sharding import PartitionSpec as P

QUERY_HEADS = 15
KEY_VALUE_HEADS = 5
HEAD_SIZE = 64


EPS = 1e-05
SCALE = 0.125
MASKED = -1e30


BF16 = jnp.bfloat16
F32 = jnp.float32
WIDTH = 960
PART = 120
PADDED = 128
SPREAD = 1024
UNIT = 1280
FF_PART = 320
FF_QUARTER = 80
DOWN_COLS = 512
DOWN_SKIP = 64
ROW_QUARTER = 32
KV_WIDTH = KEY_VALUE_HEADS * HEAD_SIZE
DISTANCES = (0, -1, 1, 2)


def segment_rows(seq_lengths, row_index):
    seq_ends = jnp.cumsum(seq_lengths)
    starts = seq_ends - seq_lengths
    segment = jnp.sum((row_index[:, None] >= seq_ends[None, :]).astype(jnp.int32), axis=1)
    slot_ids = jnp.arange(seq_lengths.shape[0], dtype=jnp.int32)
    row_start = jnp.sum(
        jnp.where(segment[:, None] == slot_ids[None, :], starts[None, :], 0), axis=1
    )
    return (segment, row_index - row_start)


def rotary_tables(position):
    frequency = 10000.0 ** (-2.0 * jnp.arange(HEAD_SIZE // 2, dtype=jnp.float32) / HEAD_SIZE)
    angles = position.astype(jnp.float32)[:, None] * frequency[None, :]
    return (jnp.cos(angles)[:, None, :], jnp.sin(angles)[:, None, :])


def rotary_embedding(vector, cosine_table, sine_portion):
    first_half = vector[..., : HEAD_SIZE // 2]
    second_half = vector[..., HEAD_SIZE // 2 :]
    return jnp.concatenate(
        [
            first_half * cosine_table - second_half * sine_portion,
            second_half * cosine_table + first_half * sine_portion,
        ],
        axis=-1,
    )


def rotary_embedding_backward(grad, cosine_table, sine_portion):
    first_half = grad[..., : HEAD_SIZE // 2]
    second_half = grad[..., HEAD_SIZE // 2 :]
    return jnp.concatenate(
        [
            first_half * cosine_table + second_half * sine_portion,
            second_half * cosine_table - first_half * sine_portion,
        ],
        axis=-1,
    )


def rms_scale(values):
    return lax.rsqrt(jnp.mean(values * values, axis=-1, keepdims=True) + EPS)


def outer_sum(left, right):
    return lax.dot_general(
        left, right, (((0,), (0,)), ((), ())), preferred_element_type=jnp.float32
    )


def backward_product(grad, weight):
    return lax.dot_general(
        grad, weight, (((1,), (1,)), ((), ())), preferred_element_type=jnp.float32
    )


def z_step(value, step):
    return lax.ppermute(value, "fsdp", [(i, (i + 2 * step) % 8) for i in range(8)])


def x_step(value, step):
    return lax.ppermute(value, "dp", [(i, (i + 2 * step) % 8) for i in range(8)])


def y_near(value):
    return lax.ppermute(value, "fsdp", [(i, i ^ 1) for i in range(8)])


def y_far(value):
    return lax.ppermute(value, "dp", [(i, i ^ 1) for i in range(8)])


def sibling(value):
    return lax.ppermute(value, "section", [(0, 1), (1, 0)])


def ring_gather(step, way, block):
    before = step(block, 1)
    after = step(block, -1)
    far = step(before if way == 1 else after, way)
    return [block, before, after, far]


def ring_sum(step, way, chunk):
    relayed = step(chunk(2).astype(BF16), way)
    other = step(chunk(-way).astype(BF16), -way)
    nearer = (chunk(way).astype(F32) + relayed.astype(F32)).astype(BF16)
    return chunk(0).astype(F32) + other.astype(F32) + step(nearer, way).astype(F32)


def direct_sum(step, chunk):
    total = chunk(0).astype(F32)
    for distance in (1, -1, 2):
        total = total + step(chunk(distance).astype(BF16), distance).astype(F32)
    return total


class Place:
    def __init__(self):
        self.section = lax.axis_index("section")
        self.shard = lax.axis_index("fsdp")
        dp = lax.axis_index("dp")
        self.z, self.y = self.shard // 2, self.shard % 2
        self.x = dp // 2
        self.first = self.section == 0
        self.near_shards = jnp.stack(
            [(self.z + d) % 4 * 2 + (self.y + near) % 2 for d in DISTANCES for near in (0, 1)]
        )
        row = lax.broadcasted_iota(jnp.int32, (WIDTH, SPREAD), 0)
        column = jnp.arange(SPREAD, dtype=jnp.int32)
        self.z_shard = jnp.repeat(self.near_shards, PADDED)
        self.by_z = (
            (row // PART == self.z_shard[None]) & (row % PART == (column % PADDED)[None])
        ).astype(BF16)
        quarters = jnp.repeat(jnp.stack([(self.x + d) % 4 for d in DISTANCES]), SPREAD // 4)
        shards = jnp.tile(jnp.repeat(self.near_shards, ROW_QUARTER), 4)
        inner = quarters * ROW_QUARTER + column % ROW_QUARTER
        self.by_x = ((row // PART == shards[None]) & (row % PART == inner[None])).astype(BF16)

    def role(self, zero, one):
        return jnp.where(self.first, zero, one)

    def roles(self, mine, other):
        return (jnp.where(self.first, mine, other), jnp.where(self.first, other, mine))


def spread(value, places):
    return jnp.dot(value, places, preferred_element_type=F32).astype(BF16)


def unspread(value, places):
    high = lax.reduce_precision(value, 8, 7)
    both = jnp.concatenate([high.astype(BF16), (value - high).astype(BF16)], axis=1)
    return backward_product(both, jnp.concatenate([places, places], axis=1))


def product(left, right):
    return jnp.dot(left, right, preferred_element_type=F32)


def gate(value, *others):
    late = False
    for other in others:
        corner = other[(0,) * other.ndim]
        late = late | (corner != corner)
    return jax.tree.map(lambda part: jnp.where(late, jnp.zeros_like(part), part), value)


def ring_gather_both(step, block):
    before = step(block, 1)
    after = step(block, -1)
    far = (step(before[0], 1), step(after[1], -1))
    layers = [[block[n], before[n], after[n], far[n]] for n in range(2)]
    return (layers, (before, after))


def gather_first(place, own):
    pair = jnp.stack([own, y_near(own)], axis=1).reshape(2, 2 * PADDED, UNIT)
    layers, near = ring_gather_both(z_step, pair)
    return ([jnp.concatenate(blocks, axis=0) for blocks in layers], near)


def gather_down(place, own, waits):
    other = y_near(own)
    low, high = (jnp.where(place.y == 0, own, other), jnp.where(place.y == 0, other, own))
    pair = jnp.stack([low, high], axis=1).reshape(2, 2 * FF_PART, DOWN_COLS)
    pair = gate(pair, *waits)
    layers, near = ring_gather_both(z_step, pair)
    wholes = []
    for blocks in layers:
        whole = jnp.zeros((4,) + pair.shape[1:], BF16)
        for distance, block in zip(DISTANCES, blocks):
            whole = lax.dynamic_update_slice_in_dim(
                whole, block[None], (place.z + distance) % 4, 0
            )
        wholes.append(whole.reshape(-1, DOWN_COLS))
    return (wholes, near)


def gather_wide(place, own):
    quarter = lax.dynamic_slice_in_dim(own, place.x * ROW_QUARTER, ROW_QUARTER, 1)
    pair = jnp.stack([quarter, y_near(quarter)], axis=1)
    column = jnp.stack(ring_gather(z_step, -1, pair), axis=1)
    column = column.reshape(2, SPREAD // 4, 2 * UNIT)
    layers, near = ring_gather_both(x_step, column)
    return ([jnp.concatenate(blocks, axis=0) for blocks in layers], near)


def layer_weights(place, mine):
    one, two, low = [(value, sibling(value)) for value in mine]
    gains = one[0].reshape(8, PADDED, UNIT)[:, PART : PART + 2, :PADDED]
    gains = backward_product(gains.transpose(1, 0, 2).reshape(2, SPREAD), place.by_z)
    return (one, two, low, gains[:1], gains[1:])


def gather_rows(own):
    pair = jnp.concatenate([own, y_near(own)], axis=0)
    return jnp.concatenate(ring_gather(z_step, 1, pair), axis=0)


def scatter_rows(partial):
    parts = partial.reshape(4, -1, partial.shape[1])
    pair = ring_sum(z_step, -1, lambda distance: parts[DISTANCES.index(distance)])
    rows = pair.shape[0] // 2
    return pair[:rows] + y_near(pair[rows:].astype(BF16)).astype(F32)


def forward_layer(place, inputs, weights, waits, cosine_table, sine_portion, allowed):
    one, two, low, gain_one, gain_two = weights
    count_of_rows = inputs.shape[0]
    inv_one = rms_scale(inputs)
    normed_one = spread((inputs * inv_one * gain_one).astype(BF16), place.by_z)
    query_key, value_part = place.roles(product(normed_one, one[0]), product(normed_one, one[1]))
    value_part = value_part[:, WIDTH:].astype(BF16)
    turned = rotary_embedding(
        query_key.reshape(count_of_rows, QUERY_HEADS + KEY_VALUE_HEADS, HEAD_SIZE),
        cosine_table,
        sine_portion,
    ).astype(BF16)
    query_rows = turned[:, :QUERY_HEADS].reshape(
        count_of_rows, KEY_VALUE_HEADS, QUERY_HEADS // KEY_VALUE_HEADS, HEAD_SIZE
    )
    key_portion = turned[:, QUERY_HEADS:].reshape(count_of_rows, KV_WIDTH)
    key_value = gather_rows(jnp.concatenate([key_portion, value_part], axis=1))
    key_value = gate(key_value, *waits[0])
    key_row_block = key_value[:, :KV_WIDTH].reshape(-1, KEY_VALUE_HEADS, HEAD_SIZE)
    value_row_block = key_value[:, KV_WIDTH:].reshape(-1, KEY_VALUE_HEADS, HEAD_SIZE)
    scores = (
        jnp.einsum("qghd,kgd->ghqk", query_rows, key_row_block, preferred_element_type=F32)
        * SCALE
    )
    scores = jnp.where(allowed, scores, MASKED)
    row_max = jnp.max(scores, axis=-1, keepdims=True)
    exponent = jnp.exp(scores - row_max)
    total = jnp.sum(exponent, axis=-1, keepdims=True)
    attention = (exponent / total).astype(BF16)
    log_total = row_max + jnp.log(total)
    mixture = jnp.einsum(
        "ghqk,kgd->qghd", attention, value_row_block, preferred_element_type=F32
    )
    mixture = gate(mixture, *waits[1])
    mixture = spread(
        mixture.astype(BF16).reshape(count_of_rows, QUERY_HEADS * HEAD_SIZE), place.by_z
    )
    unused, projected = place.roles(product(mixture, one[0]), product(mixture, one[1]))
    middle = inputs + projected[:, :WIDTH]
    inv_two = rms_scale(middle)
    normed_two = spread((middle * inv_two * gain_two).astype(BF16), place.by_x)
    gate_pre, up_pre = place.roles(product(normed_two, two[0]), product(normed_two, two[1]))
    hidden = (jax.nn.silu(gate_pre) * up_pre).astype(BF16)
    left, right = place.roles(product(hidden, low[0]), product(hidden, low[1]))
    result = middle + jnp.concatenate([left, right[:, DOWN_SKIP:]], axis=1)
    stored = (
        inputs,
        inv_one,
        normed_one,
        query_rows,
        key_row_block,
        value_row_block,
        log_total,
        mixture,
        middle,
        inv_two,
        normed_two,
        gate_pre,
        up_pre,
        hidden,
    )
    return (result, stored)


def with_sibling(own, sent):
    return jnp.concatenate([own, sibling(sent)], axis=0)


def norm_backward(grad, unit, inverse, gain):
    scaled = grad * gain
    return inverse * (scaled - unit * jnp.mean(scaled * unit, axis=-1, keepdims=True))


def partial_chunks(left, right):
    size = left.shape[1] // 4

    def chunk(distance):
        at = DISTANCES.index(distance)
        return outer_sum(left[:, at * size : (at + 1) * size], right).astype(BF16)

    return chunk


def by_quarter(place, block, rows):
    quarters = block.reshape(4, rows, block.shape[-1])

    def quarter(distance):
        return lax.dynamic_index_in_dim(quarters, (place.x + distance) % 4, 0, keepdims=False)

    return quarter


def reduce_first(left, right):
    return ring_sum(z_step, 1, partial_chunks(left, right))


def reduce_down(place, left, right):
    size = 2 * FF_PART

    def chunk(distance):
        part = lax.dynamic_slice_in_dim(left, (place.z + distance) % 4 * size, size, 1)
        return outer_sum(part, right).astype(BF16)

    pair = ring_sum(z_step, -1, chunk).astype(BF16)
    pair = pair.reshape(2, PADDED, UNIT)
    return jnp.concatenate(
        [
            lax.dynamic_index_in_dim(pair, place.y, 0, keepdims=False),
            lax.dynamic_index_in_dim(pair, 1 - place.y, 0, keepdims=False),
        ],
        axis=0,
    ).astype(F32)


def reduce_wide(left, right):
    chunk = partial_chunks(left, right)
    half = SPREAD // 8
    from_before = x_step(outer_sum(left[:, -2 * half : -half], right).astype(BF16), 1)
    from_after = x_step(outer_sum(left[:, -half:], right).astype(BF16), -1)
    after = chunk(1).astype(F32) + jnp.pad(from_before, ((0, half), (0, 0))).astype(F32)
    before = chunk(-1).astype(F32) + jnp.pad(from_after, ((half, 0), (0, 0))).astype(F32)
    column = (
        chunk(0).astype(F32)
        + x_step(after.astype(BF16), 1).astype(F32)
        + x_step(before.astype(BF16), -1).astype(F32)
    )
    parts = column.reshape(4, 2 * ROW_QUARTER, 2 * UNIT)
    pair = ring_sum(z_step, 1, lambda distance: parts[DISTANCES.index(distance)])
    quarter = pair[:ROW_QUARTER] + y_near(pair[ROW_QUARTER:].astype(BF16)).astype(F32)
    return ((from_before, from_after), column, quarter)


def across_y(pair):
    return pair[:PADDED] + y_near(pair[PADDED:].astype(BF16)).astype(F32)


def across_x(place, block):
    return direct_sum(x_step, by_quarter(place, block, ROW_QUARTER))


def finish(place, quarter):
    low = quarter.astype(BF16)
    piece = (low.astype(F32) + y_far(low).astype(F32)).astype(BF16)
    whole = jnp.zeros((4,) + piece.shape, BF16)
    for distance in DISTANCES:
        block = step_from(piece, distance)
        whole = lax.dynamic_update_slice_in_dim(
            whole, block[None], (place.x + distance) % 4, 0
        )
    return whole.reshape(-1, piece.shape[-1])


def step_from(piece, distance):
    return piece if distance == 0 else x_step(piece, -distance)


def backward_layer(
    place, grad_out, weights, stored, waits, cosine_table, sine_portion, allowed
):
    one, two, low, gain_one, gain_two = weights
    (
        inputs,
        inv_one,
        normed_one,
        query_rows,
        key_row_block,
        value_row_block,
        log_total,
        mixture,
        middle,
        inv_two,
        normed_two,
        gate_pre,
        up_pre,
        hidden,
    ) = stored
    count_of_rows = grad_out.shape[0]
    grad_low = grad_out.astype(BF16)
    left_low = grad_low[:, :DOWN_COLS]
    right_low = grad_low[:, WIDTH - DOWN_COLS :]
    right_once = jnp.where(jnp.arange(DOWN_COLS)[None] < DOWN_SKIP, 0, right_low)
    mine_low, other_low = place.roles(left_low, right_once)
    hidden_grad = backward_product(mine_low, low[0]) + backward_product(other_low, low[1])
    sigmoid_gate = jax.nn.sigmoid(gate_pre)
    grad_gate = (
        hidden_grad * up_pre * sigmoid_gate * (1.0 + gate_pre * (1.0 - sigmoid_gate))
    ).astype(BF16)
    grad_up = (hidden_grad * gate_pre * sigmoid_gate).astype(BF16)
    mine, other = place.roles(grad_gate, grad_up)
    spread_two = backward_product(mine, two[0]) + backward_product(other, two[1])
    left_rows = with_sibling(*2 * (jnp.concatenate([hidden, normed_two], axis=1),))
    right_rows = with_sibling(
        jnp.concatenate([place.role(left_low, right_low), mine], axis=1),
        jnp.concatenate([place.role(right_low, left_low), other], axis=1),
    )
    down = reduce_down(place, left_rows[:, : 2 * UNIT], right_rows[:, :DOWN_COLS])
    wide = reduce_wide(left_rows[:, 2 * UNIT :], right_rows[:, DOWN_COLS:])
    grad_normed_two = unspread(spread_two, place.by_x)
    unit_two = middle * inv_two
    grad_gain_two = jnp.sum(grad_normed_two * unit_two, axis=0)
    grad_normed_two = gate(grad_normed_two, *waits[0])
    grad_mid = grad_out + norm_backward(grad_normed_two, unit_two, inv_two, gain_two)
    none_narrow = jnp.zeros((count_of_rows, KV_WIDTH), BF16)
    output_side = jnp.concatenate([grad_mid.astype(BF16), none_narrow], axis=1)
    none = jnp.zeros_like(output_side)
    mine, other = place.roles(none, output_side)
    grad_mixture = (
        unspread(backward_product(mine, one[0]) + backward_product(other, one[1]), place.by_z)
        .astype(BF16)
        .reshape(count_of_rows, KEY_VALUE_HEADS, QUERY_HEADS // KEY_VALUE_HEADS, HEAD_SIZE)
    )
    scores = (
        jnp.einsum("qghd,kgd->ghqk", query_rows, key_row_block, preferred_element_type=F32)
        * SCALE
    )
    scores = jnp.where(allowed, scores, MASKED)
    attention_full = jnp.exp(scores - log_total)
    attention = attention_full.astype(BF16)
    value_gradient = jnp.einsum(
        "ghqk,qghd->kgd", attention, grad_mixture, preferred_element_type=F32
    )
    grad_attention = jnp.einsum(
        "qghd,kgd->ghqk", grad_mixture, value_row_block, preferred_element_type=F32
    )
    row_dots = jnp.sum(attention_full * grad_attention, axis=-1, keepdims=True)
    grad_scores = (attention_full * (grad_attention - row_dots)).astype(BF16)
    key_gradient = (
        jnp.einsum("ghqk,qghd->kgd", grad_scores, query_rows, preferred_element_type=F32)
        * SCALE
    )
    far, column, wide = wide
    key_gradient = gate(key_gradient, *waits[1], *far)
    key_value = scatter_rows(
        jnp.concatenate(
            [key_gradient.reshape(-1, KV_WIDTH), value_gradient.reshape(-1, KV_WIDTH)], axis=1
        ).astype(BF16)
    )
    grad_queries = (
        jnp.einsum("ghqk,kgd->qghd", grad_scores, key_row_block, preferred_element_type=F32)
        * SCALE
    )
    key_gradient, value_low = (key_value[:, :KV_WIDTH], key_value[:, KV_WIDTH:].astype(BF16))
    grad_query_key = rotary_embedding_backward(
        jnp.concatenate(
            [
                grad_queries.reshape(count_of_rows, QUERY_HEADS, HEAD_SIZE),
                key_gradient.reshape(count_of_rows, KEY_VALUE_HEADS, HEAD_SIZE),
            ],
            axis=1,
        ),
        cosine_table,
        sine_portion,
    )
    grad_query_key = grad_query_key.reshape(count_of_rows, UNIT).astype(BF16)
    value_side = jnp.concatenate([jnp.zeros((count_of_rows, WIDTH), BF16), value_low], axis=1)
    mine, other = place.roles(grad_query_key, value_side)
    grad_normed = unspread(
        backward_product(mine, one[0]) + backward_product(other, one[1]), place.by_z
    )
    unit_one = inputs * inv_one
    grad_gain_one = jnp.sum(grad_normed * unit_one, axis=0)
    grad_in = grad_mid + norm_backward(grad_normed, unit_one, inv_one, gain_one)
    gain_rows = jnp.stack([grad_gain_one.reshape(8, PART), grad_gain_two.reshape(8, PART)], axis=1)
    gain_rows = jnp.pad(gain_rows.reshape(16, PART).astype(BF16), ((0, 0), (0, UNIT - PART)))
    number = jnp.arange(16, dtype=jnp.int32)[:, None]
    inner = (jnp.arange(SPREAD, dtype=jnp.int32) % PADDED)[None]
    gain_place = (number // 2 == place.z_shard[None]) & (PART + number % 2 == inner)
    left_rows = with_sibling(
        jnp.concatenate([place.role(normed_one, mixture), normed_one], axis=1),
        jnp.concatenate([place.role(mixture, normed_one), normed_one], axis=1),
    )
    right_rows = with_sibling(
        jnp.concatenate([place.role(grad_query_key, output_side), place.role(none, value_side)], 1),
        jnp.concatenate([place.role(output_side, grad_query_key), place.role(value_side, none)], 1),
    )
    left_rows = gate(left_rows, column, down, *waits[2])
    left_rows = jnp.concatenate(
        [left_rows[:, :SPREAD], left_rows[:, SPREAD:], gain_place.astype(BF16)], axis=0
    )
    right_rows = jnp.concatenate([right_rows[:, :UNIT], right_rows[:, UNIT:], gain_rows], axis=0)
    return (
        gate(grad_in, down, column),
        (reduce_first(left_rows, right_rows), down, wide),
    )


def per_device(
    boundary,
    lengths,
    query_weight,
    key_matrix,
    value_matrix,
    output_weight,
    gate_weight,
    up_weight,
    down_weight,
    first_gain,
    second_gain,
):
    place = Place()
    first = place.first
    slab = boundary[0, :, 0]
    rows_dev = slab.shape[1]
    exchanged = sibling(jnp.where(first, slab[1], slab[0]))
    inputs = jnp.where(first, slab[0], exchanged).astype(F32)
    cotangent = jnp.where(first, exchanged, slab[1]).astype(F32)

    gains = jnp.pad(
        jnp.concatenate([first_gain, second_gain], axis=0), ((0, 6), (0, UNIT - PART))
    )
    role_packs = (
        (
            jnp.concatenate(
                [jnp.concatenate([query_weight[0], key_matrix[0]], axis=1), gains], axis=0
            ),
            jnp.pad(gate_weight[0], ((0, PADDED - PART), (0, 0))),
            down_weight[0, :, :DOWN_COLS],
        ),
        (
            jnp.concatenate(
                [jnp.concatenate([output_weight[0], value_matrix[0]], axis=1), gains], axis=0
            ),
            jnp.pad(up_weight[0], ((0, PADDED - PART), (0, 0))),
            down_weight[0, :, WIDTH - DOWN_COLS :],
        ),
    )
    layer_packs = ([], [])
    for zero, one in zip(*role_packs):
        kept = jnp.where(first, zero, one)
        other = sibling(jnp.where(first, one, zero))
        layer_packs[0].append(jnp.where(first, kept, other))
        layer_packs[1].append(jnp.where(first, other, kept))
    first_pack, wide_pack, down_pack = [jnp.stack(both) for both in zip(*layer_packs)]
    wide, near_wide = gather_wide(place, wide_pack)
    one, near_one = gather_first(place, first_pack)
    down, near_down = gather_down(place, down_pack, near_one)
    weights_first, weights_second = [
        layer_weights(place, mine) for mine in zip(one, wide, down)
    ]

    seq_lengths = jnp.where(first, lengths[0, 0], lengths[0, 1])
    inner = jnp.arange(rows_dev, dtype=jnp.int32)
    own_rows = place.shard * rows_dev + inner
    all_rows = (place.near_shards[:, None] * rows_dev + inner[None]).reshape(-1)
    segment_mine, position_mine = segment_rows(seq_lengths, own_rows)
    segment_all, unused_position = segment_rows(seq_lengths, all_rows)
    allowed = (segment_mine[:, None] == segment_all[None, :]) & (
        own_rows[:, None] >= all_rows[None, :]
    )
    cosine_table, sine_portion = rotary_tables(position_mine)
    live_rows = (segment_mine < seq_lengths.shape[0]).astype(F32)

    geometry = (cosine_table, sine_portion, allowed)
    middle, stored_first = forward_layer(
        place, inputs, weights_first, (near_wide, near_down), *geometry
    )
    middle = middle.astype(BF16).astype(F32)
    result, stored_second = forward_layer(place, middle, weights_second, ((), ()), *geometry)
    grad, pending = backward_layer(
        place, cotangent * live_rows[:, None], weights_second, stored_second, ((), (), ()), *geometry
    )
    pair, down, wide = pending
    before = jnp.concatenate([pair, down], axis=1)
    waits = ((), (pair, wide), ())
    grad = grad.astype(BF16).astype(F32)
    grad, remaining = backward_layer(
        place, grad, weights_first, stored_first, waits, *geometry
    )

    ends = (grad.astype(BF16), result.astype(BF16))
    received = sibling(jnp.where(first, ends[1], ends[0]))
    boundary_out = jnp.where(
        first, jnp.stack([ends[0], received]), jnp.stack([received, ends[1]])
    )[None, :, None]

    pair, down, wide_first = remaining
    early = across_x(place, across_y(jnp.concatenate([before, down], axis=1)))
    early = finish(place, jnp.concatenate([early, wide, wide_first], axis=1))
    late_first = finish(place, across_x(place, across_y(pair)))
    late_second = early[:, :UNIT]
    early_second = jnp.concatenate([early[:, UNIT : 2 * UNIT], early[:, 3 * UNIT : 5 * UNIT]], 1)
    early_first = jnp.concatenate([early[:, 2 * UNIT : 3 * UNIT], early[:, 5 * UNIT :]], 1)
    sums = []
    for for_first, for_second in ((early_first, early_second), (late_first, late_second)):
        own = jnp.where(first, for_first, for_second)
        other = sibling(jnp.where(first, for_second, for_first))
        sums.append([value.astype(F32) for value in place.roles(own, other)])
    down_left, down_right = [value[:, :UNIT].reshape(FF_PART, DOWN_COLS) for value in sums[0]]
    gate_sum, up_sum = [value[:, UNIT:] for value in sums[0]]
    query_key, output_value = sums[1]
    gain_sums = query_key[PART : PART + 2, :PART] + output_value[PART : PART + 2, :PART]
    return (
        boundary_out,
        query_key[None, :PART, :WIDTH],
        query_key[None, :PART, WIDTH:],
        output_value[None, :PART, WIDTH:],
        output_value[None, :PART, :WIDTH],
        gate_sum[None, :PART],
        up_sum[None, :PART],
        jnp.concatenate([down_left, down_right[:, DOWN_SKIP:]], axis=1)[None],
        gain_sums[:1],
        gain_sums[1:],
    )


def solution(mesh):
    placed = (
        P("section", None, "dp", "fsdp", None),
        P("dp", None, None),
        P("section", "fsdp", None),
        P("section", "fsdp", None),
        P("section", "fsdp", None),
        P("section", "fsdp", None),
        P("section", "fsdp", None),
        P("section", "fsdp", None),
        P("section", "fsdp", None),
        P("section", "fsdp"),
        P("section", "fsdp"),
    )
    return jax.shard_map(
        per_device,
        mesh=mesh,
        in_specs=placed,
        out_specs=(
            P("section", None, "dp", "fsdp", None),
            P("section", "fsdp", None),
            P("section", "fsdp", None),
            P("section", "fsdp", None),
            P("section", "fsdp", None),
            P("section", "fsdp", None),
            P("section", "fsdp", None),
            P("section", "fsdp", None),
            P("section", "fsdp"),
            P("section", "fsdp"),
        ),
        check_vma=False,
    )
```

```python
import jax
import jax.numpy as jnp
from jax import lax
from jax.sharding import PartitionSpec as P

QUERY_HEADS = 15
KEY_VALUE_HEADS = 5
HEAD_SIZE = 64


EPS = 1e-05
SCALE = 0.125
MASKED = -1e30


BF16 = jnp.bfloat16
F32 = jnp.float32
WIDTH = 960
PART = 120
PADDED = 128
SPREAD = 1024
UNIT = 1280
FF_PART = 320
FF_QUARTER = 80
DOWN_COLS = 512
DOWN_SKIP = 64
ROW_QUARTER = 32
KV_WIDTH = KEY_VALUE_HEADS * HEAD_SIZE
DISTANCES = (0, -1, 1, 2)


def segment_rows(seq_lengths, row_index):
    seq_ends = jnp.cumsum(seq_lengths)
    starts = seq_ends - seq_lengths
    segment = jnp.sum((row_index[:, None] >= seq_ends[None, :]).astype(jnp.int32), axis=1)
    slot_ids = jnp.arange(seq_lengths.shape[0], dtype=jnp.int32)
    row_start = jnp.sum(
        jnp.where(segment[:, None] == slot_ids[None, :], starts[None, :], 0), axis=1
    )
    return (segment, row_index - row_start)


def rotary_tables(position):
    frequency = 10000.0 ** (-2.0 * jnp.arange(HEAD_SIZE // 2, dtype=jnp.float32) / HEAD_SIZE)
    angles = position.astype(jnp.float32)[:, None] * frequency[None, :]
    return (jnp.cos(angles)[:, None, :], jnp.sin(angles)[:, None, :])


def rotary_embedding(vector, cosine_table, sine_portion):
    first_half = vector[..., : HEAD_SIZE // 2]
    second_half = vector[..., HEAD_SIZE // 2 :]
    return jnp.concatenate(
        [
            first_half * cosine_table - second_half * sine_portion,
            second_half * cosine_table + first_half * sine_portion,
        ],
        axis=-1,
    )


def rotary_embedding_backward(grad, cosine_table, sine_portion):
    first_half = grad[..., : HEAD_SIZE // 2]
    second_half = grad[..., HEAD_SIZE // 2 :]
    return jnp.concatenate(
        [
            first_half * cosine_table + second_half * sine_portion,
            second_half * cosine_table - first_half * sine_portion,
        ],
        axis=-1,
    )


def rms_scale(values):
    return lax.rsqrt(jnp.mean(values * values, axis=-1, keepdims=True) + EPS)


def outer_sum(left, right):
    return lax.dot_general(
        left, right, (((0,), (0,)), ((), ())), preferred_element_type=jnp.float32
    )


def backward_product(grad, weight):
    return lax.dot_general(
        grad, weight, (((1,), (1,)), ((), ())), preferred_element_type=jnp.float32
    )


def z_step(value, step):
    return lax.ppermute(value, "fsdp", [(i, (i + 2 * step) % 8) for i in range(8)])


def x_step(value, step):
    return lax.ppermute(value, "dp", [(i, (i + 2 * step) % 8) for i in range(8)])


def y_near(value):
    return lax.ppermute(value, "fsdp", [(i, i ^ 1) for i in range(8)])


def y_far(value):
    return lax.ppermute(value, "dp", [(i, i ^ 1) for i in range(8)])


def sibling(value):
    return lax.ppermute(value, "section", [(0, 1), (1, 0)])


def ring_gather(step, way, block):
    before = step(block, 1)
    after = step(block, -1)
    far = step(before if way == 1 else after, way)
    return [block, before, after, far]


def ring_sum(step, way, chunk):
    relayed = step(chunk(2).astype(BF16), way)
    other = step(chunk(-way).astype(BF16), -way)
    nearer = (chunk(way).astype(F32) + relayed.astype(F32)).astype(BF16)
    return chunk(0).astype(F32) + other.astype(F32) + step(nearer, way).astype(F32)


def direct_sum(step, chunk):
    total = chunk(0).astype(F32)
    for distance in (1, -1, 2):
        total = total + step(chunk(distance).astype(BF16), distance).astype(F32)
    return total


class Place:
    def __init__(self):
        self.section = lax.axis_index("section")
        self.shard = lax.axis_index("fsdp")
        dp = lax.axis_index("dp")
        self.z, self.y = self.shard // 2, self.shard % 2
        self.x = dp // 2
        self.first = self.section == 0
        self.near_shards = jnp.stack(
            [(self.z + d) % 4 * 2 + (self.y + near) % 2 for d in DISTANCES for near in (0, 1)]
        )
        row = lax.broadcasted_iota(jnp.int32, (WIDTH, SPREAD), 0)
        column = jnp.arange(SPREAD, dtype=jnp.int32)
        self.z_shard = jnp.repeat(self.near_shards, PADDED)
        self.by_z = (
            (row // PART == self.z_shard[None]) & (row % PART == (column % PADDED)[None])
        ).astype(BF16)
        quarters = jnp.repeat(jnp.stack([(self.x + d) % 4 for d in DISTANCES]), SPREAD // 4)
        shards = jnp.tile(jnp.repeat(self.near_shards, ROW_QUARTER), 4)
        inner = quarters * ROW_QUARTER + column % ROW_QUARTER
        self.by_x = ((row // PART == shards[None]) & (row % PART == inner[None])).astype(BF16)

    def role(self, zero, one):
        return jnp.where(self.first, zero, one)

    def roles(self, mine, other):
        return (jnp.where(self.first, mine, other), jnp.where(self.first, other, mine))


def spread(value, places):
    return jnp.dot(value, places, preferred_element_type=F32).astype(BF16)


def unspread(value, places):
    high = lax.reduce_precision(value, 8, 7)
    both = jnp.concatenate([high.astype(BF16), (value - high).astype(BF16)], axis=1)
    return backward_product(both, jnp.concatenate([places, places], axis=1))


def product(left, right):
    return jnp.dot(left, right, preferred_element_type=F32)


def gate(value, *others):
    late = False
    for other in others:
        corner = other[(-1,) * other.ndim]
        late = late | (corner != corner)
    return jax.tree.map(lambda part: jnp.where(late, jnp.zeros_like(part), part), value)


def ring_gather_both(step, block):
    before = step(block, 1)
    after = step(block, -1)
    far = (step(before[0], 1), step(after[1], -1))
    layers = [[block[n], before[n], after[n], far[n]] for n in range(2)]
    return (layers, (before, after))


def gather_first(place, own, waits):
    own = gate(own, *waits)
    pair = jnp.stack([own, y_near(own)], axis=1).reshape(2, 2 * PADDED, UNIT)
    layers, near = ring_gather_both(z_step, pair)
    return ([jnp.concatenate(blocks, axis=0) for blocks in layers], near)


def gather_down(place, own, waits):
    other = y_near(own)
    low, high = (jnp.where(place.y == 0, own, other), jnp.where(place.y == 0, other, own))
    pair = jnp.stack([low, high], axis=1).reshape(2, 2 * FF_PART, DOWN_COLS)
    pair = gate(pair, *waits)
    layers, near = ring_gather_both(z_step, pair)
    wholes = []
    for blocks in layers:
        whole = jnp.zeros((4,) + pair.shape[1:], BF16)
        for distance, block in zip(DISTANCES, blocks):
            whole = lax.dynamic_update_slice_in_dim(
                whole, block[None], (place.z + distance) % 4, 0
            )
        wholes.append(whole.reshape(-1, DOWN_COLS))
    return (wholes, near)


def gather_wide(place, own):
    quarter = lax.dynamic_slice_in_dim(own, place.x * ROW_QUARTER, ROW_QUARTER, 1)
    other = y_near(quarter)
    pair = jnp.stack([quarter, other], axis=1)
    column = jnp.stack(ring_gather(z_step, -1, pair), axis=1)
    column = column.reshape(2, SPREAD // 4, 2 * UNIT)
    layers, near = ring_gather_both(x_step, column)
    return ([jnp.concatenate(blocks, axis=0) for blocks in layers], near, (other,))


def layer_weights(place, mine):
    one, two = [(value, sibling(value)) for value in mine]
    gains = one[0].reshape(8, PADDED, UNIT)[:, PART : PART + 2, :PADDED]
    gains = backward_product(gains.transpose(1, 0, 2).reshape(2, SPREAD), place.by_z)
    return (one, two, gains[:1], gains[1:])


def gather_rows(own):
    pair = jnp.concatenate([own, y_near(own)], axis=0)
    return jnp.concatenate(ring_gather(z_step, 1, pair), axis=0)


def scatter_rows(partial):
    parts = partial.reshape(4, -1, partial.shape[1])
    pair = ring_sum(z_step, -1, lambda distance: parts[DISTANCES.index(distance)])
    rows = pair.shape[0] // 2
    return pair[:rows] + y_near(pair[rows:].astype(BF16)).astype(F32)


def forward_layer(place, inputs, weights, fetch, waits, cosine_table, sine_portion, allowed):
    one, two, gain_one, gain_two = weights
    count_of_rows = inputs.shape[0]
    inv_one = rms_scale(inputs)
    normed_one = spread((inputs * inv_one * gain_one).astype(BF16), place.by_z)
    query_key, value_part = place.roles(product(normed_one, one[0]), product(normed_one, one[1]))
    value_part = value_part[:, WIDTH:].astype(BF16)
    turned = rotary_embedding(
        query_key.reshape(count_of_rows, QUERY_HEADS + KEY_VALUE_HEADS, HEAD_SIZE),
        cosine_table,
        sine_portion,
    ).astype(BF16)
    query_rows = turned[:, :QUERY_HEADS].reshape(
        count_of_rows, KEY_VALUE_HEADS, QUERY_HEADS // KEY_VALUE_HEADS, HEAD_SIZE
    )
    key_portion = turned[:, QUERY_HEADS:].reshape(count_of_rows, KV_WIDTH)
    key_value = gather_rows(jnp.concatenate([key_portion, value_part], axis=1))
    downs, near = fetch(key_value)
    low = downs[0]
    key_value = gate(key_value, *waits)
    key_row_block = key_value[:, :KV_WIDTH].reshape(-1, KEY_VALUE_HEADS, HEAD_SIZE)
    value_row_block = key_value[:, KV_WIDTH:].reshape(-1, KEY_VALUE_HEADS, HEAD_SIZE)
    scores = (
        jnp.einsum("qghd,kgd->ghqk", query_rows, key_row_block, preferred_element_type=F32)
        * SCALE
    )
    scores = jnp.where(allowed, scores, MASKED)
    row_max = jnp.max(scores, axis=-1, keepdims=True)
    exponent = jnp.exp(scores - row_max)
    total = jnp.sum(exponent, axis=-1, keepdims=True)
    attention = (exponent / total).astype(BF16)
    log_total = row_max + jnp.log(total)
    mixture = jnp.einsum(
        "ghqk,kgd->qghd", attention, value_row_block, preferred_element_type=F32
    )
    mixture = gate(mixture, *near)
    mixture = spread(
        mixture.astype(BF16).reshape(count_of_rows, QUERY_HEADS * HEAD_SIZE), place.by_z
    )
    unused, projected = place.roles(product(mixture, one[0]), product(mixture, one[1]))
    middle = inputs + projected[:, :WIDTH]
    inv_two = rms_scale(middle)
    normed_two = spread((middle * inv_two * gain_two).astype(BF16), place.by_x)
    gate_pre, up_pre = place.roles(product(normed_two, two[0]), product(normed_two, two[1]))
    hidden = (jax.nn.silu(gate_pre) * up_pre).astype(BF16)
    left, right = place.roles(product(hidden, low[0]), product(hidden, low[1]))
    result = middle + jnp.concatenate([left, right[:, DOWN_SKIP:]], axis=1)
    stored = (
        inputs,
        inv_one,
        normed_one,
        query_rows,
        key_row_block,
        value_row_block,
        log_total,
        mixture,
        middle,
        inv_two,
        normed_two,
        gate_pre,
        up_pre,
        hidden,
    )
    return (result, stored, downs)


def with_sibling(own, sent):
    return jnp.concatenate([own, sibling(sent)], axis=0)


def norm_backward(grad, unit, inverse, gain):
    scaled = grad * gain
    return inverse * (scaled - unit * jnp.mean(scaled * unit, axis=-1, keepdims=True))


def partial_chunks(left, right):
    size = left.shape[1] // 4

    def chunk(distance):
        at = DISTANCES.index(distance)
        return outer_sum(left[:, at * size : (at + 1) * size], right).astype(BF16)

    return chunk


def by_quarter(place, block, rows):
    quarters = block.reshape(4, rows, block.shape[-1])

    def quarter(distance):
        return lax.dynamic_index_in_dim(quarters, (place.x + distance) % 4, 0, keepdims=False)

    return quarter


def reduce_first(left, right):
    return ring_sum(z_step, 1, partial_chunks(left, right))


def reduce_down(place, left, right):
    size = 2 * FF_PART

    def chunk(distance):
        part = lax.dynamic_slice_in_dim(left, (place.z + distance) % 4 * size, size, 1)
        return outer_sum(part, right).astype(BF16)

    pair = ring_sum(z_step, -1, chunk).astype(BF16)
    pair = pair.reshape(2, PADDED, UNIT)
    return jnp.concatenate(
        [
            lax.dynamic_index_in_dim(pair, place.y, 0, keepdims=False),
            lax.dynamic_index_in_dim(pair, 1 - place.y, 0, keepdims=False),
        ],
        axis=0,
    ).astype(F32)


def reduce_wide(left, right):
    chunk = partial_chunks(left, right)
    half = SPREAD // 8
    from_before = x_step(outer_sum(left[:, -2 * half : -half], right).astype(BF16), 1)
    from_after = x_step(outer_sum(left[:, -half:], right).astype(BF16), -1)
    after = chunk(1).astype(F32) + jnp.pad(from_before, ((0, half), (0, 0))).astype(F32)
    before = chunk(-1).astype(F32) + jnp.pad(from_after, ((half, 0), (0, 0))).astype(F32)
    column = (
        chunk(0).astype(F32)
        + x_step(after.astype(BF16), 1).astype(F32)
        + x_step(before.astype(BF16), -1).astype(F32)
    )
    parts = column.reshape(4, 2 * ROW_QUARTER, 2 * UNIT)
    pair = ring_sum(z_step, 1, lambda distance: parts[DISTANCES.index(distance)])
    quarter = pair[:ROW_QUARTER] + y_near(pair[ROW_QUARTER:].astype(BF16)).astype(F32)
    return ((from_before, from_after), column, quarter)


def across_y(pair):
    return pair[:PADDED] + y_near(pair[PADDED:].astype(BF16)).astype(F32)


def across_x(place, block):
    return direct_sum(x_step, by_quarter(place, block, ROW_QUARTER))


def finish(place, quarter):
    low = quarter.astype(BF16)
    piece = (low.astype(F32) + y_far(low).astype(F32)).astype(BF16)
    whole = jnp.zeros((4,) + piece.shape, BF16)
    for distance in DISTANCES:
        block = step_from(piece, distance)
        whole = lax.dynamic_update_slice_in_dim(
            whole, block[None], (place.x + distance) % 4, 0
        )
    return whole.reshape(-1, piece.shape[-1])


def step_from(piece, distance):
    return piece if distance == 0 else x_step(piece, -distance)


def backward_layer(
    place, grad_out, weights, low, stored, waits, before, cosine_table, sine_portion, allowed
):
    one, two, gain_one, gain_two = weights
    (
        inputs,
        inv_one,
        normed_one,
        query_rows,
        key_row_block,
        value_row_block,
        log_total,
        mixture,
        middle,
        inv_two,
        normed_two,
        gate_pre,
        up_pre,
        hidden,
    ) = stored
    count_of_rows = grad_out.shape[0]
    grad_low = grad_out.astype(BF16)
    left_low = grad_low[:, :DOWN_COLS]
    right_low = grad_low[:, WIDTH - DOWN_COLS :]
    right_once = jnp.where(jnp.arange(DOWN_COLS)[None] < DOWN_SKIP, 0, right_low)
    mine_low, other_low = place.roles(left_low, right_once)
    hidden_grad = backward_product(mine_low, low[0]) + backward_product(other_low, low[1])
    sigmoid_gate = jax.nn.sigmoid(gate_pre)
    grad_gate = (
        hidden_grad * up_pre * sigmoid_gate * (1.0 + gate_pre * (1.0 - sigmoid_gate))
    ).astype(BF16)
    grad_up = (hidden_grad * gate_pre * sigmoid_gate).astype(BF16)
    mine, other = place.roles(grad_gate, grad_up)
    spread_two = backward_product(mine, two[0]) + backward_product(other, two[1])
    left_rows = with_sibling(*2 * (jnp.concatenate([hidden, normed_two], axis=1),))
    right_rows = with_sibling(
        jnp.concatenate([place.role(left_low, right_low), mine], axis=1),
        jnp.concatenate([place.role(right_low, left_low), other], axis=1),
    )
    down = reduce_down(place, left_rows[:, : 2 * UNIT], right_rows[:, :DOWN_COLS])
    wide = reduce_wide(left_rows[:, 2 * UNIT :], right_rows[:, DOWN_COLS:])
    grad_normed_two = unspread(spread_two, place.by_x)
    unit_two = middle * inv_two
    grad_gain_two = jnp.sum(grad_normed_two * unit_two, axis=0)
    grad_normed_two = gate(grad_normed_two, *waits)
    grad_mid = grad_out + norm_backward(grad_normed_two, unit_two, inv_two, gain_two)
    none_narrow = jnp.zeros((count_of_rows, KV_WIDTH), BF16)
    output_side = jnp.concatenate([grad_mid.astype(BF16), none_narrow], axis=1)
    none = jnp.zeros_like(output_side)
    mine, other = place.roles(none, output_side)
    grad_mixture = (
        unspread(backward_product(mine, one[0]) + backward_product(other, one[1]), place.by_z)
        .astype(BF16)
        .reshape(count_of_rows, KEY_VALUE_HEADS, QUERY_HEADS // KEY_VALUE_HEADS, HEAD_SIZE)
    )
    scores = (
        jnp.einsum("qghd,kgd->ghqk", query_rows, key_row_block, preferred_element_type=F32)
        * SCALE
    )
    scores = jnp.where(allowed, scores, MASKED)
    attention_full = jnp.exp(scores - log_total)
    attention = attention_full.astype(BF16)
    value_gradient = jnp.einsum(
        "ghqk,qghd->kgd", attention, grad_mixture, preferred_element_type=F32
    )
    grad_attention = jnp.einsum(
        "qghd,kgd->ghqk", grad_mixture, value_row_block, preferred_element_type=F32
    )
    row_dots = jnp.sum(attention_full * grad_attention, axis=-1, keepdims=True)
    far, column, wide = wide
    row_dots = gate(row_dots, *far)
    grad_scores = (attention_full * (grad_attention - row_dots)).astype(BF16)
    key_gradient = (
        jnp.einsum("ghqk,qghd->kgd", grad_scores, query_rows, preferred_element_type=F32)
        * SCALE
    )
    key_value = scatter_rows(
        jnp.concatenate(
            [key_gradient.reshape(-1, KV_WIDTH), value_gradient.reshape(-1, KV_WIDTH)], axis=1
        ).astype(BF16)
    )
    grad_queries = (
        jnp.einsum("ghqk,kgd->qghd", grad_scores, key_row_block, preferred_element_type=F32)
        * SCALE
    )
    key_value = gate(key_value, column, down)
    before = before + [down]
    early = across_y(jnp.concatenate(before, axis=1)) if len(before) > 1 else None
    key_gradient, value_low = (key_value[:, :KV_WIDTH], key_value[:, KV_WIDTH:].astype(BF16))
    grad_query_key = rotary_embedding_backward(
        jnp.concatenate(
            [
                grad_queries.reshape(count_of_rows, QUERY_HEADS, HEAD_SIZE),
                key_gradient.reshape(count_of_rows, KEY_VALUE_HEADS, HEAD_SIZE),
            ],
            axis=1,
        ),
        cosine_table,
        sine_portion,
    )
    grad_query_key = grad_query_key.reshape(count_of_rows, UNIT).astype(BF16)
    value_side = jnp.concatenate([jnp.zeros((count_of_rows, WIDTH), BF16), value_low], axis=1)
    mine, other = place.roles(grad_query_key, value_side)
    grad_normed = unspread(
        backward_product(mine, one[0]) + backward_product(other, one[1]), place.by_z
    )
    unit_one = inputs * inv_one
    grad_gain_one = jnp.sum(grad_normed * unit_one, axis=0)
    grad_in = grad_mid + norm_backward(grad_normed, unit_one, inv_one, gain_one)
    gain_rows = jnp.stack([grad_gain_one.reshape(8, PART), grad_gain_two.reshape(8, PART)], axis=1)
    gain_rows = jnp.pad(gain_rows.reshape(16, PART).astype(BF16), ((0, 0), (0, UNIT - PART)))
    number = jnp.arange(16, dtype=jnp.int32)[:, None]
    inner = (jnp.arange(SPREAD, dtype=jnp.int32) % PADDED)[None]
    gain_place = (number // 2 == place.z_shard[None]) & (PART + number % 2 == inner)
    left_rows = with_sibling(
        jnp.concatenate([place.role(normed_one, mixture), normed_one], axis=1),
        jnp.concatenate([place.role(mixture, normed_one), normed_one], axis=1),
    )
    right_rows = with_sibling(
        jnp.concatenate([place.role(grad_query_key, output_side), place.role(none, value_side)], 1),
        jnp.concatenate([place.role(output_side, grad_query_key), place.role(value_side, none)], 1),
    )
    if len(before) > 1:
        early = across_x(place, early)
        left_rows = gate(left_rows, early)
    left_rows = jnp.concatenate(
        [left_rows[:, :SPREAD], left_rows[:, SPREAD:], gain_place.astype(BF16)], axis=0
    )
    right_rows = jnp.concatenate([right_rows[:, :UNIT], right_rows[:, UNIT:], gain_rows], axis=0)
    return (
        grad_in,
        (reduce_first(left_rows, right_rows), down, wide),
        early,
    )


def per_device(
    boundary,
    lengths,
    query_weight,
    key_matrix,
    value_matrix,
    output_weight,
    gate_weight,
    up_weight,
    down_weight,
    first_gain,
    second_gain,
):
    place = Place()
    first = place.first
    slab = boundary[0, :, 0]
    rows_dev = slab.shape[1]
    exchanged = sibling(jnp.where(first, slab[1], slab[0]))
    inputs = jnp.where(first, slab[0], exchanged).astype(F32)
    cotangent = jnp.where(first, exchanged, slab[1]).astype(F32)

    gains = jnp.pad(
        jnp.concatenate([first_gain, second_gain], axis=0), ((0, 6), (0, UNIT - PART))
    )
    role_packs = (
        (
            jnp.concatenate(
                [jnp.concatenate([query_weight[0], key_matrix[0]], axis=1), gains], axis=0
            ),
            jnp.pad(gate_weight[0], ((0, PADDED - PART), (0, 0))),
            down_weight[0, :, :DOWN_COLS],
        ),
        (
            jnp.concatenate(
                [jnp.concatenate([output_weight[0], value_matrix[0]], axis=1), gains], axis=0
            ),
            jnp.pad(up_weight[0], ((0, PADDED - PART), (0, 0))),
            down_weight[0, :, WIDTH - DOWN_COLS :],
        ),
    )
    layer_packs = ([], [])
    for zero, one in zip(*role_packs):
        kept = jnp.where(first, zero, one)
        other = sibling(jnp.where(first, one, zero))
        layer_packs[0].append(jnp.where(first, kept, other))
        layer_packs[1].append(jnp.where(first, other, kept))
    first_pack, wide_pack, down_pack = [jnp.stack(both) for both in zip(*layer_packs)]
    wide, near_wide, started = gather_wide(place, wide_pack)
    one, unused = gather_first(place, first_pack, started)
    weights_first, weights_second = [layer_weights(place, mine) for mine in zip(one, wide)]

    seq_lengths = jnp.where(first, lengths[0, 0], lengths[0, 1])
    inner = jnp.arange(rows_dev, dtype=jnp.int32)
    own_rows = place.shard * rows_dev + inner
    all_rows = (place.near_shards[:, None] * rows_dev + inner[None]).reshape(-1)
    segment_mine, position_mine = segment_rows(seq_lengths, own_rows)
    segment_all, unused_position = segment_rows(seq_lengths, all_rows)
    allowed = (segment_mine[:, None] == segment_all[None, :]) & (
        own_rows[:, None] >= all_rows[None, :]
    )
    cosine_table, sine_portion = rotary_tables(position_mine)
    live_rows = (segment_mine < seq_lengths.shape[0]).astype(F32)

    geometry = (cosine_table, sine_portion, allowed)
    def fetch(key_value):
        wholes, near = gather_down(place, down_pack, (key_value,))
        return ([(value, sibling(value)) for value in wholes], near)

    middle, stored_first, downs = forward_layer(
        place, inputs, weights_first, fetch, near_wide, *geometry
    )
    middle = middle.astype(BF16).astype(F32)
    result, stored_second, unused = forward_layer(
        place, middle, weights_second, lambda key_value: (downs[1:], ()), (), *geometry
    )
    grad, (pair, down, wide), unused = backward_layer(
        place,
        cotangent * live_rows[:, None],
        weights_second,
        downs[1],
        stored_second,
        (),
        [],
        *geometry,
    )
    grad = grad.astype(BF16).astype(F32)
    grad, (last, unused, wide_first), early = backward_layer(
        place,
        grad,
        weights_first,
        downs[0],
        stored_first,
        (pair, wide),
        [pair, down],
        *geometry,
    )

    ends = (grad.astype(BF16), result.astype(BF16))
    received = sibling(jnp.where(first, ends[1], ends[0]))
    boundary_out = jnp.where(
        first, jnp.stack([ends[0], received]), jnp.stack([received, ends[1]])
    )[None, :, None]

    early = finish(place, jnp.concatenate([early, wide, wide_first], axis=1))
    late_first = finish(place, across_x(place, across_y(last)))
    late_second = early[:, :UNIT]
    early_second = jnp.concatenate([early[:, UNIT : 2 * UNIT], early[:, 3 * UNIT : 5 * UNIT]], 1)
    early_first = jnp.concatenate([early[:, 2 * UNIT : 3 * UNIT], early[:, 5 * UNIT :]], 1)
    sums = []
    for for_first, for_second in ((early_first, early_second), (late_first, late_second)):
        own = jnp.where(first, for_first, for_second)
        other = sibling(jnp.where(first, for_second, for_first))
        sums.append([value.astype(F32) for value in place.roles(own, other)])
    down_left, down_right = [value[:, :UNIT].reshape(FF_PART, DOWN_COLS) for value in sums[0]]
    gate_sum, up_sum = [value[:, UNIT:] for value in sums[0]]
    query_key, output_value = sums[1]
    gain_sums = query_key[PART : PART + 2, :PART] + output_value[PART : PART + 2, :PART]
    return (
        boundary_out,
        query_key[None, :PART, :WIDTH],
        query_key[None, :PART, WIDTH:],
        output_value[None, :PART, WIDTH:],
        output_value[None, :PART, :WIDTH],
        gate_sum[None, :PART],
        up_sum[None, :PART],
        jnp.concatenate([down_left, down_right[:, DOWN_SKIP:]], axis=1)[None],
        gain_sums[:1],
        gain_sums[1:],
    )


def solution(mesh):
    placed = (
        P("section", None, "dp", "fsdp", None),
        P("dp", None, None),
        P("section", "fsdp", None),
        P("section", "fsdp", None),
        P("section", "fsdp", None),
        P("section", "fsdp", None),
        P("section", "fsdp", None),
        P("section", "fsdp", None),
        P("section", "fsdp", None),
        P("section", "fsdp"),
        P("section", "fsdp"),
    )
    return jax.shard_map(
        per_device,
        mesh=mesh,
        in_specs=placed,
        out_specs=(
            P("section", None, "dp", "fsdp", None),
            P("section", "fsdp", None),
            P("section", "fsdp", None),
            P("section", "fsdp", None),
            P("section", "fsdp", None),
            P("section", "fsdp", None),
            P("section", "fsdp", None),
            P("section", "fsdp", None),
            P("section", "fsdp"),
            P("section", "fsdp"),
        ),
        check_vma=False,
    )
```

```python
import jax
import jax.numpy as jnp
from jax import lax
from jax.sharding import PartitionSpec as P

QUERY_HEADS = 15
KEY_VALUE_HEADS = 5
HEAD_SIZE = 64


EPS = 1e-05
SCALE = 0.125
MASKED = -1e30


BF16 = jnp.bfloat16
F32 = jnp.float32
WIDTH = 960
PART = 120
PADDED = 128
SPREAD = 1024
UNIT = 1280
FF_PART = 320
FF_QUARTER = 80
DOWN_COLS = 512
DOWN_SKIP = 64
ROW_QUARTER = 32
KV_WIDTH = KEY_VALUE_HEADS * HEAD_SIZE
DISTANCES = (0, -1, 1, 2)


def segment_rows(seq_lengths, row_index):
    seq_ends = jnp.cumsum(seq_lengths)
    starts = seq_ends - seq_lengths
    segment = jnp.sum((row_index[:, None] >= seq_ends[None, :]).astype(jnp.int32), axis=1)
    slot_ids = jnp.arange(seq_lengths.shape[0], dtype=jnp.int32)
    row_start = jnp.sum(
        jnp.where(segment[:, None] == slot_ids[None, :], starts[None, :], 0), axis=1
    )
    return (segment, row_index - row_start)


def rotary_tables(position):
    frequency = 10000.0 ** (-2.0 * jnp.arange(HEAD_SIZE // 2, dtype=jnp.float32) / HEAD_SIZE)
    angles = position.astype(jnp.float32)[:, None] * frequency[None, :]
    return (jnp.cos(angles)[:, None, :], jnp.sin(angles)[:, None, :])


def rotary_embedding(vector, cosine_table, sine_portion):
    first_half = vector[..., : HEAD_SIZE // 2]
    second_half = vector[..., HEAD_SIZE // 2 :]
    return jnp.concatenate(
        [
            first_half * cosine_table - second_half * sine_portion,
            second_half * cosine_table + first_half * sine_portion,
        ],
        axis=-1,
    )


def rotary_embedding_backward(grad, cosine_table, sine_portion):
    first_half = grad[..., : HEAD_SIZE // 2]
    second_half = grad[..., HEAD_SIZE // 2 :]
    return jnp.concatenate(
        [
            first_half * cosine_table + second_half * sine_portion,
            second_half * cosine_table - first_half * sine_portion,
        ],
        axis=-1,
    )


def rms_scale(values):
    return lax.rsqrt(jnp.mean(values * values, axis=-1, keepdims=True) + EPS)


def outer_sum(left, right):
    return lax.dot_general(
        left, right, (((0,), (0,)), ((), ())), preferred_element_type=jnp.float32
    )


def backward_product(grad, weight):
    return lax.dot_general(
        grad, weight, (((1,), (1,)), ((), ())), preferred_element_type=jnp.float32
    )


def z_step(value, step):
    return lax.ppermute(value, "fsdp", [(i, (i + 2 * step) % 8) for i in range(8)])


def x_step(value, step):
    return lax.ppermute(value, "dp", [(i, (i + 2 * step) % 8) for i in range(8)])


def y_near(value):
    return lax.ppermute(value, "fsdp", [(i, i ^ 1) for i in range(8)])


def y_far(value):
    return lax.ppermute(value, "dp", [(i, i ^ 1) for i in range(8)])


def sibling(value):
    return lax.ppermute(value, "section", [(0, 1), (1, 0)])


def ring_gather(step, way, block):
    before = step(block, 1)
    after = step(block, -1)
    far = step(before if way == 1 else after, way)
    return [block, before, after, far]


def ring_sum(step, way, chunk, waits=((), ())):
    relayed = gate(step(chunk(2).astype(BF16), way), *waits[0])
    other = step(chunk(-way).astype(BF16), -way)
    nearer = (chunk(way).astype(F32) + relayed.astype(F32)).astype(BF16)
    total = chunk(0).astype(F32) + other.astype(F32) + step(nearer, way).astype(F32)
    return gate(total, *waits[1])


def direct_sum(step, chunk):
    total = chunk(0).astype(F32)
    for distance in (1, -1, 2):
        total = total + step(chunk(distance).astype(BF16), distance).astype(F32)
    return total


class Place:
    def __init__(self):
        self.section = lax.axis_index("section")
        self.shard = lax.axis_index("fsdp")
        dp = lax.axis_index("dp")
        self.z, self.y = self.shard // 2, self.shard % 2
        self.x = dp // 2
        self.first = self.section == 0
        self.near_shards = jnp.stack(
            [(self.z + d) % 4 * 2 + (self.y + near) % 2 for d in DISTANCES for near in (0, 1)]
        )
        row = lax.broadcasted_iota(jnp.int32, (WIDTH, SPREAD), 0)
        column = jnp.arange(SPREAD, dtype=jnp.int32)
        self.z_shard = jnp.repeat(self.near_shards, PADDED)
        self.by_z = (
            (row // PART == self.z_shard[None]) & (row % PART == (column % PADDED)[None])
        ).astype(BF16)
        quarters = jnp.repeat(jnp.stack([(self.x + d) % 4 for d in DISTANCES]), SPREAD // 4)
        shards = jnp.tile(jnp.repeat(self.near_shards, ROW_QUARTER), 4)
        inner = quarters * ROW_QUARTER + column % ROW_QUARTER
        self.by_x = ((row // PART == shards[None]) & (row % PART == inner[None])).astype(BF16)

    def role(self, zero, one):
        return jnp.where(self.first, zero, one)

    def roles(self, mine, other):
        return (jnp.where(self.first, mine, other), jnp.where(self.first, other, mine))


def spread(value, places):
    return jnp.dot(value, places, preferred_element_type=F32).astype(BF16)


def unspread(value, places):
    high = lax.reduce_precision(value, 8, 7)
    both = jnp.concatenate([high.astype(BF16), (value - high).astype(BF16)], axis=1)
    return backward_product(both, jnp.concatenate([places, places], axis=1))


def product(left, right):
    return jnp.dot(left, right, preferred_element_type=F32)


def gate(value, *others):
    late = False
    for other in others:
        corner = other[(-1,) * other.ndim]
        late = late | (corner != corner)
    return jax.tree.map(lambda part: jnp.where(late, jnp.zeros_like(part), part), value)


def ring_gather_both(step, block):
    before = step(block, 1)
    after = step(block, -1)
    far = (step(before[0], 1), step(after[1], -1))
    layers = [[block[n], before[n], after[n], far[n]] for n in range(2)]
    return (layers, (before, after))


def gather_first(place, own, waits):
    own = gate(own, waits[0])
    other = y_near(own)
    pair = jnp.stack([own, other], axis=1).reshape(2, 2 * PADDED, UNIT)
    pair = gate(pair, waits[1])
    layers, unused = ring_gather_both(z_step, pair)
    return ([jnp.concatenate(blocks, axis=0) for blocks in layers], other)


def gather_down(place, own, start, waits):
    own = gate(own, start)
    other = y_near(own)
    low, high = (jnp.where(place.y == 0, own, other), jnp.where(place.y == 0, other, own))
    pair = jnp.stack([low, high], axis=1).reshape(2, 2 * FF_PART, DOWN_COLS)
    pair = gate(pair, *waits)
    layers, near = ring_gather_both(z_step, pair)
    wholes = []
    for blocks in layers:
        whole = jnp.zeros((4,) + pair.shape[1:], BF16)
        for distance, block in zip(DISTANCES, blocks):
            whole = lax.dynamic_update_slice_in_dim(
                whole, block[None], (place.z + distance) % 4, 0
            )
        wholes.append(whole.reshape(-1, DOWN_COLS))
    return (wholes, near)


def gather_wide(place, own):
    quarter = lax.dynamic_slice_in_dim(own, place.x * ROW_QUARTER, ROW_QUARTER, 1)
    other = y_near(quarter)
    pair = jnp.stack([quarter, other], axis=1)
    blocks = ring_gather(z_step, -1, pair)
    column = jnp.stack(blocks, axis=1)
    column = column.reshape(2, SPREAD // 4, 2 * UNIT)
    layers, near = ring_gather_both(x_step, column)
    started = (other, blocks[-1])
    return ([jnp.concatenate(blocks, axis=0) for blocks in layers], near, started)


def layer_weights(place, mine):
    one, two = [(value, sibling(value)) for value in mine]
    gains = one[0].reshape(8, PADDED, UNIT)[:, PART : PART + 2, :PADDED]
    gains = backward_product(gains.transpose(1, 0, 2).reshape(2, SPREAD), place.by_z)
    return (one, two, gains[:1], gains[1:])


def gather_rows(own):
    pair = jnp.concatenate([own, y_near(own)], axis=0)
    return jnp.concatenate(ring_gather(z_step, 1, pair), axis=0)


def scatter_rows(partial):
    parts = partial.reshape(4, -1, partial.shape[1])
    pair = ring_sum(z_step, -1, lambda distance: parts[DISTANCES.index(distance)])
    rows = pair.shape[0] // 2
    return pair[:rows] + y_near(pair[rows:].astype(BF16)).astype(F32)


def forward_layer(place, inputs, weights, fetch, waits, cosine_table, sine_portion, allowed):
    one, two, gain_one, gain_two = weights
    count_of_rows = inputs.shape[0]
    inv_one = rms_scale(inputs)
    normed_one = spread((inputs * inv_one * gain_one).astype(BF16), place.by_z)
    query_key, value_part = place.roles(product(normed_one, one[0]), product(normed_one, one[1]))
    value_part = value_part[:, WIDTH:].astype(BF16)
    turned = rotary_embedding(
        query_key.reshape(count_of_rows, QUERY_HEADS + KEY_VALUE_HEADS, HEAD_SIZE),
        cosine_table,
        sine_portion,
    ).astype(BF16)
    query_rows = turned[:, :QUERY_HEADS].reshape(
        count_of_rows, KEY_VALUE_HEADS, QUERY_HEADS // KEY_VALUE_HEADS, HEAD_SIZE
    )
    key_portion = turned[:, QUERY_HEADS:].reshape(count_of_rows, KV_WIDTH)
    key_value = gather_rows(jnp.concatenate([key_portion, value_part], axis=1))
    downs, near = fetch(key_value)
    low = downs[0]
    key_value = gate(key_value, *waits)
    key_row_block = key_value[:, :KV_WIDTH].reshape(-1, KEY_VALUE_HEADS, HEAD_SIZE)
    value_row_block = key_value[:, KV_WIDTH:].reshape(-1, KEY_VALUE_HEADS, HEAD_SIZE)
    scores = (
        jnp.einsum("qghd,kgd->ghqk", query_rows, key_row_block, preferred_element_type=F32)
        * SCALE
    )
    scores = jnp.where(allowed, scores, MASKED)
    row_max = jnp.max(scores, axis=-1, keepdims=True)
    exponent = jnp.exp(scores - row_max)
    total = jnp.sum(exponent, axis=-1, keepdims=True)
    attention = (exponent / total).astype(BF16)
    log_total = row_max + jnp.log(total)
    mixture = jnp.einsum(
        "ghqk,kgd->qghd", attention, value_row_block, preferred_element_type=F32
    )
    mixture = gate(mixture, *near)
    mixture = spread(
        mixture.astype(BF16).reshape(count_of_rows, QUERY_HEADS * HEAD_SIZE), place.by_z
    )
    unused, projected = place.roles(product(mixture, one[0]), product(mixture, one[1]))
    middle = inputs + projected[:, :WIDTH]
    inv_two = rms_scale(middle)
    normed_two = spread((middle * inv_two * gain_two).astype(BF16), place.by_x)
    gate_pre, up_pre = place.roles(product(normed_two, two[0]), product(normed_two, two[1]))
    hidden = (jax.nn.silu(gate_pre) * up_pre).astype(BF16)
    left, right = place.roles(product(hidden, low[0]), product(hidden, low[1]))
    result = middle + jnp.concatenate([left, right[:, DOWN_SKIP:]], axis=1)
    stored = (
        inputs,
        inv_one,
        normed_one,
        query_rows,
        key_row_block,
        value_row_block,
        log_total,
        mixture,
        middle,
        inv_two,
        normed_two,
        gate_pre,
        up_pre,
        hidden,
    )
    return (result, stored, downs)


def with_sibling(own, sent):
    return jnp.concatenate([own, sibling(sent)], axis=0)


def norm_backward(grad, unit, inverse, gain):
    scaled = grad * gain
    return inverse * (scaled - unit * jnp.mean(scaled * unit, axis=-1, keepdims=True))


def partial_chunks(left, right):
    size = left.shape[1] // 4

    def chunk(distance):
        at = DISTANCES.index(distance)
        return outer_sum(left[:, at * size : (at + 1) * size], right).astype(BF16)

    return chunk


def by_quarter(place, block, rows):
    quarters = block.reshape(4, rows, block.shape[-1])

    def quarter(distance):
        return lax.dynamic_index_in_dim(quarters, (place.x + distance) % 4, 0, keepdims=False)

    return quarter


def reduce_first(left, right, waits):
    return ring_sum(z_step, 1, partial_chunks(left, right), waits)


def reduce_down(place, left, right):
    size = 2 * FF_PART

    def chunk(distance):
        part = lax.dynamic_slice_in_dim(left, (place.z + distance) % 4 * size, size, 1)
        return outer_sum(part, right).astype(BF16)

    pair = ring_sum(z_step, -1, chunk).astype(BF16)
    pair = pair.reshape(2, PADDED, UNIT)
    return jnp.concatenate(
        [
            lax.dynamic_index_in_dim(pair, place.y, 0, keepdims=False),
            lax.dynamic_index_in_dim(pair, 1 - place.y, 0, keepdims=False),
        ],
        axis=0,
    ).astype(F32)


def reduce_wide(left, right):
    chunk = partial_chunks(left, right)
    half = SPREAD // 8
    from_before = x_step(outer_sum(left[:, -2 * half : -half], right).astype(BF16), 1)
    from_after = x_step(outer_sum(left[:, -half:], right).astype(BF16), -1)
    after = chunk(1).astype(F32) + jnp.pad(from_before, ((0, half), (0, 0))).astype(F32)
    before = chunk(-1).astype(F32) + jnp.pad(from_after, ((half, 0), (0, 0))).astype(F32)
    column = (
        chunk(0).astype(F32)
        + x_step(after.astype(BF16), 1).astype(F32)
        + x_step(before.astype(BF16), -1).astype(F32)
    )
    parts = column.reshape(4, 2 * ROW_QUARTER, 2 * UNIT)
    pair = ring_sum(z_step, 1, lambda distance: parts[DISTANCES.index(distance)])
    quarter = pair[:ROW_QUARTER] + y_near(pair[ROW_QUARTER:].astype(BF16)).astype(F32)
    return ((from_before, from_after), column, quarter)


def across_y(pair):
    return pair[:PADDED] + y_near(pair[PADDED:].astype(BF16)).astype(F32)


def across_x(place, block):
    return direct_sum(x_step, by_quarter(place, block, ROW_QUARTER))


def across_far(quarter):
    low = quarter.astype(BF16)
    return (low.astype(F32) + y_far(low).astype(F32)).astype(BF16)


def all_quarters(place, piece):
    whole = jnp.zeros((4,) + piece.shape, BF16)
    for distance in DISTANCES:
        block = step_from(piece, distance)
        whole = lax.dynamic_update_slice_in_dim(
            whole, block[None], (place.x + distance) % 4, 0
        )
    return whole.reshape(-1, piece.shape[-1])


def step_from(piece, distance):
    return piece if distance == 0 else x_step(piece, -distance)


def backward_layer(
    place, grad_out, weights, low, stored, waits, before, cosine_table, sine_portion, allowed
):
    one, two, gain_one, gain_two = weights
    (
        inputs,
        inv_one,
        normed_one,
        query_rows,
        key_row_block,
        value_row_block,
        log_total,
        mixture,
        middle,
        inv_two,
        normed_two,
        gate_pre,
        up_pre,
        hidden,
    ) = stored
    count_of_rows = grad_out.shape[0]
    grad_low = grad_out.astype(BF16)
    left_low = grad_low[:, :DOWN_COLS]
    right_low = grad_low[:, WIDTH - DOWN_COLS :]
    right_once = jnp.where(jnp.arange(DOWN_COLS)[None] < DOWN_SKIP, 0, right_low)
    mine_low, other_low = place.roles(left_low, right_once)
    hidden_grad = backward_product(mine_low, low[0]) + backward_product(other_low, low[1])
    sigmoid_gate = jax.nn.sigmoid(gate_pre)
    grad_gate = (
        hidden_grad * up_pre * sigmoid_gate * (1.0 + gate_pre * (1.0 - sigmoid_gate))
    ).astype(BF16)
    grad_up = (hidden_grad * gate_pre * sigmoid_gate).astype(BF16)
    mine, other = place.roles(grad_gate, grad_up)
    spread_two = backward_product(mine, two[0]) + backward_product(other, two[1])
    left_rows = with_sibling(*2 * (jnp.concatenate([hidden, normed_two], axis=1),))
    right_rows = with_sibling(
        jnp.concatenate([place.role(left_low, right_low), mine], axis=1),
        jnp.concatenate([place.role(right_low, left_low), other], axis=1),
    )
    down = reduce_down(place, left_rows[:, : 2 * UNIT], right_rows[:, :DOWN_COLS])
    wide = reduce_wide(left_rows[:, 2 * UNIT :], right_rows[:, DOWN_COLS:])
    grad_normed_two = unspread(spread_two, place.by_x)
    unit_two = middle * inv_two
    grad_gain_two = jnp.sum(grad_normed_two * unit_two, axis=0)
    grad_normed_two = gate(grad_normed_two, *waits)
    grad_mid = grad_out + norm_backward(grad_normed_two, unit_two, inv_two, gain_two)
    none_narrow = jnp.zeros((count_of_rows, KV_WIDTH), BF16)
    output_side = jnp.concatenate([grad_mid.astype(BF16), none_narrow], axis=1)
    none = jnp.zeros_like(output_side)
    mine, other = place.roles(none, output_side)
    grad_mixture = (
        unspread(backward_product(mine, one[0]) + backward_product(other, one[1]), place.by_z)
        .astype(BF16)
        .reshape(count_of_rows, KEY_VALUE_HEADS, QUERY_HEADS // KEY_VALUE_HEADS, HEAD_SIZE)
    )
    scores = (
        jnp.einsum("qghd,kgd->ghqk", query_rows, key_row_block, preferred_element_type=F32)
        * SCALE
    )
    scores = jnp.where(allowed, scores, MASKED)
    attention_full = jnp.exp(scores - log_total)
    attention = attention_full.astype(BF16)
    value_gradient = jnp.einsum(
        "ghqk,qghd->kgd", attention, grad_mixture, preferred_element_type=F32
    )
    grad_attention = jnp.einsum(
        "qghd,kgd->ghqk", grad_mixture, value_row_block, preferred_element_type=F32
    )
    row_dots = jnp.sum(attention_full * grad_attention, axis=-1, keepdims=True)
    far, column, wide = wide
    row_dots = gate(row_dots, *far)
    grad_scores = (attention_full * (grad_attention - row_dots)).astype(BF16)
    key_gradient = (
        jnp.einsum("ghqk,qghd->kgd", grad_scores, query_rows, preferred_element_type=F32)
        * SCALE
    )
    key_value = scatter_rows(
        jnp.concatenate(
            [key_gradient.reshape(-1, KV_WIDTH), value_gradient.reshape(-1, KV_WIDTH)], axis=1
        ).astype(BF16)
    )
    grad_queries = (
        jnp.einsum("ghqk,kgd->qghd", grad_scores, key_row_block, preferred_element_type=F32)
        * SCALE
    )
    key_value = gate(key_value, column, down)
    early = None
    if before:
        early = across_y(jnp.concatenate(before[:2] + [down], axis=1))
    key_gradient, value_low = (key_value[:, :KV_WIDTH], key_value[:, KV_WIDTH:].astype(BF16))
    grad_query_key = rotary_embedding_backward(
        jnp.concatenate(
            [
                grad_queries.reshape(count_of_rows, QUERY_HEADS, HEAD_SIZE),
                key_gradient.reshape(count_of_rows, KEY_VALUE_HEADS, HEAD_SIZE),
            ],
            axis=1,
        ),
        cosine_table,
        sine_portion,
    )
    grad_query_key = grad_query_key.reshape(count_of_rows, UNIT).astype(BF16)
    value_side = jnp.concatenate([jnp.zeros((count_of_rows, WIDTH), BF16), value_low], axis=1)
    mine, other = place.roles(grad_query_key, value_side)
    grad_normed = unspread(
        backward_product(mine, one[0]) + backward_product(other, one[1]), place.by_z
    )
    unit_one = inputs * inv_one
    grad_gain_one = jnp.sum(grad_normed * unit_one, axis=0)
    grad_in = grad_mid + norm_backward(grad_normed, unit_one, inv_one, gain_one)
    gain_rows = jnp.stack([grad_gain_one.reshape(8, PART), grad_gain_two.reshape(8, PART)], axis=1)
    gain_rows = jnp.pad(gain_rows.reshape(16, PART).astype(BF16), ((0, 0), (0, UNIT - PART)))
    number = jnp.arange(16, dtype=jnp.int32)[:, None]
    inner = (jnp.arange(SPREAD, dtype=jnp.int32) % PADDED)[None]
    gain_place = (number // 2 == place.z_shard[None]) & (PART + number % 2 == inner)
    left_rows = with_sibling(
        jnp.concatenate([place.role(normed_one, mixture), normed_one], axis=1),
        jnp.concatenate([place.role(mixture, normed_one), normed_one], axis=1),
    )
    right_rows = with_sibling(
        jnp.concatenate([place.role(grad_query_key, output_side), place.role(none, value_side)], 1),
        jnp.concatenate([place.role(output_side, grad_query_key), place.role(value_side, none)], 1),
    )
    waits = ((), ())
    if before:
        left_rows = gate(left_rows, early)
        early = across_x(place, early)
        piece = across_far(jnp.concatenate([early, before[2]], axis=1))
        waits = ((early,), (piece,))
        early = all_quarters(place, piece)
    left_rows = jnp.concatenate(
        [left_rows[:, :SPREAD], left_rows[:, SPREAD:], gain_place.astype(BF16)], axis=0
    )
    right_rows = jnp.concatenate([right_rows[:, :UNIT], right_rows[:, UNIT:], gain_rows], axis=0)
    return (
        grad_in,
        (reduce_first(left_rows, right_rows, waits), down, wide),
        early,
    )


def per_device(
    boundary,
    lengths,
    query_weight,
    key_matrix,
    value_matrix,
    output_weight,
    gate_weight,
    up_weight,
    down_weight,
    first_gain,
    second_gain,
):
    place = Place()
    first = place.first
    slab = boundary[0, :, 0]
    rows_dev = slab.shape[1]
    exchanged = sibling(jnp.where(first, slab[1], slab[0]))
    inputs = jnp.where(first, slab[0], exchanged).astype(F32)
    cotangent = jnp.where(first, exchanged, slab[1]).astype(F32)

    gains = jnp.pad(
        jnp.concatenate([first_gain, second_gain], axis=0), ((0, 6), (0, UNIT - PART))
    )
    role_packs = (
        (
            jnp.concatenate(
                [jnp.concatenate([query_weight[0], key_matrix[0]], axis=1), gains], axis=0
            ),
            jnp.pad(gate_weight[0], ((0, PADDED - PART), (0, 0))),
            down_weight[0, :, :DOWN_COLS],
        ),
        (
            jnp.concatenate(
                [jnp.concatenate([output_weight[0], value_matrix[0]], axis=1), gains], axis=0
            ),
            jnp.pad(up_weight[0], ((0, PADDED - PART), (0, 0))),
            down_weight[0, :, WIDTH - DOWN_COLS :],
        ),
    )
    layer_packs = ([], [])
    for zero, one in zip(*role_packs):
        kept = jnp.where(first, zero, one)
        other = sibling(jnp.where(first, one, zero))
        layer_packs[0].append(jnp.where(first, kept, other))
        layer_packs[1].append(jnp.where(first, other, kept))
    first_pack, wide_pack, down_pack = [jnp.stack(both) for both in zip(*layer_packs)]
    wide, near_wide, started = gather_wide(place, wide_pack)
    one, other = gather_first(place, first_pack, started)
    weights_first, weights_second = [layer_weights(place, mine) for mine in zip(one, wide)]

    seq_lengths = jnp.where(first, lengths[0, 0], lengths[0, 1])
    inner = jnp.arange(rows_dev, dtype=jnp.int32)
    own_rows = place.shard * rows_dev + inner
    all_rows = (place.near_shards[:, None] * rows_dev + inner[None]).reshape(-1)
    segment_mine, position_mine = segment_rows(seq_lengths, own_rows)
    segment_all, unused_position = segment_rows(seq_lengths, all_rows)
    allowed = (segment_mine[:, None] == segment_all[None, :]) & (
        own_rows[:, None] >= all_rows[None, :]
    )
    cosine_table, sine_portion = rotary_tables(position_mine)
    live_rows = (segment_mine < seq_lengths.shape[0]).astype(F32)

    geometry = (cosine_table, sine_portion, allowed)
    def fetch(key_value):
        wholes, near = gather_down(place, down_pack, other, (key_value,))
        return ([(value, sibling(value)) for value in wholes], near)

    middle, stored_first, downs = forward_layer(
        place, inputs, weights_first, fetch, near_wide, *geometry
    )
    middle = middle.astype(BF16).astype(F32)
    result, stored_second, unused = forward_layer(
        place, middle, weights_second, lambda key_value: (downs[1:], ()), (), *geometry
    )
    grad, (pair, down, wide), unused = backward_layer(
        place,
        cotangent * live_rows[:, None],
        weights_second,
        downs[1],
        stored_second,
        (),
        [],
        *geometry,
    )
    grad = grad.astype(BF16).astype(F32)
    grad, (last, unused, wide_first), early = backward_layer(
        place,
        grad,
        weights_first,
        downs[0],
        stored_first,
        (pair, wide),
        [pair, down, wide],
        *geometry,
    )

    ends = (grad.astype(BF16), result.astype(BF16))
    received = sibling(jnp.where(first, ends[1], ends[0]))
    boundary_out = jnp.where(
        first, jnp.stack([ends[0], received]), jnp.stack([received, ends[1]])
    )[None, :, None]

    late = across_x(place, across_y(gate(last, early)))
    late = all_quarters(place, across_far(jnp.concatenate([late, wide_first], axis=1)))
    late_first = late[:, :UNIT]
    early_first = jnp.concatenate([early[:, 2 * UNIT : 3 * UNIT], late[:, UNIT:]], axis=1)
    late_second = early[:, :UNIT]
    early_second = jnp.concatenate([early[:, UNIT : 2 * UNIT], early[:, 3 * UNIT :]], axis=1)

    sums = []
    for for_first, for_second in ((early_first, early_second), (late_first, late_second)):
        own = jnp.where(first, for_first, for_second)
        other = sibling(jnp.where(first, for_second, for_first))
        sums.append([value.astype(F32) for value in place.roles(own, other)])
    down_left, down_right = [value[:, :UNIT].reshape(FF_PART, DOWN_COLS) for value in sums[0]]
    gate_sum, up_sum = [value[:, UNIT:] for value in sums[0]]
    query_key, output_value = sums[1]
    gain_sums = query_key[PART : PART + 2, :PART] + output_value[PART : PART + 2, :PART]
    return (
        boundary_out,
        query_key[None, :PART, :WIDTH],
        query_key[None, :PART, WIDTH:],
        output_value[None, :PART, WIDTH:],
        output_value[None, :PART, :WIDTH],
        gate_sum[None, :PART],
        up_sum[None, :PART],
        jnp.concatenate([down_left, down_right[:, DOWN_SKIP:]], axis=1)[None],
        gain_sums[:1],
        gain_sums[1:],
    )


def solution(mesh):
    placed = (
        P("section", None, "dp", "fsdp", None),
        P("dp", None, None),
        P("section", "fsdp", None),
        P("section", "fsdp", None),
        P("section", "fsdp", None),
        P("section", "fsdp", None),
        P("section", "fsdp", None),
        P("section", "fsdp", None),
        P("section", "fsdp", None),
        P("section", "fsdp"),
        P("section", "fsdp"),
    )
    return jax.shard_map(
        per_device,
        mesh=mesh,
        in_specs=placed,
        out_specs=(
            P("section", None, "dp", "fsdp", None),
            P("section", "fsdp", None),
            P("section", "fsdp", None),
            P("section", "fsdp", None),
            P("section", "fsdp", None),
            P("section", "fsdp", None),
            P("section", "fsdp", None),
            P("section", "fsdp", None),
            P("section", "fsdp"),
            P("section", "fsdp"),
        ),
        check_vma=False,
    )
```

```python
import jax
import jax.numpy as jnp
from jax import lax
from jax.sharding import PartitionSpec as P

QUERY_HEADS = 15
KEY_VALUE_HEADS = 5
HEAD_SIZE = 64


EPS = 1e-05
SCALE = 0.125
MASKED = -1e30


BF16 = jnp.bfloat16
F32 = jnp.float32
WIDTH = 960
PART = 120
PADDED = 128
SPREAD = 1024
UNIT = 1280
FF_PART = 320
FF_QUARTER = 80
DOWN_COLS = 512
DOWN_SKIP = 64
ROW_QUARTER = 32
KV_WIDTH = KEY_VALUE_HEADS * HEAD_SIZE
DISTANCES = (0, -1, 1, 2)


def segment_rows(seq_lengths, row_index):
    seq_ends = jnp.cumsum(seq_lengths)
    starts = seq_ends - seq_lengths
    segment = jnp.sum((row_index[:, None] >= seq_ends[None, :]).astype(jnp.int32), axis=1)
    slot_ids = jnp.arange(seq_lengths.shape[0], dtype=jnp.int32)
    row_start = jnp.sum(
        jnp.where(segment[:, None] == slot_ids[None, :], starts[None, :], 0), axis=1
    )
    return (segment, row_index - row_start)


def rotary_tables(position):
    frequency = 10000.0 ** (-2.0 * jnp.arange(HEAD_SIZE // 2, dtype=jnp.float32) / HEAD_SIZE)
    angles = position.astype(jnp.float32)[:, None] * frequency[None, :]
    return (jnp.cos(angles)[:, None, :], jnp.sin(angles)[:, None, :])


def rotary_embedding(vector, cosine_table, sine_portion):
    first_half = vector[..., : HEAD_SIZE // 2]
    second_half = vector[..., HEAD_SIZE // 2 :]
    return jnp.concatenate(
        [
            first_half * cosine_table - second_half * sine_portion,
            second_half * cosine_table + first_half * sine_portion,
        ],
        axis=-1,
    )


def rotary_embedding_backward(grad, cosine_table, sine_portion):
    first_half = grad[..., : HEAD_SIZE // 2]
    second_half = grad[..., HEAD_SIZE // 2 :]
    return jnp.concatenate(
        [
            first_half * cosine_table + second_half * sine_portion,
            second_half * cosine_table - first_half * sine_portion,
        ],
        axis=-1,
    )


def rms_scale(values):
    return lax.rsqrt(jnp.mean(values * values, axis=-1, keepdims=True) + EPS)


def outer_sum(left, right):
    return lax.dot_general(
        left, right, (((0,), (0,)), ((), ())), preferred_element_type=jnp.float32
    )


def backward_product(grad, weight):
    return lax.dot_general(
        grad, weight, (((1,), (1,)), ((), ())), preferred_element_type=jnp.float32
    )


def z_step(value, step):
    return lax.ppermute(value, "fsdp", [(i, (i + 2 * step) % 8) for i in range(8)])


def x_step(value, step):
    return lax.ppermute(value, "dp", [(i, (i + 2 * step) % 8) for i in range(8)])


def y_near(value):
    return lax.ppermute(value, "fsdp", [(i, i ^ 1) for i in range(8)])


def y_far(value):
    return lax.ppermute(value, "dp", [(i, i ^ 1) for i in range(8)])


def sibling(value):
    return lax.ppermute(value, "section", [(0, 1), (1, 0)])


def ring_gather(step, way, block):
    before = step(block, 1)
    after = step(block, -1)
    far = step(before if way == 1 else after, way)
    return [block, before, after, far]


def ring_sum(step, way, chunk, waits=((), ())):
    relayed = gate(step(chunk(2).astype(BF16), way), *waits[0])
    other = step(chunk(-way).astype(BF16), -way)
    nearer = (chunk(way).astype(F32) + relayed.astype(F32)).astype(BF16)
    total = chunk(0).astype(F32) + other.astype(F32) + step(nearer, way).astype(F32)
    return gate(total, *waits[1])


def direct_sum(step, chunk):
    total = chunk(0).astype(F32)
    for distance in (1, -1, 2):
        total = total + step(chunk(distance).astype(BF16), distance).astype(F32)
    return total


class Place:
    def __init__(self):
        self.section = lax.axis_index("section")
        self.shard = lax.axis_index("fsdp")
        dp = lax.axis_index("dp")
        self.z, self.y = self.shard // 2, self.shard % 2
        self.x = dp // 2
        self.first = self.section == 0
        self.near_shards = jnp.stack(
            [(self.z + d) % 4 * 2 + (self.y + near) % 2 for d in DISTANCES for near in (0, 1)]
        )
        row = lax.broadcasted_iota(jnp.int32, (WIDTH, SPREAD), 0)
        column = jnp.arange(SPREAD, dtype=jnp.int32)
        self.z_shard = jnp.repeat(self.near_shards, PADDED)
        self.by_z = (
            (row // PART == self.z_shard[None]) & (row % PART == (column % PADDED)[None])
        ).astype(BF16)
        quarters = jnp.repeat(jnp.stack([(self.x + d) % 4 for d in DISTANCES]), SPREAD // 4)
        shards = jnp.tile(jnp.repeat(self.near_shards, ROW_QUARTER), 4)
        inner = quarters * ROW_QUARTER + column % ROW_QUARTER
        self.by_x = ((row // PART == shards[None]) & (row % PART == inner[None])).astype(BF16)

    def role(self, zero, one):
        return jnp.where(self.first, zero, one)

    def roles(self, mine, other):
        return (jnp.where(self.first, mine, other), jnp.where(self.first, other, mine))


def spread(value, places):
    return jnp.dot(value, places, preferred_element_type=F32).astype(BF16)


def unspread(value, places):
    high = lax.reduce_precision(value, 8, 7)
    both = jnp.concatenate([high.astype(BF16), (value - high).astype(BF16)], axis=1)
    return backward_product(both, jnp.concatenate([places, places], axis=1))


def product(left, right):
    return jnp.dot(left, right, preferred_element_type=F32)


def gate(value, *others):
    late = False
    for other in others:
        corner = other[(-1,) * other.ndim]
        late = late | (corner != corner)
    return jax.tree.map(lambda part: jnp.where(late, jnp.zeros_like(part), part), value)


def ring_gather_both(step, block, near=None, waits=()):
    before, after = (step(block, 1), step(block, -1)) if near is None else near
    far = (step(gate(before[0], *waits), 1), step(gate(after[1], *waits), -1))
    layers = [[block[n], before[n], after[n], far[n]] for n in range(2)]
    return (layers, (before, after))


def gather_first(place, own, waits):
    own = gate(own, waits[0])
    other = y_near(own)
    pair = jnp.stack([own, other], axis=1).reshape(2, 2 * PADDED, UNIT)
    pair = gate(pair, waits[1])
    layers, unused = ring_gather_both(z_step, pair)
    return ([jnp.concatenate(blocks, axis=0) for blocks in layers], other)


def gather_down(place, own, start, waits):
    own = gate(own, start)
    other = y_near(own)
    low, high = (jnp.where(place.y == 0, own, other), jnp.where(place.y == 0, other, own))
    pair = jnp.stack([low, high], axis=1).reshape(2, 2 * FF_PART, DOWN_COLS)
    pair = gate(pair, *waits)
    layers, near = ring_gather_both(z_step, pair)
    wholes = []
    for blocks in layers:
        whole = jnp.zeros((4,) + pair.shape[1:], BF16)
        for distance, block in zip(DISTANCES, blocks):
            whole = lax.dynamic_update_slice_in_dim(
                whole, block[None], (place.z + distance) % 4, 0
            )
        wholes.append(whole.reshape(-1, DOWN_COLS))
    return (wholes, near)


def gather_wide(place, own):
    quarter = lax.dynamic_slice_in_dim(own, place.x * ROW_QUARTER, ROW_QUARTER, 1)
    other = y_near(quarter)
    pair = jnp.stack([quarter, other], axis=1)
    blocks = ring_gather(z_step, -1, pair)
    column = jnp.stack(blocks, axis=1)
    column = column.reshape(2, SPREAD // 4, 2 * UNIT)
    near = (x_step(column, 1), x_step(column, -1))
    return (column, near, (other, blocks[-1]))


def layer_weights(place, mine):
    one = (mine, sibling(mine))
    gains = one[0].reshape(8, PADDED, UNIT)[:, PART : PART + 2, :PADDED]
    gains = backward_product(gains.transpose(1, 0, 2).reshape(2, SPREAD), place.by_z)
    return (one, gains[:1], gains[1:])


def gather_rows(own):
    pair = jnp.concatenate([own, y_near(own)], axis=0)
    return jnp.concatenate(ring_gather(z_step, 1, pair), axis=0)


def scatter_rows(partial):
    parts = partial.reshape(4, -1, partial.shape[1])
    pair = ring_sum(z_step, -1, lambda distance: parts[DISTANCES.index(distance)])
    rows = pair.shape[0] // 2
    return pair[:rows] + y_near(pair[rows:].astype(BF16)).astype(F32)


def forward_layer(place, inputs, weights, fetch, waits, cosine_table, sine_portion, allowed):
    one, gain_one, gain_two = weights
    count_of_rows = inputs.shape[0]
    inv_one = rms_scale(inputs)
    normed_one = spread((inputs * inv_one * gain_one).astype(BF16), place.by_z)
    query_key, value_part = place.roles(product(normed_one, one[0]), product(normed_one, one[1]))
    value_part = value_part[:, WIDTH:].astype(BF16)
    turned = rotary_embedding(
        query_key.reshape(count_of_rows, QUERY_HEADS + KEY_VALUE_HEADS, HEAD_SIZE),
        cosine_table,
        sine_portion,
    ).astype(BF16)
    query_rows = turned[:, :QUERY_HEADS].reshape(
        count_of_rows, KEY_VALUE_HEADS, QUERY_HEADS // KEY_VALUE_HEADS, HEAD_SIZE
    )
    key_portion = turned[:, QUERY_HEADS:].reshape(count_of_rows, KV_WIDTH)
    key_value = gather_rows(jnp.concatenate([key_portion, value_part], axis=1))
    others, near = fetch(key_value)
    two, low = others[0]
    key_value = gate(key_value, *waits)
    key_row_block = key_value[:, :KV_WIDTH].reshape(-1, KEY_VALUE_HEADS, HEAD_SIZE)
    value_row_block = key_value[:, KV_WIDTH:].reshape(-1, KEY_VALUE_HEADS, HEAD_SIZE)
    scores = (
        jnp.einsum("qghd,kgd->ghqk", query_rows, key_row_block, preferred_element_type=F32)
        * SCALE
    )
    scores = jnp.where(allowed, scores, MASKED)
    row_max = jnp.max(scores, axis=-1, keepdims=True)
    exponent = jnp.exp(scores - row_max)
    total = jnp.sum(exponent, axis=-1, keepdims=True)
    attention = (exponent / total).astype(BF16)
    log_total = row_max + jnp.log(total)
    mixture = jnp.einsum(
        "ghqk,kgd->qghd", attention, value_row_block, preferred_element_type=F32
    )
    mixture = gate(mixture, *near)
    mixture = spread(
        mixture.astype(BF16).reshape(count_of_rows, QUERY_HEADS * HEAD_SIZE), place.by_z
    )
    unused, projected = place.roles(product(mixture, one[0]), product(mixture, one[1]))
    middle = inputs + projected[:, :WIDTH]
    inv_two = rms_scale(middle)
    normed_two = spread((middle * inv_two * gain_two).astype(BF16), place.by_x)
    gate_pre, up_pre = place.roles(product(normed_two, two[0]), product(normed_two, two[1]))
    hidden = (jax.nn.silu(gate_pre) * up_pre).astype(BF16)
    left, right = place.roles(product(hidden, low[0]), product(hidden, low[1]))
    result = middle + jnp.concatenate([left, right[:, DOWN_SKIP:]], axis=1)
    stored = (
        inputs,
        inv_one,
        normed_one,
        query_rows,
        key_row_block,
        value_row_block,
        log_total,
        mixture,
        middle,
        inv_two,
        normed_two,
        gate_pre,
        up_pre,
        hidden,
    )
    return (result, stored, others)


def with_sibling(own, sent):
    return jnp.concatenate([own, sibling(sent)], axis=0)


def norm_backward(grad, unit, inverse, gain):
    scaled = grad * gain
    return inverse * (scaled - unit * jnp.mean(scaled * unit, axis=-1, keepdims=True))


def partial_chunks(left, right):
    size = left.shape[1] // 4

    def chunk(distance):
        at = DISTANCES.index(distance)
        return outer_sum(left[:, at * size : (at + 1) * size], right).astype(BF16)

    return chunk


def by_quarter(place, block, rows):
    quarters = block.reshape(4, rows, block.shape[-1])

    def quarter(distance):
        return lax.dynamic_index_in_dim(quarters, (place.x + distance) % 4, 0, keepdims=False)

    return quarter


def reduce_first(left, right, waits):
    return ring_sum(z_step, 1, partial_chunks(left, right), waits)


def reduce_down(place, left, right):
    size = 2 * FF_PART

    def chunk(distance):
        part = lax.dynamic_slice_in_dim(left, (place.z + distance) % 4 * size, size, 1)
        return outer_sum(part, right).astype(BF16)

    pair = ring_sum(z_step, -1, chunk).astype(BF16)
    pair = pair.reshape(2, PADDED, UNIT)
    return jnp.concatenate(
        [
            lax.dynamic_index_in_dim(pair, place.y, 0, keepdims=False),
            lax.dynamic_index_in_dim(pair, 1 - place.y, 0, keepdims=False),
        ],
        axis=0,
    ).astype(F32)


def reduce_wide(left, right):
    chunk = partial_chunks(left, right)
    half = SPREAD // 8
    from_before = x_step(outer_sum(left[:, -2 * half : -half], right).astype(BF16), 1)
    from_after = x_step(outer_sum(left[:, -half:], right).astype(BF16), -1)
    after = chunk(1).astype(F32) + jnp.pad(from_before, ((0, half), (0, 0))).astype(F32)
    before = chunk(-1).astype(F32) + jnp.pad(from_after, ((half, 0), (0, 0))).astype(F32)
    column = (
        chunk(0).astype(F32)
        + x_step(after.astype(BF16), 1).astype(F32)
        + x_step(before.astype(BF16), -1).astype(F32)
    )
    parts = column.reshape(4, 2 * ROW_QUARTER, 2 * UNIT)
    pair = ring_sum(z_step, 1, lambda distance: parts[DISTANCES.index(distance)])
    quarter = pair[:ROW_QUARTER] + y_near(pair[ROW_QUARTER:].astype(BF16)).astype(F32)
    return ((from_before, from_after), column, quarter)


def across_y(pair):
    return pair[:PADDED] + y_near(pair[PADDED:].astype(BF16)).astype(F32)


def across_x(place, block):
    return direct_sum(x_step, by_quarter(place, block, ROW_QUARTER))


def across_far(quarter):
    low = quarter.astype(BF16)
    return (low.astype(F32) + y_far(low).astype(F32)).astype(BF16)


def all_quarters(place, piece):
    whole = jnp.zeros((4,) + piece.shape, BF16)
    for distance in DISTANCES:
        block = step_from(piece, distance)
        whole = lax.dynamic_update_slice_in_dim(
            whole, block[None], (place.x + distance) % 4, 0
        )
    return whole.reshape(-1, piece.shape[-1])


def step_from(piece, distance):
    return piece if distance == 0 else x_step(piece, -distance)


def backward_layer(
    place, grad_out, weights, others, stored, waits, before, cosine_table, sine_portion, allowed
):
    one, gain_one, gain_two = weights
    two, low = others
    (
        inputs,
        inv_one,
        normed_one,
        query_rows,
        key_row_block,
        value_row_block,
        log_total,
        mixture,
        middle,
        inv_two,
        normed_two,
        gate_pre,
        up_pre,
        hidden,
    ) = stored
    count_of_rows = grad_out.shape[0]
    grad_low = grad_out.astype(BF16)
    left_low = grad_low[:, :DOWN_COLS]
    right_low = grad_low[:, WIDTH - DOWN_COLS :]
    right_once = jnp.where(jnp.arange(DOWN_COLS)[None] < DOWN_SKIP, 0, right_low)
    mine_low, other_low = place.roles(left_low, right_once)
    hidden_grad = backward_product(mine_low, low[0]) + backward_product(other_low, low[1])
    sigmoid_gate = jax.nn.sigmoid(gate_pre)
    grad_gate = (
        hidden_grad * up_pre * sigmoid_gate * (1.0 + gate_pre * (1.0 - sigmoid_gate))
    ).astype(BF16)
    grad_up = (hidden_grad * gate_pre * sigmoid_gate).astype(BF16)
    mine, other = place.roles(grad_gate, grad_up)
    spread_two = backward_product(mine, two[0]) + backward_product(other, two[1])
    left_rows = with_sibling(*2 * (jnp.concatenate([hidden, normed_two], axis=1),))
    right_rows = with_sibling(
        jnp.concatenate([place.role(left_low, right_low), mine], axis=1),
        jnp.concatenate([place.role(right_low, left_low), other], axis=1),
    )
    down = reduce_down(place, left_rows[:, : 2 * UNIT], right_rows[:, :DOWN_COLS])
    wide = reduce_wide(left_rows[:, 2 * UNIT :], right_rows[:, DOWN_COLS:])
    grad_normed_two = unspread(spread_two, place.by_x)
    unit_two = middle * inv_two
    grad_gain_two = jnp.sum(grad_normed_two * unit_two, axis=0)
    grad_normed_two = gate(grad_normed_two, *waits)
    grad_mid = grad_out + norm_backward(grad_normed_two, unit_two, inv_two, gain_two)
    none_narrow = jnp.zeros((count_of_rows, KV_WIDTH), BF16)
    output_side = jnp.concatenate([grad_mid.astype(BF16), none_narrow], axis=1)
    none = jnp.zeros_like(output_side)
    mine, other = place.roles(none, output_side)
    grad_mixture = (
        unspread(backward_product(mine, one[0]) + backward_product(other, one[1]), place.by_z)
        .astype(BF16)
        .reshape(count_of_rows, KEY_VALUE_HEADS, QUERY_HEADS // KEY_VALUE_HEADS, HEAD_SIZE)
    )
    scores = (
        jnp.einsum("qghd,kgd->ghqk", query_rows, key_row_block, preferred_element_type=F32)
        * SCALE
    )
    scores = jnp.where(allowed, scores, MASKED)
    attention_full = jnp.exp(scores - log_total)
    attention = attention_full.astype(BF16)
    value_gradient = jnp.einsum(
        "ghqk,qghd->kgd", attention, grad_mixture, preferred_element_type=F32
    )
    grad_attention = jnp.einsum(
        "qghd,kgd->ghqk", grad_mixture, value_row_block, preferred_element_type=F32
    )
    row_dots = jnp.sum(attention_full * grad_attention, axis=-1, keepdims=True)
    far, column, wide = wide
    early = None
    if before:
        early = across_y(jnp.concatenate(before[:2], axis=1))
        far = far + (early,)
    row_dots = gate(row_dots, *far)
    grad_scores = (attention_full * (grad_attention - row_dots)).astype(BF16)
    key_gradient = (
        jnp.einsum("ghqk,qghd->kgd", grad_scores, query_rows, preferred_element_type=F32)
        * SCALE
    )
    key_value = scatter_rows(
        jnp.concatenate(
            [key_gradient.reshape(-1, KV_WIDTH), value_gradient.reshape(-1, KV_WIDTH)], axis=1
        ).astype(BF16)
    )
    grad_queries = (
        jnp.einsum("ghqk,kgd->qghd", grad_scores, key_row_block, preferred_element_type=F32)
        * SCALE
    )
    key_value = gate(key_value, column, down)
    if before:
        early = across_x(place, early)
        key_value = gate(key_value, early)
        piece = jnp.concatenate([early, before[2]], axis=1).astype(BF16)
        pieces = lax.all_gather(piece, "dp").astype(F32)
        early = (pieces[0::2] + pieces[1::2]).astype(BF16).reshape(-1, piece.shape[-1])
    key_gradient, value_low = (key_value[:, :KV_WIDTH], key_value[:, KV_WIDTH:].astype(BF16))
    grad_query_key = rotary_embedding_backward(
        jnp.concatenate(
            [
                grad_queries.reshape(count_of_rows, QUERY_HEADS, HEAD_SIZE),
                key_gradient.reshape(count_of_rows, KEY_VALUE_HEADS, HEAD_SIZE),
            ],
            axis=1,
        ),
        cosine_table,
        sine_portion,
    )
    grad_query_key = grad_query_key.reshape(count_of_rows, UNIT).astype(BF16)
    value_side = jnp.concatenate([jnp.zeros((count_of_rows, WIDTH), BF16), value_low], axis=1)
    mine, other = place.roles(grad_query_key, value_side)
    grad_normed = unspread(
        backward_product(mine, one[0]) + backward_product(other, one[1]), place.by_z
    )
    unit_one = inputs * inv_one
    grad_gain_one = jnp.sum(grad_normed * unit_one, axis=0)
    grad_in = grad_mid + norm_backward(grad_normed, unit_one, inv_one, gain_one)
    gain_rows = jnp.stack([grad_gain_one.reshape(8, PART), grad_gain_two.reshape(8, PART)], axis=1)
    gain_rows = jnp.pad(gain_rows.reshape(16, PART).astype(BF16), ((0, 0), (0, UNIT - PART)))
    number = jnp.arange(16, dtype=jnp.int32)[:, None]
    inner = (jnp.arange(SPREAD, dtype=jnp.int32) % PADDED)[None]
    gain_place = (number // 2 == place.z_shard[None]) & (PART + number % 2 == inner)
    left_rows = with_sibling(
        jnp.concatenate([place.role(normed_one, mixture), normed_one], axis=1),
        jnp.concatenate([place.role(mixture, normed_one), normed_one], axis=1),
    )
    right_rows = with_sibling(
        jnp.concatenate([place.role(grad_query_key, output_side), place.role(none, value_side)], 1),
        jnp.concatenate([place.role(output_side, grad_query_key), place.role(value_side, none)], 1),
    )
    waits = ((), ())
    if before:
        down = across_x(place, across_y(down))
        waits = ((down,), ())
    left_rows = jnp.concatenate(
        [left_rows[:, :SPREAD], left_rows[:, SPREAD:], gain_place.astype(BF16)], axis=0
    )
    right_rows = jnp.concatenate([right_rows[:, :UNIT], right_rows[:, UNIT:], gain_rows], axis=0)
    return (
        grad_in,
        (reduce_first(left_rows, right_rows, waits), down, wide),
        early,
    )


def per_device(
    boundary,
    lengths,
    query_weight,
    key_matrix,
    value_matrix,
    output_weight,
    gate_weight,
    up_weight,
    down_weight,
    first_gain,
    second_gain,
):
    place = Place()
    first = place.first
    slab = boundary[0, :, 0]
    rows_dev = slab.shape[1]
    exchanged = sibling(jnp.where(first, slab[1], slab[0]))
    inputs = jnp.where(first, slab[0], exchanged).astype(F32)
    cotangent = jnp.where(first, exchanged, slab[1]).astype(F32)

    gains = jnp.pad(
        jnp.concatenate([first_gain, second_gain], axis=0), ((0, 6), (0, UNIT - PART))
    )
    role_packs = (
        (
            jnp.concatenate(
                [jnp.concatenate([query_weight[0], key_matrix[0]], axis=1), gains], axis=0
            ),
            jnp.pad(gate_weight[0], ((0, PADDED - PART), (0, 0))),
            down_weight[0, :, :DOWN_COLS],
        ),
        (
            jnp.concatenate(
                [jnp.concatenate([output_weight[0], value_matrix[0]], axis=1), gains], axis=0
            ),
            jnp.pad(up_weight[0], ((0, PADDED - PART), (0, 0))),
            down_weight[0, :, WIDTH - DOWN_COLS :],
        ),
    )
    layer_packs = ([], [])
    for zero, one in zip(*role_packs):
        kept = jnp.where(first, zero, one)
        other = sibling(jnp.where(first, one, zero))
        layer_packs[0].append(jnp.where(first, kept, other))
        layer_packs[1].append(jnp.where(first, other, kept))
    first_pack, wide_pack, down_pack = [jnp.stack(both) for both in zip(*layer_packs)]
    column, near_wide, started = gather_wide(place, wide_pack)
    one, other = gather_first(place, first_pack, started)
    weights_first, weights_second = [layer_weights(place, mine) for mine in one]

    seq_lengths = jnp.where(first, lengths[0, 0], lengths[0, 1])
    inner = jnp.arange(rows_dev, dtype=jnp.int32)
    own_rows = place.shard * rows_dev + inner
    all_rows = (place.near_shards[:, None] * rows_dev + inner[None]).reshape(-1)
    segment_mine, position_mine = segment_rows(seq_lengths, own_rows)
    segment_all, unused_position = segment_rows(seq_lengths, all_rows)
    allowed = (segment_mine[:, None] == segment_all[None, :]) & (
        own_rows[:, None] >= all_rows[None, :]
    )
    cosine_table, sine_portion = rotary_tables(position_mine)
    live_rows = (segment_mine < seq_lengths.shape[0]).astype(F32)

    geometry = (cosine_table, sine_portion, allowed)
    def fetch(key_value):
        layers, unused = ring_gather_both(x_step, column, near_wide, (key_value,))
        wide = [jnp.concatenate(blocks, axis=0) for blocks in layers]
        wholes, near = gather_down(place, down_pack, other, (key_value,))
        return ([[(value, sibling(value)) for value in pair] for pair in zip(wide, wholes)], near)

    middle, stored_first, others = forward_layer(
        place, inputs, weights_first, fetch, near_wide, *geometry
    )
    middle = middle.astype(BF16).astype(F32)
    result, stored_second, unused = forward_layer(
        place, middle, weights_second, lambda key_value: (others[1:], ()), (), *geometry
    )
    grad, (pair, down, wide), unused = backward_layer(
        place,
        cotangent * live_rows[:, None],
        weights_second,
        others[1],
        stored_second,
        (),
        [],
        *geometry,
    )
    grad = grad.astype(BF16).astype(F32)
    grad, (last, down_first, wide_first), early = backward_layer(
        place,
        grad,
        weights_first,
        others[0],
        stored_first,
        (pair, wide),
        [pair, down, wide],
        *geometry,
    )

    ends = (grad.astype(BF16), result.astype(BF16))
    received = sibling(jnp.where(first, ends[1], ends[0]))
    boundary_out = jnp.where(
        first, jnp.stack([ends[0], received]), jnp.stack([received, ends[1]])
    )[None, :, None]

    late = across_x(place, across_y(last))
    late = jnp.concatenate([late, down_first, wide_first], axis=1)
    late = all_quarters(place, across_far(late))
    late_first, early_first = (late[:, :UNIT], late[:, UNIT:])
    late_second, early_second = (early[:, :UNIT], early[:, UNIT:])
    sums = []
    for for_first, for_second in ((early_first, early_second), (late_first, late_second)):
        own = jnp.where(first, for_first, for_second)
        other = sibling(jnp.where(first, for_second, for_first))
        sums.append([value.astype(F32) for value in place.roles(own, other)])
    down_left, down_right = [value[:, :UNIT].reshape(FF_PART, DOWN_COLS) for value in sums[0]]
    gate_sum, up_sum = [value[:, UNIT:] for value in sums[0]]
    query_key, output_value = sums[1]
    gain_sums = query_key[PART : PART + 2, :PART] + output_value[PART : PART + 2, :PART]
    return (
        boundary_out,
        query_key[None, :PART, :WIDTH],
        query_key[None, :PART, WIDTH:],
        output_value[None, :PART, WIDTH:],
        output_value[None, :PART, :WIDTH],
        gate_sum[None, :PART],
        up_sum[None, :PART],
        jnp.concatenate([down_left, down_right[:, DOWN_SKIP:]], axis=1)[None],
        gain_sums[:1],
        gain_sums[1:],
    )


def solution(mesh):
    placed = (
        P("section", None, "dp", "fsdp", None),
        P("dp", None, None),
        P("section", "fsdp", None),
        P("section", "fsdp", None),
        P("section", "fsdp", None),
        P("section", "fsdp", None),
        P("section", "fsdp", None),
        P("section", "fsdp", None),
        P("section", "fsdp", None),
        P("section", "fsdp"),
        P("section", "fsdp"),
    )
    return jax.shard_map(
        per_device,
        mesh=mesh,
        in_specs=placed,
        out_specs=(
            P("section", None, "dp", "fsdp", None),
            P("section", "fsdp", None),
            P("section", "fsdp", None),
            P("section", "fsdp", None),
            P("section", "fsdp", None),
            P("section", "fsdp", None),
            P("section", "fsdp", None),
            P("section", "fsdp", None),
            P("section", "fsdp"),
            P("section", "fsdp"),
        ),
        check_vma=False,
    )
```

```python
import jax
import jax.numpy as jnp
from jax import lax
from jax.sharding import PartitionSpec as P

QUERY_HEADS = 15
KEY_VALUE_HEADS = 5
HEAD_SIZE = 64


EPS = 1e-05
SCALE = 0.125
MASKED = -1e30


BF16 = jnp.bfloat16
F32 = jnp.float32
WIDTH = 960
PART = 120
PADDED = 128
SPREAD = 1024
UNIT = 1280
FF_PART = 320
FF_QUARTER = 80
DOWN_COLS = 512
DOWN_SKIP = 64
ROW_QUARTER = 32
KV_WIDTH = KEY_VALUE_HEADS * HEAD_SIZE
DISTANCES = (0, -1, 1, 2)


def segment_rows(seq_lengths, row_index):
    seq_ends = jnp.cumsum(seq_lengths)
    starts = seq_ends - seq_lengths
    segment = jnp.sum((row_index[:, None] >= seq_ends[None, :]).astype(jnp.int32), axis=1)
    slot_ids = jnp.arange(seq_lengths.shape[0], dtype=jnp.int32)
    row_start = jnp.sum(
        jnp.where(segment[:, None] == slot_ids[None, :], starts[None, :], 0), axis=1
    )
    return (segment, row_index - row_start)


def rotary_tables(position):
    frequency = 10000.0 ** (-2.0 * jnp.arange(HEAD_SIZE // 2, dtype=jnp.float32) / HEAD_SIZE)
    angles = position.astype(jnp.float32)[:, None] * frequency[None, :]
    return (jnp.cos(angles)[:, None, :], jnp.sin(angles)[:, None, :])


def rotary_embedding(vector, cosine_table, sine_portion):
    first_half = vector[..., : HEAD_SIZE // 2]
    second_half = vector[..., HEAD_SIZE // 2 :]
    return jnp.concatenate(
        [
            first_half * cosine_table - second_half * sine_portion,
            second_half * cosine_table + first_half * sine_portion,
        ],
        axis=-1,
    )


def rotary_embedding_backward(grad, cosine_table, sine_portion):
    first_half = grad[..., : HEAD_SIZE // 2]
    second_half = grad[..., HEAD_SIZE // 2 :]
    return jnp.concatenate(
        [
            first_half * cosine_table + second_half * sine_portion,
            second_half * cosine_table - first_half * sine_portion,
        ],
        axis=-1,
    )


def rms_scale(values):
    return lax.rsqrt(jnp.mean(values * values, axis=-1, keepdims=True) + EPS)


def outer_sum(left, right):
    return lax.dot_general(
        left, right, (((0,), (0,)), ((), ())), preferred_element_type=jnp.float32
    )


def backward_product(grad, weight):
    return lax.dot_general(
        grad, weight, (((1,), (1,)), ((), ())), preferred_element_type=jnp.float32
    )


def z_step(value, step):
    return lax.ppermute(value, "fsdp", [(i, (i + 2 * step) % 8) for i in range(8)])


def x_step(value, step):
    return lax.ppermute(value, "dp", [(i, (i + 2 * step) % 8) for i in range(8)])


def y_near(value):
    return lax.ppermute(value, "fsdp", [(i, i ^ 1) for i in range(8)])


def y_far(value):
    return lax.ppermute(value, "dp", [(i, i ^ 1) for i in range(8)])


def sibling(value):
    return lax.ppermute(value, "section", [(0, 1), (1, 0)])


def ring_gather(step, way, block):
    before = step(block, 1)
    after = step(block, -1)
    far = step(before if way == 1 else after, way)
    return [block, before, after, far]


def ring_sum(step, way, chunk, waits=((), ())):
    relayed = gate(step(chunk(2).astype(BF16), way), *waits[0])
    other = step(chunk(-way).astype(BF16), -way)
    nearer = (chunk(way).astype(F32) + relayed.astype(F32)).astype(BF16)
    total = chunk(0).astype(F32) + other.astype(F32) + step(nearer, way).astype(F32)
    return gate(total, *waits[1])


def direct_sum(step, chunk):
    total = chunk(0).astype(F32)
    for distance in (1, -1, 2):
        total = total + step(chunk(distance).astype(BF16), distance).astype(F32)
    return total


class Place:
    def __init__(self):
        self.section = lax.axis_index("section")
        self.shard = lax.axis_index("fsdp")
        dp = lax.axis_index("dp")
        self.z, self.y = self.shard // 2, self.shard % 2
        self.x = dp // 2
        self.first = self.section == 0
        self.near_shards = jnp.stack(
            [(self.z + d) % 4 * 2 + (self.y + near) % 2 for d in DISTANCES for near in (0, 1)]
        )
        row = lax.broadcasted_iota(jnp.int32, (WIDTH, SPREAD), 0)
        column = jnp.arange(SPREAD, dtype=jnp.int32)
        self.z_shard = jnp.repeat(self.near_shards, PADDED)
        self.by_z = (
            (row // PART == self.z_shard[None]) & (row % PART == (column % PADDED)[None])
        ).astype(BF16)
        quarters = jnp.repeat(jnp.stack([(self.x + d) % 4 for d in DISTANCES]), SPREAD // 4)
        shards = jnp.tile(jnp.repeat(self.near_shards, ROW_QUARTER), 4)
        inner = quarters * ROW_QUARTER + column % ROW_QUARTER
        self.by_x = ((row // PART == shards[None]) & (row % PART == inner[None])).astype(BF16)

    def role(self, zero, one):
        return jnp.where(self.first, zero, one)

    def roles(self, mine, other):
        return (jnp.where(self.first, mine, other), jnp.where(self.first, other, mine))


def spread(value, places):
    return jnp.dot(value, places, preferred_element_type=F32).astype(BF16)


def unspread(value, places):
    high = lax.reduce_precision(value, 8, 7)
    both = jnp.concatenate([high.astype(BF16), (value - high).astype(BF16)], axis=1)
    return backward_product(both, jnp.concatenate([places, places], axis=1))


def product(left, right):
    return jnp.dot(left, right, preferred_element_type=F32)


def gate(value, *others):
    late = False
    for other in others:
        corner = other[(-1,) * other.ndim]
        late = late | (corner != corner)
    return jax.tree.map(lambda part: jnp.where(late, jnp.zeros_like(part), part), value)


def ring_gather_both(step, block, near=None, waits=()):
    before, after = (step(block, 1), step(block, -1)) if near is None else near
    far = (step(gate(before[0], *waits), 1), step(gate(after[1], *waits), -1))
    layers = [[block[n], before[n], after[n], far[n]] for n in range(2)]
    return (layers, (before, after))


def gather_first(place, own, waits):
    own = gate(own, waits[0])
    other = y_near(own)
    pair = jnp.stack([own, other], axis=1).reshape(2, 2 * PADDED, UNIT)
    pair = gate(pair, *waits[1:])
    layers, unused = ring_gather_both(z_step, pair)
    return ([jnp.concatenate(blocks, axis=0) for blocks in layers], other)


def gather_down(place, own, start, waits):
    own = gate(own, start)
    other = y_near(own)
    low, high = (jnp.where(place.y == 0, own, other), jnp.where(place.y == 0, other, own))
    pair = jnp.stack([low, high], axis=1).reshape(2, 2 * FF_PART, DOWN_COLS)
    pair = gate(pair, *waits)
    layers, near = ring_gather_both(z_step, pair)
    wholes = []
    for blocks in layers:
        whole = jnp.zeros((4,) + pair.shape[1:], BF16)
        for distance, block in zip(DISTANCES, blocks):
            whole = lax.dynamic_update_slice_in_dim(
                whole, block[None], (place.z + distance) % 4, 0
            )
        wholes.append(whole.reshape(-1, DOWN_COLS))
    return (wholes, near)


def gather_wide(place, own):
    quarter = lax.dynamic_slice_in_dim(own, place.x * ROW_QUARTER, ROW_QUARTER, 1)
    other = y_near(quarter)
    pair = jnp.stack([quarter, other], axis=1)
    blocks = ring_gather(z_step, -1, pair)
    column = jnp.stack(blocks, axis=1)
    column = column.reshape(2, SPREAD // 4, 2 * UNIT)
    near = (x_step(column, 1), x_step(column, -1))
    return (column, near, (other, blocks[1], blocks[-1]))


def layer_weights(place, mine):
    one = (mine, sibling(mine))
    gains = one[0].reshape(8, PADDED, UNIT)[:, PART : PART + 2, :PADDED]
    gains = backward_product(gains.transpose(1, 0, 2).reshape(2, SPREAD), place.by_z)
    return (one, gains[:1], gains[1:])


def gather_rows(own):
    other = y_near(own)
    pair = jnp.concatenate([own, other], axis=0)
    return (jnp.concatenate(ring_gather(z_step, 1, pair), axis=0), other)


def scatter_rows(partial):
    parts = partial.reshape(4, -1, partial.shape[1])
    pair = ring_sum(z_step, -1, lambda distance: parts[DISTANCES.index(distance)])
    rows = pair.shape[0] // 2
    return pair[:rows] + y_near(pair[rows:].astype(BF16)).astype(F32)


def forward_layer(place, inputs, weights, fetch, waits, cosine_table, sine_portion, allowed):
    one, gain_one, gain_two = weights
    count_of_rows = inputs.shape[0]
    inv_one = rms_scale(inputs)
    normed_one = spread((inputs * inv_one * gain_one).astype(BF16), place.by_z)
    query_key, value_part = place.roles(product(normed_one, one[0]), product(normed_one, one[1]))
    value_part = value_part[:, WIDTH:].astype(BF16)
    turned = rotary_embedding(
        query_key.reshape(count_of_rows, QUERY_HEADS + KEY_VALUE_HEADS, HEAD_SIZE),
        cosine_table,
        sine_portion,
    ).astype(BF16)
    query_rows = turned[:, :QUERY_HEADS].reshape(
        count_of_rows, KEY_VALUE_HEADS, QUERY_HEADS // KEY_VALUE_HEADS, HEAD_SIZE
    )
    key_portion = turned[:, QUERY_HEADS:].reshape(count_of_rows, KV_WIDTH)
    key_value, near_rows = gather_rows(jnp.concatenate([key_portion, value_part], axis=1))
    others, near = fetch(key_value, near_rows)
    two, low = others[0]
    key_value = gate(key_value, *waits)
    key_row_block = key_value[:, :KV_WIDTH].reshape(-1, KEY_VALUE_HEADS, HEAD_SIZE)
    value_row_block = key_value[:, KV_WIDTH:].reshape(-1, KEY_VALUE_HEADS, HEAD_SIZE)
    scores = (
        jnp.einsum("qghd,kgd->ghqk", query_rows, key_row_block, preferred_element_type=F32)
        * SCALE
    )
    scores = jnp.where(allowed, scores, MASKED)
    row_max = jnp.max(scores, axis=-1, keepdims=True)
    exponent = jnp.exp(scores - row_max)
    total = jnp.sum(exponent, axis=-1, keepdims=True)
    attention = (exponent / total).astype(BF16)
    log_total = row_max + jnp.log(total)
    mixture = jnp.einsum(
        "ghqk,kgd->qghd", attention, value_row_block, preferred_element_type=F32
    )
    mixture = gate(mixture, *near)
    mixture = spread(
        mixture.astype(BF16).reshape(count_of_rows, QUERY_HEADS * HEAD_SIZE), place.by_z
    )
    unused, projected = place.roles(product(mixture, one[0]), product(mixture, one[1]))
    middle = inputs + projected[:, :WIDTH]
    inv_two = rms_scale(middle)
    normed_two = spread((middle * inv_two * gain_two).astype(BF16), place.by_x)
    gate_pre, up_pre = place.roles(product(normed_two, two[0]), product(normed_two, two[1]))
    hidden = (jax.nn.silu(gate_pre) * up_pre).astype(BF16)
    left, right = place.roles(product(hidden, low[0]), product(hidden, low[1]))
    result = middle + jnp.concatenate([left, right[:, DOWN_SKIP:]], axis=1)
    stored = (
        inputs,
        inv_one,
        normed_one,
        query_rows,
        key_row_block,
        value_row_block,
        log_total,
        mixture,
        middle,
        inv_two,
        normed_two,
        gate_pre,
        up_pre,
        hidden,
    )
    return (result, stored, others)


def with_sibling(own, sent):
    return jnp.concatenate([own, sibling(sent)], axis=0)


def norm_backward(grad, unit, inverse, gain):
    scaled = grad * gain
    return inverse * (scaled - unit * jnp.mean(scaled * unit, axis=-1, keepdims=True))


def partial_chunks(left, right):
    size = left.shape[1] // 4

    def chunk(distance):
        at = DISTANCES.index(distance)
        return outer_sum(left[:, at * size : (at + 1) * size], right).astype(BF16)

    return chunk


def by_quarter(place, block, rows):
    quarters = block.reshape(4, rows, block.shape[-1])

    def quarter(distance):
        return lax.dynamic_index_in_dim(quarters, (place.x + distance) % 4, 0, keepdims=False)

    return quarter


def reduce_first(left, right, waits):
    return ring_sum(z_step, 1, partial_chunks(left, right), waits)


def reduce_down(place, left, right):
    size = 2 * FF_PART

    def chunk(distance):
        part = lax.dynamic_slice_in_dim(left, (place.z + distance) % 4 * size, size, 1)
        return outer_sum(part, right).astype(BF16)

    pair = ring_sum(z_step, -1, chunk).astype(BF16)
    pair = pair.reshape(2, PADDED, UNIT)
    return jnp.concatenate(
        [
            lax.dynamic_index_in_dim(pair, place.y, 0, keepdims=False),
            lax.dynamic_index_in_dim(pair, 1 - place.y, 0, keepdims=False),
        ],
        axis=0,
    ).astype(F32)


def reduce_wide(left, right):
    chunk = partial_chunks(left, right)
    half = SPREAD // 8
    from_before = x_step(outer_sum(left[:, -2 * half : -half], right).astype(BF16), 1)
    from_after = x_step(outer_sum(left[:, -half:], right).astype(BF16), -1)
    after = chunk(1).astype(F32) + jnp.pad(from_before, ((0, half), (0, 0))).astype(F32)
    before = chunk(-1).astype(F32) + jnp.pad(from_after, ((half, 0), (0, 0))).astype(F32)
    column = (
        chunk(0).astype(F32)
        + x_step(after.astype(BF16), 1).astype(F32)
        + x_step(before.astype(BF16), -1).astype(F32)
    )
    parts = column.reshape(4, 2 * ROW_QUARTER, 2 * UNIT)
    pair = ring_sum(z_step, 1, lambda distance: parts[DISTANCES.index(distance)])
    quarter = pair[:ROW_QUARTER] + y_near(pair[ROW_QUARTER:].astype(BF16)).astype(F32)
    return ((from_before, from_after), column, quarter)


def across_y(pair):
    return pair[:PADDED] + y_near(pair[PADDED:].astype(BF16)).astype(F32)


def across_x(place, block):
    return direct_sum(x_step, by_quarter(place, block, ROW_QUARTER))


def across_far(quarter):
    low = quarter.astype(BF16)
    return (low.astype(F32) + y_far(low).astype(F32)).astype(BF16)


def all_quarters(place, piece):
    whole = jnp.zeros((4,) + piece.shape, BF16)
    for distance in DISTANCES:
        block = step_from(piece, distance)
        whole = lax.dynamic_update_slice_in_dim(
            whole, block[None], (place.x + distance) % 4, 0
        )
    return whole.reshape(-1, piece.shape[-1])


def step_from(piece, distance):
    return piece if distance == 0 else x_step(piece, -distance)


def backward_layer(
    place, grad_out, weights, others, stored, waits, before, cosine_table, sine_portion, allowed
):
    one, gain_one, gain_two = weights
    two, low = others
    (
        inputs,
        inv_one,
        normed_one,
        query_rows,
        key_row_block,
        value_row_block,
        log_total,
        mixture,
        middle,
        inv_two,
        normed_two,
        gate_pre,
        up_pre,
        hidden,
    ) = stored
    count_of_rows = grad_out.shape[0]
    grad_low = grad_out.astype(BF16)
    left_low = grad_low[:, :DOWN_COLS]
    right_low = grad_low[:, WIDTH - DOWN_COLS :]
    right_once = jnp.where(jnp.arange(DOWN_COLS)[None] < DOWN_SKIP, 0, right_low)
    mine_low, other_low = place.roles(left_low, right_once)
    hidden_grad = backward_product(mine_low, low[0]) + backward_product(other_low, low[1])
    sigmoid_gate = jax.nn.sigmoid(gate_pre)
    grad_gate = (
        hidden_grad * up_pre * sigmoid_gate * (1.0 + gate_pre * (1.0 - sigmoid_gate))
    ).astype(BF16)
    grad_up = (hidden_grad * gate_pre * sigmoid_gate).astype(BF16)
    mine, other = place.roles(grad_gate, grad_up)
    spread_two = backward_product(mine, two[0]) + backward_product(other, two[1])
    left_rows = with_sibling(*2 * (jnp.concatenate([hidden, normed_two], axis=1),))
    right_rows = with_sibling(
        jnp.concatenate([place.role(left_low, right_low), mine], axis=1),
        jnp.concatenate([place.role(right_low, left_low), other], axis=1),
    )
    down = reduce_down(place, left_rows[:, : 2 * UNIT], right_rows[:, :DOWN_COLS])
    wide = reduce_wide(left_rows[:, 2 * UNIT :], right_rows[:, DOWN_COLS:])
    grad_normed_two = unspread(spread_two, place.by_x)
    unit_two = middle * inv_two
    grad_gain_two = jnp.sum(grad_normed_two * unit_two, axis=0)
    grad_normed_two = gate(grad_normed_two, *waits)
    grad_mid = grad_out + norm_backward(grad_normed_two, unit_two, inv_two, gain_two)
    none_narrow = jnp.zeros((count_of_rows, KV_WIDTH), BF16)
    output_side = jnp.concatenate([grad_mid.astype(BF16), none_narrow], axis=1)
    none = jnp.zeros_like(output_side)
    mine, other = place.roles(none, output_side)
    grad_mixture = (
        unspread(backward_product(mine, one[0]) + backward_product(other, one[1]), place.by_z)
        .astype(BF16)
        .reshape(count_of_rows, KEY_VALUE_HEADS, QUERY_HEADS // KEY_VALUE_HEADS, HEAD_SIZE)
    )
    scores = (
        jnp.einsum("qghd,kgd->ghqk", query_rows, key_row_block, preferred_element_type=F32)
        * SCALE
    )
    scores = jnp.where(allowed, scores, MASKED)
    attention_full = jnp.exp(scores - log_total)
    attention = attention_full.astype(BF16)
    value_gradient = jnp.einsum(
        "ghqk,qghd->kgd", attention, grad_mixture, preferred_element_type=F32
    )
    grad_attention = jnp.einsum(
        "qghd,kgd->ghqk", grad_mixture, value_row_block, preferred_element_type=F32
    )
    row_dots = jnp.sum(attention_full * grad_attention, axis=-1, keepdims=True)
    far, column, wide = wide
    row_dots = gate(row_dots, *far)
    grad_scores = (attention_full * (grad_attention - row_dots)).astype(BF16)
    key_gradient = (
        jnp.einsum("ghqk,qghd->kgd", grad_scores, query_rows, preferred_element_type=F32)
        * SCALE
    )
    key_value = scatter_rows(
        jnp.concatenate(
            [key_gradient.reshape(-1, KV_WIDTH), value_gradient.reshape(-1, KV_WIDTH)], axis=1
        ).astype(BF16)
    )
    grad_queries = (
        jnp.einsum("ghqk,kgd->qghd", grad_scores, key_row_block, preferred_element_type=F32)
        * SCALE
    )
    key_value = gate(key_value, column, down)
    early = None
    if before:
        early = across_y(jnp.concatenate(before[:2] + [down], axis=1))
    key_gradient, value_low = (key_value[:, :KV_WIDTH], key_value[:, KV_WIDTH:].astype(BF16))
    grad_query_key = rotary_embedding_backward(
        jnp.concatenate(
            [
                grad_queries.reshape(count_of_rows, QUERY_HEADS, HEAD_SIZE),
                key_gradient.reshape(count_of_rows, KEY_VALUE_HEADS, HEAD_SIZE),
            ],
            axis=1,
        ),
        cosine_table,
        sine_portion,
    )
    grad_query_key = grad_query_key.reshape(count_of_rows, UNIT).astype(BF16)
    value_side = jnp.concatenate([jnp.zeros((count_of_rows, WIDTH), BF16), value_low], axis=1)
    mine, other = place.roles(grad_query_key, value_side)
    grad_normed = unspread(
        backward_product(mine, one[0]) + backward_product(other, one[1]), place.by_z
    )
    unit_one = inputs * inv_one
    grad_gain_one = jnp.sum(grad_normed * unit_one, axis=0)
    grad_in = grad_mid + norm_backward(grad_normed, unit_one, inv_one, gain_one)
    gain_rows = jnp.stack([grad_gain_one.reshape(8, PART), grad_gain_two.reshape(8, PART)], axis=1)
    gain_rows = jnp.pad(gain_rows.reshape(16, PART).astype(BF16), ((0, 0), (0, UNIT - PART)))
    number = jnp.arange(16, dtype=jnp.int32)[:, None]
    inner = (jnp.arange(SPREAD, dtype=jnp.int32) % PADDED)[None]
    gain_place = (number // 2 == place.z_shard[None]) & (PART + number % 2 == inner)
    left_rows = with_sibling(
        jnp.concatenate([place.role(normed_one, mixture), normed_one], axis=1),
        jnp.concatenate([place.role(mixture, normed_one), normed_one], axis=1),
    )
    right_rows = with_sibling(
        jnp.concatenate([place.role(grad_query_key, output_side), place.role(none, value_side)], 1),
        jnp.concatenate([place.role(output_side, grad_query_key), place.role(value_side, none)], 1),
    )
    waits = ((), ())
    if before:
        left_rows = gate(left_rows, early, wide)
        early = across_x(place, early)
        piece = across_far(jnp.concatenate([early, before[2]], axis=1))
        early = all_quarters(place, piece)
    left_rows = jnp.concatenate(
        [left_rows[:, :SPREAD], left_rows[:, SPREAD:], gain_place.astype(BF16)], axis=0
    )
    right_rows = jnp.concatenate([right_rows[:, :UNIT], right_rows[:, UNIT:], gain_rows], axis=0)
    return (
        grad_in,
        (reduce_first(left_rows, right_rows, waits), down, wide),
        early,
    )


def per_device(
    boundary,
    lengths,
    query_weight,
    key_matrix,
    value_matrix,
    output_weight,
    gate_weight,
    up_weight,
    down_weight,
    first_gain,
    second_gain,
):
    place = Place()
    first = place.first
    slab = boundary[0, :, 0]
    rows_dev = slab.shape[1]
    exchanged = sibling(jnp.where(first, slab[1], slab[0]))
    inputs = jnp.where(first, slab[0], exchanged).astype(F32)
    cotangent = jnp.where(first, exchanged, slab[1]).astype(F32)

    gains = jnp.pad(
        jnp.concatenate([first_gain, second_gain], axis=0), ((0, 6), (0, UNIT - PART))
    )
    role_packs = (
        (
            jnp.concatenate(
                [jnp.concatenate([query_weight[0], key_matrix[0]], axis=1), gains], axis=0
            ),
            jnp.pad(gate_weight[0], ((0, PADDED - PART), (0, 0))),
            down_weight[0, :, :DOWN_COLS],
        ),
        (
            jnp.concatenate(
                [jnp.concatenate([output_weight[0], value_matrix[0]], axis=1), gains], axis=0
            ),
            jnp.pad(up_weight[0], ((0, PADDED - PART), (0, 0))),
            down_weight[0, :, WIDTH - DOWN_COLS :],
        ),
    )
    layer_packs = ([], [])
    for zero, one in zip(*role_packs):
        kept = jnp.where(first, zero, one)
        other = sibling(jnp.where(first, one, zero))
        layer_packs[0].append(jnp.where(first, kept, other))
        layer_packs[1].append(jnp.where(first, other, kept))
    first_pack, wide_pack, down_pack = [jnp.stack(both) for both in zip(*layer_packs)]
    column, near_wide, started = gather_wide(place, wide_pack)
    one, other = gather_first(place, first_pack, started)
    weights_first, weights_second = [layer_weights(place, mine) for mine in one]

    seq_lengths = jnp.where(first, lengths[0, 0], lengths[0, 1])
    inner = jnp.arange(rows_dev, dtype=jnp.int32)
    own_rows = place.shard * rows_dev + inner
    all_rows = (place.near_shards[:, None] * rows_dev + inner[None]).reshape(-1)
    segment_mine, position_mine = segment_rows(seq_lengths, own_rows)
    segment_all, unused_position = segment_rows(seq_lengths, all_rows)
    allowed = (segment_mine[:, None] == segment_all[None, :]) & (
        own_rows[:, None] >= all_rows[None, :]
    )
    cosine_table, sine_portion = rotary_tables(position_mine)
    live_rows = (segment_mine < seq_lengths.shape[0]).astype(F32)

    geometry = (cosine_table, sine_portion, allowed)
    def fetch(key_value, near_rows):
        layers, unused = ring_gather_both(x_step, column, near_wide, (near_rows,))
        wide = [jnp.concatenate(blocks, axis=0) for blocks in layers]
        wholes, near = gather_down(place, down_pack, other, (key_value,))
        return ([[(value, sibling(value)) for value in pair] for pair in zip(wide, wholes)], near)

    middle, stored_first, others = forward_layer(
        place, inputs, weights_first, fetch, near_wide, *geometry
    )
    middle = middle.astype(BF16).astype(F32)
    result, stored_second, unused = forward_layer(
        place, middle, weights_second, lambda *unused: (others[1:], ()), (), *geometry
    )
    grad, (pair, down, wide), unused = backward_layer(
        place,
        cotangent * live_rows[:, None],
        weights_second,
        others[1],
        stored_second,
        (),
        [],
        *geometry,
    )
    grad = grad.astype(BF16).astype(F32)
    grad, (last, unused, wide_first), early = backward_layer(
        place,
        grad,
        weights_first,
        others[0],
        stored_first,
        (pair, wide),
        [pair, down, wide],
        *geometry,
    )

    ends = (grad.astype(BF16), result.astype(BF16))
    received = sibling(jnp.where(first, ends[1], ends[0]))
    boundary_out = jnp.where(
        first, jnp.stack([ends[0], received]), jnp.stack([received, ends[1]])
    )[None, :, None]

    late = across_x(place, across_y(last))
    late = all_quarters(place, across_far(jnp.concatenate([late, wide_first], axis=1)))
    late_first = late[:, :UNIT]
    early_first = jnp.concatenate([early[:, 2 * UNIT : 3 * UNIT], late[:, UNIT:]], axis=1)
    late_second = early[:, :UNIT]
    early_second = jnp.concatenate([early[:, UNIT : 2 * UNIT], early[:, 3 * UNIT :]], axis=1)

    sums = []
    for for_first, for_second in ((early_first, early_second), (late_first, late_second)):
        own = jnp.where(first, for_first, for_second)
        other = sibling(jnp.where(first, for_second, for_first))
        sums.append([value.astype(F32) for value in place.roles(own, other)])
    down_left, down_right = [value[:, :UNIT].reshape(FF_PART, DOWN_COLS) for value in sums[0]]
    gate_sum, up_sum = [value[:, UNIT:] for value in sums[0]]
    query_key, output_value = sums[1]
    gain_sums = query_key[PART : PART + 2, :PART] + output_value[PART : PART + 2, :PART]
    return (
        boundary_out,
        query_key[None, :PART, :WIDTH],
        query_key[None, :PART, WIDTH:],
        output_value[None, :PART, WIDTH:],
        output_value[None, :PART, :WIDTH],
        gate_sum[None, :PART],
        up_sum[None, :PART],
        jnp.concatenate([down_left, down_right[:, DOWN_SKIP:]], axis=1)[None],
        gain_sums[:1],
        gain_sums[1:],
    )


def solution(mesh):
    placed = (
        P("section", None, "dp", "fsdp", None),
        P("dp", None, None),
        P("section", "fsdp", None),
        P("section", "fsdp", None),
        P("section", "fsdp", None),
        P("section", "fsdp", None),
        P("section", "fsdp", None),
        P("section", "fsdp", None),
        P("section", "fsdp", None),
        P("section", "fsdp"),
        P("section", "fsdp"),
    )
    return jax.shard_map(
        per_device,
        mesh=mesh,
        in_specs=placed,
        out_specs=(
            P("section", None, "dp", "fsdp", None),
            P("section", "fsdp", None),
            P("section", "fsdp", None),
            P("section", "fsdp", None),
            P("section", "fsdp", None),
            P("section", "fsdp", None),
            P("section", "fsdp", None),
            P("section", "fsdp", None),
            P("section", "fsdp"),
            P("section", "fsdp"),
        ),
        check_vma=False,
    )
```

```python
import jax
import jax.numpy as jnp
from jax import lax
from jax.sharding import PartitionSpec as P

QUERY_HEADS = 15
KEY_VALUE_HEADS = 5
HEAD_SIZE = 64


EPS = 1e-05
SCALE = 0.125
MASKED = -1e30


BF16 = jnp.bfloat16
F32 = jnp.float32
WIDTH = 960
PART = 120
PADDED = 128
SPREAD = 1024
UNIT = 1280
FF_PART = 320
FF_QUARTER = 80
DOWN_COLS = 512
DOWN_SKIP = 64
ROW_QUARTER = 32
KV_WIDTH = KEY_VALUE_HEADS * HEAD_SIZE
DISTANCES = (0, -1, 1, 2)


def segment_rows(seq_lengths, row_index):
    seq_ends = jnp.cumsum(seq_lengths)
    starts = seq_ends - seq_lengths
    segment = jnp.sum((row_index[:, None] >= seq_ends[None, :]).astype(jnp.int32), axis=1)
    slot_ids = jnp.arange(seq_lengths.shape[0], dtype=jnp.int32)
    row_start = jnp.sum(
        jnp.where(segment[:, None] == slot_ids[None, :], starts[None, :], 0), axis=1
    )
    return (segment, row_index - row_start)


def rotary_tables(position):
    frequency = 10000.0 ** (-2.0 * jnp.arange(HEAD_SIZE // 2, dtype=jnp.float32) / HEAD_SIZE)
    angles = position.astype(jnp.float32)[:, None] * frequency[None, :]
    return (jnp.cos(angles)[:, None, :], jnp.sin(angles)[:, None, :])


def rotary_embedding(vector, cosine_table, sine_portion):
    first_half = vector[..., : HEAD_SIZE // 2]
    second_half = vector[..., HEAD_SIZE // 2 :]
    return jnp.concatenate(
        [
            first_half * cosine_table - second_half * sine_portion,
            second_half * cosine_table + first_half * sine_portion,
        ],
        axis=-1,
    )


def rotary_embedding_backward(grad, cosine_table, sine_portion):
    first_half = grad[..., : HEAD_SIZE // 2]
    second_half = grad[..., HEAD_SIZE // 2 :]
    return jnp.concatenate(
        [
            first_half * cosine_table + second_half * sine_portion,
            second_half * cosine_table - first_half * sine_portion,
        ],
        axis=-1,
    )


def rms_scale(values):
    return lax.rsqrt(jnp.mean(values * values, axis=-1, keepdims=True) + EPS)


def outer_sum(left, right):
    return lax.dot_general(
        left, right, (((0,), (0,)), ((), ())), preferred_element_type=jnp.float32
    )


def backward_product(grad, weight):
    return lax.dot_general(
        grad, weight, (((1,), (1,)), ((), ())), preferred_element_type=jnp.float32
    )


def z_step(value, step):
    return lax.ppermute(value, "fsdp", [(i, (i + 2 * step) % 8) for i in range(8)])


def x_step(value, step):
    return lax.ppermute(value, "dp", [(i, (i + 2 * step) % 8) for i in range(8)])


def y_near(value):
    return lax.ppermute(value, "fsdp", [(i, i ^ 1) for i in range(8)])


def y_far(value):
    return lax.ppermute(value, "dp", [(i, i ^ 1) for i in range(8)])


def sibling(value):
    return lax.ppermute(value, "section", [(0, 1), (1, 0)])


def ring_gather(step, way, block):
    before = step(block, 1)
    after = step(block, -1)
    far = step(before if way == 1 else after, way)
    return [block, before, after, far]


def ring_sum(step, way, chunk, waits=((), ())):
    relayed = gate(step(chunk(2).astype(BF16), way), *waits[0])
    other = step(chunk(-way).astype(BF16), -way)
    nearer = (chunk(way).astype(F32) + relayed.astype(F32)).astype(BF16)
    total = chunk(0).astype(F32) + other.astype(F32) + step(nearer, way).astype(F32)
    return gate(total, *waits[1])


def direct_sum(step, chunk):
    total = chunk(0).astype(F32)
    for distance in (1, -1, 2):
        total = total + step(chunk(distance).astype(BF16), distance).astype(F32)
    return total


class Place:
    def __init__(self):
        self.section = lax.axis_index("section")
        self.shard = lax.axis_index("fsdp")
        dp = lax.axis_index("dp")
        self.z, self.y = self.shard // 2, self.shard % 2
        self.x = dp // 2
        self.first = self.section == 0
        self.near_shards = jnp.stack(
            [(self.z + d) % 4 * 2 + (self.y + near) % 2 for d in DISTANCES for near in (0, 1)]
        )
        row = lax.broadcasted_iota(jnp.int32, (WIDTH, SPREAD), 0)
        column = jnp.arange(SPREAD, dtype=jnp.int32)
        self.z_shard = jnp.repeat(self.near_shards, PADDED)
        self.by_z = (
            (row // PART == self.z_shard[None]) & (row % PART == (column % PADDED)[None])
        ).astype(BF16)
        quarters = jnp.repeat(jnp.stack([(self.x + d) % 4 for d in DISTANCES]), SPREAD // 4)
        shards = jnp.tile(jnp.repeat(self.near_shards, ROW_QUARTER), 4)
        inner = quarters * ROW_QUARTER + column % ROW_QUARTER
        self.by_x = ((row // PART == shards[None]) & (row % PART == inner[None])).astype(BF16)

    def role(self, zero, one):
        return jnp.where(self.first, zero, one)

    def roles(self, mine, other):
        return (jnp.where(self.first, mine, other), jnp.where(self.first, other, mine))


def spread(value, places):
    return jnp.dot(value, places, preferred_element_type=F32).astype(BF16)


def unspread(value, places):
    high = lax.reduce_precision(value, 8, 7)
    both = jnp.concatenate([high.astype(BF16), (value - high).astype(BF16)], axis=1)
    return backward_product(both, jnp.concatenate([places, places], axis=1))


def product(left, right):
    return jnp.dot(left, right, preferred_element_type=F32)


def gate(value, *others):
    late = False
    for other in others:
        corner = other[(-1,) * other.ndim]
        late = late | (corner != corner)
    return jax.tree.map(lambda part: jnp.where(late, jnp.zeros_like(part), part), value)


def ring_gather_both(step, block):
    before = step(block, 1)
    after = step(block, -1)
    far = (step(before[0], 1), step(after[1], -1))
    layers = [[block[n], before[n], after[n], far[n]] for n in range(2)]
    return (layers, (before, after))


def gather_first(place, own, waits):
    own = gate(own, waits[0])
    other = y_near(own)
    pair = jnp.stack([own, other], axis=1).reshape(2, 2 * PADDED, UNIT)
    pair = gate(pair, waits[1])
    layers, unused = ring_gather_both(z_step, pair)
    return ([jnp.concatenate(blocks, axis=0) for blocks in layers], other)


def gather_down(place, own, start, waits):
    own = gate(own, start)
    other = y_near(own)
    low, high = (jnp.where(place.y == 0, own, other), jnp.where(place.y == 0, other, own))
    pair = jnp.stack([low, high], axis=1).reshape(2, 2 * FF_PART, DOWN_COLS)
    pair = gate(pair, *waits)
    layers, near = ring_gather_both(z_step, pair)
    wholes = []
    for blocks in layers:
        whole = jnp.zeros((4,) + pair.shape[1:], BF16)
        for distance, block in zip(DISTANCES, blocks):
            whole = lax.dynamic_update_slice_in_dim(
                whole, block[None], (place.z + distance) % 4, 0
            )
        wholes.append(whole.reshape(-1, DOWN_COLS))
    return (wholes, near)


def gather_wide(place, own):
    quarter = lax.dynamic_slice_in_dim(own, place.x * ROW_QUARTER, ROW_QUARTER, 1)
    other = y_near(quarter)
    pair = jnp.stack([quarter, other], axis=1)
    blocks = ring_gather(z_step, -1, pair)
    column = jnp.stack(blocks, axis=1)
    column = column.reshape(2, SPREAD // 4, 2 * UNIT)
    layers, near = ring_gather_both(x_step, column)
    started = (other, blocks[-1])
    return ([jnp.concatenate(blocks, axis=0) for blocks in layers], near, started)


def layer_weights(place, mine):
    one, two = [(value, sibling(value)) for value in mine]
    gains = one[0].reshape(8, PADDED, UNIT)[:, PART : PART + 2, :PADDED]
    gains = backward_product(gains.transpose(1, 0, 2).reshape(2, SPREAD), place.by_z)
    return (one, two, gains[:1], gains[1:])


def gather_rows(own):
    pair = jnp.concatenate([own, y_near(own)], axis=0)
    return jnp.concatenate(ring_gather(z_step, 1, pair), axis=0)


def scatter_rows(partial):
    parts = partial.reshape(4, -1, partial.shape[1])
    pair = ring_sum(z_step, -1, lambda distance: parts[DISTANCES.index(distance)])
    rows = pair.shape[0] // 2
    return pair[:rows] + y_near(pair[rows:].astype(BF16)).astype(F32)


def forward_layer(place, inputs, weights, fetch, waits, cosine_table, sine_portion, allowed):
    one, two, gain_one, gain_two = weights
    count_of_rows = inputs.shape[0]
    inv_one = rms_scale(inputs)
    normed_one = spread((inputs * inv_one * gain_one).astype(BF16), place.by_z)
    query_key, value_part = place.roles(product(normed_one, one[0]), product(normed_one, one[1]))
    value_part = value_part[:, WIDTH:].astype(BF16)
    turned = rotary_embedding(
        query_key.reshape(count_of_rows, QUERY_HEADS + KEY_VALUE_HEADS, HEAD_SIZE),
        cosine_table,
        sine_portion,
    ).astype(BF16)
    query_rows = turned[:, :QUERY_HEADS].reshape(
        count_of_rows, KEY_VALUE_HEADS, QUERY_HEADS // KEY_VALUE_HEADS, HEAD_SIZE
    )
    key_portion = turned[:, QUERY_HEADS:].reshape(count_of_rows, KV_WIDTH)
    key_value = gather_rows(jnp.concatenate([key_portion, value_part], axis=1))
    downs, near = fetch(key_value)
    low = downs[0]
    key_value = gate(key_value, *waits)
    key_row_block = key_value[:, :KV_WIDTH].reshape(-1, KEY_VALUE_HEADS, HEAD_SIZE)
    value_row_block = key_value[:, KV_WIDTH:].reshape(-1, KEY_VALUE_HEADS, HEAD_SIZE)
    scores = (
        jnp.einsum("qghd,kgd->ghqk", query_rows, key_row_block, preferred_element_type=F32)
        * SCALE
    )
    scores = jnp.where(allowed, scores, MASKED)
    row_max = jnp.max(scores, axis=-1, keepdims=True)
    exponent = jnp.exp(scores - row_max)
    total = jnp.sum(exponent, axis=-1, keepdims=True)
    attention = (exponent / total).astype(BF16)
    log_total = row_max + jnp.log(total)
    mixture = jnp.einsum(
        "ghqk,kgd->qghd", attention, value_row_block, preferred_element_type=F32
    )
    mixture = gate(mixture, *near)
    mixture = spread(
        mixture.astype(BF16).reshape(count_of_rows, QUERY_HEADS * HEAD_SIZE), place.by_z
    )
    unused, projected = place.roles(product(mixture, one[0]), product(mixture, one[1]))
    middle = inputs + projected[:, :WIDTH]
    inv_two = rms_scale(middle)
    normed_two = spread((middle * inv_two * gain_two).astype(BF16), place.by_x)
    gate_pre, up_pre = place.roles(product(normed_two, two[0]), product(normed_two, two[1]))
    hidden = (jax.nn.silu(gate_pre) * up_pre).astype(BF16)
    left, right = place.roles(product(hidden, low[0]), product(hidden, low[1]))
    result = middle + jnp.concatenate([left, right[:, DOWN_SKIP:]], axis=1)
    stored = (
        inputs,
        inv_one,
        normed_one,
        query_rows,
        key_row_block,
        value_row_block,
        log_total,
        mixture,
        middle,
        inv_two,
        normed_two,
        gate_pre,
        up_pre,
        hidden,
    )
    return (result, stored, downs)


def with_sibling(own, sent):
    return jnp.concatenate([own, sibling(sent)], axis=0)


def norm_backward(grad, unit, inverse, gain):
    scaled = grad * gain
    return inverse * (scaled - unit * jnp.mean(scaled * unit, axis=-1, keepdims=True))


def partial_chunks(left, right):
    size = left.shape[1] // 4

    def chunk(distance):
        at = DISTANCES.index(distance)
        return outer_sum(left[:, at * size : (at + 1) * size], right).astype(BF16)

    return chunk


def by_quarter(place, block, rows):
    quarters = block.reshape(4, rows, block.shape[-1])

    def quarter(distance):
        return lax.dynamic_index_in_dim(quarters, (place.x + distance) % 4, 0, keepdims=False)

    return quarter


def reduce_first(left, right, waits):
    return ring_sum(z_step, 1, partial_chunks(left, right), waits)


def reduce_down(place, left, right):
    size = 2 * FF_PART

    def chunk(distance):
        part = lax.dynamic_slice_in_dim(left, (place.z + distance) % 4 * size, size, 1)
        return outer_sum(part, right).astype(BF16)

    pair = ring_sum(z_step, -1, chunk).astype(BF16)
    pair = pair.reshape(2, PADDED, UNIT)
    return jnp.concatenate(
        [
            lax.dynamic_index_in_dim(pair, place.y, 0, keepdims=False),
            lax.dynamic_index_in_dim(pair, 1 - place.y, 0, keepdims=False),
        ],
        axis=0,
    ).astype(F32)


def reduce_wide(left, right):
    chunk = partial_chunks(left, right)
    half = SPREAD // 8
    from_before = x_step(outer_sum(left[:, -2 * half : -half], right).astype(BF16), 1)
    from_after = x_step(outer_sum(left[:, -half:], right).astype(BF16), -1)
    after = chunk(1).astype(F32) + jnp.pad(from_before, ((0, half), (0, 0))).astype(F32)
    before = chunk(-1).astype(F32) + jnp.pad(from_after, ((half, 0), (0, 0))).astype(F32)
    column = (
        chunk(0).astype(F32)
        + x_step(after.astype(BF16), 1).astype(F32)
        + x_step(before.astype(BF16), -1).astype(F32)
    )
    parts = column.reshape(4, 2 * ROW_QUARTER, 2 * UNIT)
    pair = ring_sum(z_step, 1, lambda distance: parts[DISTANCES.index(distance)])
    quarter = pair[:ROW_QUARTER] + y_near(pair[ROW_QUARTER:].astype(BF16)).astype(F32)
    return ((from_before, from_after), column, quarter)


def across_y(pair):
    return pair[:PADDED] + y_near(pair[PADDED:].astype(BF16)).astype(F32)


def across_x(place, block):
    return direct_sum(x_step, by_quarter(place, block, ROW_QUARTER))


def across_far(quarter):
    low = quarter.astype(BF16)
    return (low.astype(F32) + y_far(low).astype(F32)).astype(BF16)


def all_quarters(place, piece):
    whole = jnp.zeros((4,) + piece.shape, BF16)
    for distance in DISTANCES:
        block = step_from(piece, distance)
        whole = lax.dynamic_update_slice_in_dim(
            whole, block[None], (place.x + distance) % 4, 0
        )
    return whole.reshape(-1, piece.shape[-1])


def step_from(piece, distance):
    return piece if distance == 0 else x_step(piece, -distance)


def backward_layer(
    place, grad_out, weights, low, stored, waits, before, cosine_table, sine_portion, allowed
):
    one, two, gain_one, gain_two = weights
    (
        inputs,
        inv_one,
        normed_one,
        query_rows,
        key_row_block,
        value_row_block,
        log_total,
        mixture,
        middle,
        inv_two,
        normed_two,
        gate_pre,
        up_pre,
        hidden,
    ) = stored
    count_of_rows = grad_out.shape[0]
    grad_low = grad_out.astype(BF16)
    left_low = grad_low[:, :DOWN_COLS]
    right_low = grad_low[:, WIDTH - DOWN_COLS :]
    right_once = jnp.where(jnp.arange(DOWN_COLS)[None] < DOWN_SKIP, 0, right_low)
    mine_low, other_low = place.roles(left_low, right_once)
    hidden_grad = backward_product(mine_low, low[0]) + backward_product(other_low, low[1])
    sigmoid_gate = jax.nn.sigmoid(gate_pre)
    grad_gate = (
        hidden_grad * up_pre * sigmoid_gate * (1.0 + gate_pre * (1.0 - sigmoid_gate))
    ).astype(BF16)
    grad_up = (hidden_grad * gate_pre * sigmoid_gate).astype(BF16)
    mine, other = place.roles(grad_gate, grad_up)
    spread_two = backward_product(mine, two[0]) + backward_product(other, two[1])
    left_rows = with_sibling(*2 * (jnp.concatenate([hidden, normed_two], axis=1),))
    right_rows = with_sibling(
        jnp.concatenate([place.role(left_low, right_low), mine], axis=1),
        jnp.concatenate([place.role(right_low, left_low), other], axis=1),
    )
    down = reduce_down(place, left_rows[:, : 2 * UNIT], right_rows[:, :DOWN_COLS])
    wide = reduce_wide(left_rows[:, 2 * UNIT :], right_rows[:, DOWN_COLS:])
    grad_normed_two = unspread(spread_two, place.by_x)
    unit_two = middle * inv_two
    grad_gain_two = jnp.sum(grad_normed_two * unit_two, axis=0)
    grad_normed_two = gate(grad_normed_two, *waits)
    grad_mid = grad_out + norm_backward(grad_normed_two, unit_two, inv_two, gain_two)
    none_narrow = jnp.zeros((count_of_rows, KV_WIDTH), BF16)
    output_side = jnp.concatenate([grad_mid.astype(BF16), none_narrow], axis=1)
    none = jnp.zeros_like(output_side)
    mine, other = place.roles(none, output_side)
    grad_mixture = (
        unspread(backward_product(mine, one[0]) + backward_product(other, one[1]), place.by_z)
        .astype(BF16)
        .reshape(count_of_rows, KEY_VALUE_HEADS, QUERY_HEADS // KEY_VALUE_HEADS, HEAD_SIZE)
    )
    scores = (
        jnp.einsum("qghd,kgd->ghqk", query_rows, key_row_block, preferred_element_type=F32)
        * SCALE
    )
    scores = jnp.where(allowed, scores, MASKED)
    attention_full = jnp.exp(scores - log_total)
    attention = attention_full.astype(BF16)
    value_gradient = jnp.einsum(
        "ghqk,qghd->kgd", attention, grad_mixture, preferred_element_type=F32
    )
    grad_attention = jnp.einsum(
        "qghd,kgd->ghqk", grad_mixture, value_row_block, preferred_element_type=F32
    )
    row_dots = jnp.sum(attention_full * grad_attention, axis=-1, keepdims=True)
    far, column, wide = wide
    row_dots = gate(row_dots, *far)
    grad_scores = (attention_full * (grad_attention - row_dots)).astype(BF16)
    key_gradient = (
        jnp.einsum("ghqk,qghd->kgd", grad_scores, query_rows, preferred_element_type=F32)
        * SCALE
    )
    key_value = scatter_rows(
        jnp.concatenate(
            [key_gradient.reshape(-1, KV_WIDTH), value_gradient.reshape(-1, KV_WIDTH)], axis=1
        ).astype(BF16)
    )
    grad_queries = (
        jnp.einsum("ghqk,kgd->qghd", grad_scores, key_row_block, preferred_element_type=F32)
        * SCALE
    )
    key_value = gate(key_value, column, down)
    early = None
    if before:
        early = across_y(jnp.concatenate(before[:2] + [down], axis=1))
    key_gradient, value_low = (key_value[:, :KV_WIDTH], key_value[:, KV_WIDTH:].astype(BF16))
    grad_query_key = rotary_embedding_backward(
        jnp.concatenate(
            [
                grad_queries.reshape(count_of_rows, QUERY_HEADS, HEAD_SIZE),
                key_gradient.reshape(count_of_rows, KEY_VALUE_HEADS, HEAD_SIZE),
            ],
            axis=1,
        ),
        cosine_table,
        sine_portion,
    )
    grad_query_key = grad_query_key.reshape(count_of_rows, UNIT).astype(BF16)
    value_side = jnp.concatenate([jnp.zeros((count_of_rows, WIDTH), BF16), value_low], axis=1)
    mine, other = place.roles(grad_query_key, value_side)
    grad_normed = unspread(
        backward_product(mine, one[0]) + backward_product(other, one[1]), place.by_z
    )
    unit_one = inputs * inv_one
    grad_gain_one = jnp.sum(grad_normed * unit_one, axis=0)
    grad_in = grad_mid + norm_backward(grad_normed, unit_one, inv_one, gain_one)
    gain_rows = jnp.stack([grad_gain_one.reshape(8, PART), grad_gain_two.reshape(8, PART)], axis=1)
    gain_rows = jnp.pad(gain_rows.reshape(16, PART).astype(BF16), ((0, 0), (0, UNIT - PART)))
    number = jnp.arange(16, dtype=jnp.int32)[:, None]
    inner = (jnp.arange(SPREAD, dtype=jnp.int32) % PADDED)[None]
    gain_place = (number // 2 == place.z_shard[None]) & (PART + number % 2 == inner)
    left_rows = with_sibling(
        jnp.concatenate([place.role(normed_one, mixture), normed_one], axis=1),
        jnp.concatenate([place.role(mixture, normed_one), normed_one], axis=1),
    )
    right_rows = with_sibling(
        jnp.concatenate([place.role(grad_query_key, output_side), place.role(none, value_side)], 1),
        jnp.concatenate([place.role(output_side, grad_query_key), place.role(value_side, none)], 1),
    )
    waits = ((), ())
    if before:
        left_rows = gate(left_rows, early, wide)
        early = across_x(place, early)
        piece = across_far(jnp.concatenate([early, before[2]], axis=1))
        early = all_quarters(place, piece)
    left_rows = jnp.concatenate(
        [left_rows[:, :SPREAD], left_rows[:, SPREAD:], gain_place.astype(BF16)], axis=0
    )
    right_rows = jnp.concatenate([right_rows[:, :UNIT], right_rows[:, UNIT:], gain_rows], axis=0)
    return (
        grad_in,
        (reduce_first(left_rows, right_rows, waits), down, wide),
        early,
    )


def per_device(
    boundary,
    lengths,
    query_weight,
    key_matrix,
    value_matrix,
    output_weight,
    gate_weight,
    up_weight,
    down_weight,
    first_gain,
    second_gain,
):
    place = Place()
    first = place.first
    slab = boundary[0, :, 0]
    rows_dev = slab.shape[1]
    exchanged = sibling(jnp.where(first, slab[1], slab[0]))
    inputs = jnp.where(first, slab[0], exchanged).astype(F32)
    cotangent = jnp.where(first, exchanged, slab[1]).astype(F32)

    gains = jnp.pad(
        jnp.concatenate([first_gain, second_gain], axis=0), ((0, 6), (0, UNIT - PART))
    )
    role_packs = (
        (
            jnp.concatenate(
                [jnp.concatenate([query_weight[0], key_matrix[0]], axis=1), gains], axis=0
            ),
            jnp.pad(gate_weight[0], ((0, PADDED - PART), (0, 0))),
            down_weight[0, :, :DOWN_COLS],
        ),
        (
            jnp.concatenate(
                [jnp.concatenate([output_weight[0], value_matrix[0]], axis=1), gains], axis=0
            ),
            jnp.pad(up_weight[0], ((0, PADDED - PART), (0, 0))),
            down_weight[0, :, WIDTH - DOWN_COLS :],
        ),
    )
    layer_packs = ([], [])
    for zero, one in zip(*role_packs):
        kept = jnp.where(first, zero, one)
        other = sibling(jnp.where(first, one, zero))
        layer_packs[0].append(jnp.where(first, kept, other))
        layer_packs[1].append(jnp.where(first, other, kept))
    first_pack, wide_pack, down_pack = [jnp.stack(both) for both in zip(*layer_packs)]
    wide, near_wide, started = gather_wide(place, wide_pack)
    one, other = gather_first(place, first_pack, started)
    weights_first, weights_second = [layer_weights(place, mine) for mine in zip(one, wide)]

    seq_lengths = jnp.where(first, lengths[0, 0], lengths[0, 1])
    inner = jnp.arange(rows_dev, dtype=jnp.int32)
    own_rows = place.shard * rows_dev + inner
    all_rows = (place.near_shards[:, None] * rows_dev + inner[None]).reshape(-1)
    segment_mine, position_mine = segment_rows(seq_lengths, own_rows)
    segment_all, unused_position = segment_rows(seq_lengths, all_rows)
    allowed = (segment_mine[:, None] == segment_all[None, :]) & (
        own_rows[:, None] >= all_rows[None, :]
    )
    cosine_table, sine_portion = rotary_tables(position_mine)
    live_rows = (segment_mine < seq_lengths.shape[0]).astype(F32)

    geometry = (cosine_table, sine_portion, allowed)
    def fetch(key_value):
        wholes, near = gather_down(place, down_pack, other, (key_value,))
        return ([(value, sibling(value)) for value in wholes], near)

    middle, stored_first, downs = forward_layer(
        place, inputs, weights_first, fetch, near_wide, *geometry
    )
    middle = middle.astype(BF16).astype(F32)
    result, stored_second, unused = forward_layer(
        place, middle, weights_second, lambda key_value: (downs[1:], ()), (), *geometry
    )
    grad, (pair, down, wide), unused = backward_layer(
        place,
        cotangent * live_rows[:, None],
        weights_second,
        downs[1],
        stored_second,
        (),
        [],
        *geometry,
    )
    grad = grad.astype(BF16).astype(F32)
    grad, (last, unused, wide_first), early = backward_layer(
        place,
        grad,
        weights_first,
        downs[0],
        stored_first,
        (pair, wide),
        [pair, down, wide],
        *geometry,
    )

    ends = (grad.astype(BF16), result.astype(BF16))
    received = sibling(jnp.where(first, ends[1], ends[0]))
    boundary_out = jnp.where(
        first, jnp.stack([ends[0], received]), jnp.stack([received, ends[1]])
    )[None, :, None]

    late = across_x(place, across_y(last))
    late = all_quarters(place, across_far(jnp.concatenate([late, wide_first], axis=1)))
    late_first = late[:, :UNIT]
    early_first = jnp.concatenate([early[:, 2 * UNIT : 3 * UNIT], late[:, UNIT:]], axis=1)
    late_second = early[:, :UNIT]
    early_second = jnp.concatenate([early[:, UNIT : 2 * UNIT], early[:, 3 * UNIT :]], axis=1)

    sums = []
    for for_first, for_second in ((early_first, early_second), (late_first, late_second)):
        own = jnp.where(first, for_first, for_second)
        other = sibling(jnp.where(first, for_second, for_first))
        sums.append([value.astype(F32) for value in place.roles(own, other)])
    down_left, down_right = [value[:, :UNIT].reshape(FF_PART, DOWN_COLS) for value in sums[0]]
    gate_sum, up_sum = [value[:, UNIT:] for value in sums[0]]
    query_key, output_value = sums[1]
    gain_sums = query_key[PART : PART + 2, :PART] + output_value[PART : PART + 2, :PART]
    return (
        boundary_out,
        query_key[None, :PART, :WIDTH],
        query_key[None, :PART, WIDTH:],
        output_value[None, :PART, WIDTH:],
        output_value[None, :PART, :WIDTH],
        gate_sum[None, :PART],
        up_sum[None, :PART],
        jnp.concatenate([down_left, down_right[:, DOWN_SKIP:]], axis=1)[None],
        gain_sums[:1],
        gain_sums[1:],
    )


def solution(mesh):
    placed = (
        P("section", None, "dp", "fsdp", None),
        P("dp", None, None),
        P("section", "fsdp", None),
        P("section", "fsdp", None),
        P("section", "fsdp", None),
        P("section", "fsdp", None),
        P("section", "fsdp", None),
        P("section", "fsdp", None),
        P("section", "fsdp", None),
        P("section", "fsdp"),
        P("section", "fsdp"),
    )
    return jax.shard_map(
        per_device,
        mesh=mesh,
        in_specs=placed,
        out_specs=(
            P("section", None, "dp", "fsdp", None),
            P("section", "fsdp", None),
            P("section", "fsdp", None),
            P("section", "fsdp", None),
            P("section", "fsdp", None),
            P("section", "fsdp", None),
            P("section", "fsdp", None),
            P("section", "fsdp", None),
            P("section", "fsdp"),
            P("section", "fsdp"),
        ),
        check_vma=False,
    )
```
